128 devices in a mesh: dp: 64 (over y, z, x), width: 2 (over core).
Axes of the slice: x: 4, y: 4, z: 4, core: 2. Of those that a mesh axis runs over, the one named last changes fastest.
Arguments:
- queries: bfloat16 [4096, 4096], P('dp', 'width'), may hold values from -4 to 4
- passages: bfloat16 [4096, 4096], P('dp', 'width'), may hold values from -4 to 4
- passage_ids: int32 [4096], P('dp'), may hold values from 0 to 4095
- pos_index: int32 [4096], P('dp'), may hold values from 0 to 4095
Outputs:
- loss: float32 [4096], P('dp')
- grad_q: float32 [4096, 4096], P('dp', 'width')
- grad_p: float32 [4096, 4096], P('dp', 'width')
The draws below stay inside these ranges and needn't reach their ends.
All inputs are finite; a program needn't handle non-finite values.
Results may differ from the reference program's by a relative error of at most 0.001.
Values may be sent and summed in bfloat16 or wider, within the bound.
No kernel may reach another device: no remote copies, remote signals or barrier semaphores. Data moves between devices by JAX's collectives and lax.ppermute only.
A program may use at most 128 MiB of HBM per device.

```python
import math
import jax
import jax.numpy as jnp
import numpy as np
from jax import lax

D = 4096
TOTAL = 4096


def draw_queries(key, part):
    key = jax.random.fold_in(key, 11)
    return jnp.clip(jax.random.normal(key, (TOTAL, D), jnp.float32), -4.0, 4.0).astype(jnp.bfloat16)


def draw_passages(key, part):
    key = jax.random.fold_in(key, 23)
    return jnp.clip(jax.random.normal(key, (TOTAL, D), jnp.float32), -4.0, 4.0).astype(jnp.bfloat16)


def with_ends(result, own_key, smallest, high):
    index_at = [jax.random.randint(jax.random.fold_in(own_key, axis), (), 0, length) for axis, length in enumerate(result.shape)]
    widest = result.shape.index(max(result.shape))
    beside = index_at[:widest] + [(index_at[widest] + 1) % result.shape[widest]] + index_at[widest + 1:]
    return result.at[tuple(index_at)].set(smallest).at[tuple(beside)].set(high)


def rank_bounds(number_of, skew):
    portions = [(1 << 20) // math.isqrt(grade ** skew) + 1 for grade in range(1, number_of + 1)]
    scale = 1 + sum(portions) // (1 << 30)
    return np.cumsum(np.array([max(1, weight // scale) for weight in portions]))


def skewed_ids(key, extent, count, skew):
    table = rank_bounds(count, skew)
    ticket = jax.random.randint(jax.random.fold_in(key, 1), extent, 0, int(table[count - 1]))
    standing = jnp.searchsorted(jnp.asarray(table, jnp.int32), ticket, side="right")
    return jax.random.permutation(jax.random.fold_in(key, 2), count)[standing].astype(jnp.int32)


def setup_inputs(seed: int = 0) -> dict:
    seeds = jax.random.split(jax.random.key(seed), 5)
    queries = draw_queries(jax.random.fold_in(seeds[4], 71), 0)
    passages = draw_passages(jax.random.fold_in(seeds[4], 71), 0)
    passage_ids = with_ends(skewed_ids(seeds[2], (TOTAL,), TOTAL, 2), jax.random.fold_in(seeds[2], 3), 0, TOTAL - 1).astype(jnp.int32)
    pos_index = with_ends(jax.random.randint(seeds[3], (TOTAL,), 0, TOTAL), jax.random.fold_in(seeds[3], 1), 0, TOTAL - 1).astype(jnp.int32)
    return {"queries": queries, "passages": passages, "passage_ids": passage_ids, "pos_index": pos_index}


def reference(queries, passages, passage_ids, pos_index):
    total = queries.shape[0]
    scale = 3.0 / math.sqrt(D)
    block = min(512, total)
    count = total // block
    cols = jnp.arange(total, dtype=jnp.int32)
    target_ids = passage_ids[pos_index]
    minus = jnp.float32(-jnp.inf)

    def one(carry, index):
        acc_q, acc_p = carry
        start = (index * block).astype(jnp.int32)
        q_blk = lax.dynamic_slice_in_dim(queries, start, block, 0)
        p_blk = lax.dynamic_slice_in_dim(passages, start, block, 0)
        pos_blk = lax.dynamic_slice_in_dim(pos_index, start, block, 0)
        tid_blk = lax.dynamic_slice_in_dim(target_ids, start, block, 0)
        own_ids = lax.dynamic_slice_in_dim(passage_ids, start, block, 0)
        rows = start + jnp.arange(block, dtype=jnp.int32)
        s_qp = jnp.dot(q_blk, passages.T, preferred_element_type=jnp.float32) * scale
        s_qq = jnp.dot(q_blk, queries.T, preferred_element_type=jnp.float32) * scale
        s_pp = jnp.dot(p_blk, passages.T, preferred_element_type=jnp.float32) * scale
        is_pos = cols[None, :] == pos_blk[:, None]
        keep_qp = is_pos | (passage_ids[None, :] != tid_blk[:, None])
        keep_qq = cols[None, :] != rows[:, None]
        keep_pp = keep_qq & (passage_ids[None, :] != own_ids[:, None])
        top = jnp.maximum(lax.optimization_barrier(jnp.max(jnp.where(keep_qp, s_qp, minus), axis=1)), jnp.maximum(lax.optimization_barrier(jnp.max(jnp.where(keep_qq, s_qq, minus), axis=1)), lax.optimization_barrier(jnp.max(jnp.where(keep_pp, s_pp, minus), axis=1))))
        summed = lax.optimization_barrier(jnp.sum(jnp.where(keep_qp, jnp.exp(s_qp - top[:, None]), 0.0), axis=1)) + lax.optimization_barrier(jnp.sum(jnp.where(keep_qq, jnp.exp(s_qq - top[:, None]), 0.0), axis=1)) + lax.optimization_barrier(jnp.sum(jnp.where(keep_pp, jnp.exp(s_pp - top[:, None]), 0.0), axis=1))
        lse = top + jnp.log(summed)
        loss = lse - lax.optimization_barrier(jnp.sum(jnp.where(is_pos, s_qp, 0.0), axis=1))
        g_qp = (jnp.where(keep_qp, jnp.exp(s_qp - lse[:, None]), 0.0) - is_pos.astype(jnp.float32)).astype(jnp.bfloat16)
        w_qq = jnp.where(keep_qq, jnp.exp(s_qq - lse[:, None]), 0.0).astype(jnp.bfloat16)
        w_pp = jnp.where(keep_pp, jnp.exp(s_pp - lse[:, None]), 0.0).astype(jnp.bfloat16)
        row_q = jnp.dot(g_qp, passages, preferred_element_type=jnp.float32) + jnp.dot(w_qq, queries, preferred_element_type=jnp.float32)
        row_p = jnp.dot(w_pp, passages, preferred_element_type=jnp.float32)
        acc_q = acc_q + jnp.dot(w_qq.T, q_blk, preferred_element_type=jnp.float32)
        acc_p = acc_p + jnp.dot(g_qp.T, q_blk, preferred_element_type=jnp.float32) + jnp.dot(w_pp.T, p_blk, preferred_element_type=jnp.float32)
        return ((acc_q, acc_p), (loss, row_q, row_p))
    zeros = jnp.zeros((total, queries.shape[1]), jnp.float32)
    (acc_q, acc_p), (loss, row_q, row_p) = lax.scan(one, (zeros, zeros), jnp.arange(count, dtype=jnp.int32))
    grad_q = row_q.reshape(total, -1) + acc_q
    grad_p = row_p.reshape(total, -1) + acc_p
    return (loss.reshape(total), grad_q, grad_p)
```

```python
import functools
import math

import jax
import jax.numpy as jnp
from jax import lax
from jax.experimental import pallas as pl
from jax.experimental.pallas import tpu as pltpu
from jax.sharding import Mesh, PartitionSpec as P

D = 4096
N = 64
H = N // 2
SCALE = 3.0 / math.sqrt(D)
BIG = 1e30
GRID = ("y", "z", "x", "w")
UP = [(i, (i + 1) % 4) for i in range(4)]
DOWN = [(i, (i - 1) % 4) for i in range(4)]
FAR = [(i, (i + 2) % 4) for i in range(4)]
RING = (0, 1, 3, 2)
PARTS = (256, 256, 256, 256)
J = sum(PARTS)


def steps(first, second, by):
    moves = []
    for y in range(4):
        for z in range(4):
            for x in range(4):
                for w in range(2):
                    axis = second if w else first
                    to_y, to_z = ((y + by) % 4, z) if axis == "y" else (y, (z + by) % 4)
                    flat = lambda y, z: ((y * 4 + z) * 4 + x) * 2 + w
                    moves.append((flat(y, z), flat(to_y, to_z)))
    return moves


FIRST = {by: steps("y", "z", by) for by in (1, 2, 3)}
SECOND = {by: steps("z", "y", by) for by in (1, 2, 3)}


def along(value, moves):
    return lax.ppermute(value, GRID, moves)


def swap(value):
    return lax.ppermute(value, "w", [(0, 1), (1, 0)])


def up(value):
    return lax.ppermute(value, "x", UP)


def down(value):
    return lax.ppermute(value, "x", DOWN)


def far(value):
    return lax.ppermute(value, "x", FAR)


def inner(left, right):
    return lax.dot_general(
        left, right, (((1,), (1,)), ((), ())), preferred_element_type=jnp.float32
    )


def plain(left, right):
    return jnp.dot(left, right, preferred_element_type=jnp.float32)


VMEM = pl.BlockSpec(memory_space=pltpu.VMEM)
SMEM = pl.BlockSpec(memory_space=pltpu.SMEM)


def params(mib):
    return pltpu.CompilerParams(vmem_limit_bytes=mib << 20)


def cost(flops, moved, transcendentals=0):
    return pl.CostEstimate(flops=flops, bytes_accessed=moved, transcendentals=transcendentals)


def pack_kernel(plan, *refs):
    pieces, out = refs[:-1], refs[-1]
    at = 0
    for k, start, count in plan:
        out[:, at:at + count, :] = pieces[k][:, start:start + count, :]
        at += count


def pack(plan, *pieces):
    rows, wide = sum(count for _, _, count in plan), pieces[0].shape[2]
    return pl.pallas_call(
        functools.partial(pack_kernel, plan),
        out_shape=jax.ShapeDtypeStruct((2, rows, wide), jnp.bfloat16),
        in_specs=[VMEM] * len(pieces),
        out_specs=VMEM,
        compiler_params=params(8),
        cost_estimate=cost(0, 8 * rows * wide),
    )(*pieces)


def rows_kernel(*refs):
    mine, theirs, outs = refs[:5], refs[5:10], refs[10:]
    for k, pieces in enumerate((mine, theirs)):
        at = 4 * k * N
        for piece in pieces:
            count = piece.shape[1]
            for h in (0, 1):
                outs[h][at:at + count, :] = piece[h ^ k]
            at += count


def rows_from(mine, theirs):
    wide = mine[0].shape[2]
    return pl.pallas_call(
        rows_kernel,
        out_shape=[jax.ShapeDtypeStruct((8 * N, wide), jnp.bfloat16)] * 2,
        in_specs=[VMEM] * 10,
        out_specs=[VMEM] * 2,
        compiler_params=params(12),
        cost_estimate=cost(0, 8 << 20),
    )(*mine, *theirs)


def masks(rows, cols, at, count):
    same_u, cross_u, cross_e = (rows[pl.ds(at, count), k:k + 1] for k in range(3))
    same_v, cross_v, cross_p = (cols[k:k + 1, :] for k in range(3))
    hit = cross_e == cross_p
    return same_u != same_v, (cross_u != cross_v) | hit, hit


def scores_at(parts, at, count):
    return jnp.concatenate([part[pl.ds(at, count), :] for part in parts], axis=1) * SCALE


STATS = 16


def stats_kernel(core, amax, *refs):
    parts, (rows, cols, out, keep) = refs[:-4], refs[-4:]
    step = 32
    inc = core[0] == 1
    keep[...] = jnp.zeros_like(keep)

    @pl.loop(0, 4 * N // step)
    def _(k):
        at = pl.multiple_of(k * step, step)
        keep_s, keep_c, hit = masks(rows, cols, at, step)
        keep_c = keep_c & inc
        same = scores_at(parts, at, step)
        cross = scores_at(parts, pl.multiple_of(at + 4 * N, step), step)
        same = jnp.where(keep_s, same, -BIG)
        hits = jnp.sum(jnp.where(hit & inc, cross, 0.0), axis=1, keepdims=True)
        cross = jnp.where(keep_c, cross, -BIG)
        top = jnp.max(jnp.maximum(same, cross), axis=1, keepdims=True)
        total = jnp.sum(
            jnp.where(keep_s, jnp.exp(same - top), 0.0) + jnp.where(keep_c, jnp.exp(cross - top), 0.0),
            axis=1,
            keepdims=True,
        )
        group, low = k // (N // step), pl.multiple_of((k % (N // step)) * step, step)
        for n, value in enumerate((top, total, hits)):
            keep[n * 4 + group, pl.ds(low, step), :] = jnp.broadcast_to(value, (step, 128))

    for n in range(12):
        out[n:n + 1, :] = keep[n].T[0:1, :]
    out[12:16, :] = jnp.full((4, 128), amax[0], jnp.float32)


def stats_of(core, amax, parts, rows, cols):
    return pl.pallas_call(
        stats_kernel,
        out_shape=jax.ShapeDtypeStruct((STATS, 128), jnp.float32),
        in_specs=[SMEM] * 2 + [VMEM] * (len(parts) + 2),
        out_specs=VMEM,
        scratch_shapes=[pltpu.VMEM((12, 128, 128), jnp.float32)],
        compiler_params=params(8),
        cost_estimate=cost(10 << 20, 2 << 20, 1 << 19),
    )(core, amax, *parts, rows, cols)


TURNED = ((0, 1, 2, 3), (2, 0, 3, 1), (1, 3, 0, 2), (3, 2, 1, 0))


def merge_kernel(core, *refs):
    (mine, theirs), (out, ends) = (refs[:4], refs[4:8]), refs[8:]
    first = core[0] == 0
    a = [ref[...] for ref in mine]
    b = [ref[...] for ref in theirs]
    line = [jnp.where(first, u, v) for u, v in zip(a, b)] + [jnp.where(first, v, u) for u, v in zip(a, b)]
    loose = jnp.zeros((1, 128), jnp.float32)
    valid = lax.broadcasted_iota(jnp.int32, (1, 128), 1) < N
    for g in range(4):
        of = lambda k: [v[4 * k + t[g]:4 * k + t[g] + 1] for v, t in zip(line, TURNED * 2)]
        tops, sums, hits = of(0), of(1), of(2)
        top = functools.reduce(jnp.maximum, tops)
        total = sum(u * jnp.exp(t - top) for u, t in zip(sums, tops))
        lse = top + jnp.log(total)
        gap = lse - sum(hits)
        out[g:g + 1, :] = lse
        out[4 + g:5 + g, :] = gap
        loose = jnp.maximum(loose, jnp.where(valid, 1.0 - jnp.exp(-gap), 0.0))
        if g == 0:
            ends[0:1, :] = lse
    ends[1:2, :] = loose
    most = functools.reduce(jnp.maximum, [v[12:13] for v in line])
    ends[2:8, :] = jnp.broadcast_to(most, (6, 128))


def merged(core, mine, theirs):
    return pl.pallas_call(
        merge_kernel,
        out_shape=[jax.ShapeDtypeStruct((8, 128), jnp.float32)] * 2,
        in_specs=[SMEM] + [VMEM] * 8,
        out_specs=[VMEM] * 2,
        compiler_params=params(4),
        cost_estimate=cost(1 << 16, 1 << 16, 1 << 14),
    )(core, *mine, *theirs)


def lanes_of(rows):
    lane = lax.broadcasted_iota(jnp.int32, (8, 128), 1)
    wide = lambda v: jnp.broadcast_to(v, (8, 128))
    turn = lambda v, by: pltpu.roll(wide(v), by, axis=1) if by % 128 else wide(v)
    out = []
    for b in range(3):
        for a in (0, 2):
            out.append(jnp.where(lane < 64, wide(rows[4 * b + a]), turn(rows[4 * b + a + 1], 64)))
    for h in (0, 1):
        q = [turn(rows[12 + a], (32 * a - 32 * h) % 128) for a in range(4)]
        out.append(jnp.where(lane < 64, jnp.where(lane < 32, q[0], q[1]), jnp.where(lane < 96, q[2], q[3])))
    return jnp.concatenate(out, axis=1)[0:1]


def weights_kernel(first, count, core, *refs):
    parts, (rows, cols, lse_i, *plane, out, bound, col) = refs[:len(PARTS)], refs[len(PARTS):]
    step = 32
    w = core[0]
    for g in range(4):
        line = jnp.broadcast_to(lse_i[g:g + 1, :], (128, 128)).T[:N]
        col[0, g * N:(g + 1) * N, :] = line
        col[1, g * N:(g + 1) * N, :] = jnp.where(w == 1, line, 0.0)
    ends = [ref[8 * a:8 * a + 8, :] for ref in plane for a in range(4)]
    lj = lanes_of([v[0:1] for v in ends])
    cross_j = jnp.where(w == 1, 0.0, lj)
    loose = jnp.max(functools.reduce(jnp.maximum, [v[1:2] for v in ends]), axis=1, keepdims=True)
    most = jnp.max(functools.reduce(jnp.maximum, [v[2:3] for v in ends]), axis=1, keepdims=True)
    bound[...] = jnp.broadcast_to(jnp.maximum(loose, 1e-3) * jnp.maximum(most, 1e-20), (8, 128))

    @pl.loop(0, count * N // step)
    def _(k):
        at = pl.multiple_of(first * N + k * step, step)
        keep_s, keep_c, hit = masks(rows, cols, at, step)
        li = col[0, pl.ds(at, step), 0:1]
        lc = col[1, pl.ds(at, step), 0:1]
        same = scores_at(parts, at, step)
        cross = scores_at(parts, pl.multiple_of(at + 4 * N, step), step)
        m_s = jnp.where(keep_s, jnp.exp(same - li) + jnp.exp(same - lj), 0.0)
        m_c = jnp.where(keep_c, jnp.exp((cross - lc) - cross_j), 0.0) - jnp.where(hit, 1.0, 0.0)
        group = k // (N // step)
        base = group * 2 * N + (k % (N // step)) * step
        out[pl.ds(pl.multiple_of(base + w * N, step), step), :] = m_s.astype(jnp.bfloat16)
        out[pl.ds(pl.multiple_of(base + (1 - w) * N, step), step), :] = m_c.astype(jnp.bfloat16)


def weights_of(first, count, core, parts, rows, cols, lse_i, plane):
    return pl.pallas_call(
        functools.partial(weights_kernel, first, count),
        out_shape=[
            jax.ShapeDtypeStruct((count * 2 * N, J), jnp.bfloat16),
            jax.ShapeDtypeStruct((8, 128), jnp.float32),
        ],
        in_specs=[SMEM] + [VMEM] * (len(parts) + 7),
        out_specs=[VMEM] * 2,
        scratch_shapes=[pltpu.VMEM((2, 4 * N, 128), jnp.float32)],
        compiler_params=params(8),
        cost_estimate=cost(count * (3 << 20), count << 19, count * 3 * N * J),
    )(core, *parts, rows, cols, lse_i, *plane)


def product_kernel(bound, rest, rest_o, far, far_o, *refs):
    blocks, (here, down_o, up_o, far_out) = refs[:-4], refs[-4:]
    shrink = 1.0 / bound[0:1, 0:1]

    def total(mine, theirs):
        out = None
        for k, weights in enumerate((mine, theirs)):
            for n, size in enumerate(PARTS):
                at = sum(PARTS[:n])
                term = plain(weights[:, at:at + size], blocks[k * len(PARTS) + n][0])
                out = term if out is None else out + term
        return out

    far_out[...] = total(far, far_o) * shrink
    near = total(rest, rest_o)
    here[...] = near[:2 * N]
    down_o[...] = near[2 * N:4 * N] * shrink
    up_o[...] = near[4 * N:] * shrink


def product_of(bound, rest, rest_o, far, far_o, blocks, others):
    wide, step = blocks[0].shape[2], 256
    whole = lambda a: pl.BlockSpec(a.shape, lambda i: (0, 0))
    own = [pl.BlockSpec((1, a.shape[1], step), lambda i: (0, 0, i)) for a in blocks]
    other = [pl.BlockSpec((1, a.shape[1], step), lambda i: (1, 0, i)) for a in others]
    heads = (bound, rest, rest_o, far, far_o)
    return pl.pallas_call(
        product_kernel,
        grid=(wide // step,),
        out_shape=[jax.ShapeDtypeStruct((2 * N, wide), jnp.float32)] * 4,
        in_specs=[whole(a) for a in heads] + own + other,
        out_specs=[pl.BlockSpec((2 * N, step), lambda i: (0, i))] * 4,
        compiler_params=params(16),
        cost_estimate=cost(32 * N * J * wide, 4 * J * wide + 32 * N * wide),
    )(*heads, *blocks, *others)


def after(value, *others):
    return lax.optimization_barrier((value, *others))[0]


def settle(*values):
    return lax.optimization_barrier(values)


def body(queries, passages, passage_ids, pos_index):
    y, z, x, w = (lax.axis_index(name) for name in GRID)
    first = w == 0
    core = w.astype(jnp.int32).reshape(1)
    pick = lambda a, b: jnp.where(first, a, b)
    rows_of = functools.partial(lax.slice_in_dim, axis=1)
    low = lambda a: [rows_of(a, k * N, k * N + H) for k in range(a.shape[1] // N)]
    high = lambda a: [rows_of(a, k * N + H, (k + 1) * N) for k in range(a.shape[1] // N)]
    join = lambda parts: jnp.concatenate(parts, axis=1)
    line = lambda v, k: (up, far, down)[k - 1](v)
    by_first = lambda v, k: along(v, FIRST[k])
    by_second = lambda v, k: along(v, SECOND[k])
    ring = lambda v, send: [v] + [send(v, k) for k in RING[1:]]

    got = swap(pick(passages, queries))
    own = jnp.stack([pick(queries, passages), got])
    ints = jnp.stack([passage_ids, pos_index])

    fl, fr, own, *ints = settle(along(own, FIRST[1]), along(own, FIRST[3]), own, *ring(ints, line))
    f_low, f_high, own, fl, fr, *ints = settle(
        along(low(fl)[0], FIRST[1]), along(high(fr)[0], FIRST[3]), own, fl, fr, *ring(jnp.stack(ints), by_first)
    )
    group = pack(((0, 0, N), (1, 0, N), (2, 0, N), (3, 0, H), (4, 0, H)), own, fl, fr, f_low, f_high)
    group, own, *ints = settle(group, own, *ring(jnp.stack(ints), by_second))
    ints = jnp.stack(ints)
    ids = ints[..., 0, :]
    dev, off = ints[..., 1, :] // N, ints[..., 1, :] % N
    near = lambda at, other: (lambda d: d ^ (d >> 1))((at - other) % 4)
    dy, dz, dx = near(y, dev // 16), near(z, dev // 4 % 4), near(x, dev % 4)
    pos = ((pick(dz, dy) * 4 + pick(dy, dz)) * 4 + dx) * N + off
    pair = jnp.arange(64 * N, dtype=jnp.int32).reshape(4, 4, 4, N)
    i_of = lambda t: t[0, 0].reshape(-1)
    j_of = lambda t: jnp.concatenate(
        [t[:3, :, 0].reshape(-1), t[3, :, 0].reshape(4, 2, H).transpose(1, 0, 2).reshape(-1)]
    )
    i_pair, i_id, i_pos = i_of(pair), i_of(ids), i_of(pos)
    j_pair, j_id, j_pos = j_of(pair), j_of(ids), j_of(pos)
    table, every = ids.reshape(1, -1), pair.reshape(1, -1)
    look = lambda at: jnp.sum(jnp.where(at[:, None] == every, table, 0), axis=1)
    i_tgt, j_tgt = look(i_pos), look(j_pos)
    rows = jnp.stack([pick(i_pair, i_id), pick(i_id, i_tgt), pick(i_pair, i_pos)] + [i_pair] * 5, axis=1)
    cols = jnp.stack([pick(j_pair, j_id), pick(j_tgt, j_id), pick(j_pos, j_pair)] + [j_pair] * 5)
    xl, xr = up(own), down(own)
    mine = [own, xl, xr, up(low(xl)[0]), down(high(xr)[0])]
    dl, dr, group, rows, cols, *held = settle(
        along(group, SECOND[1]), along(group, SECOND[3]), group, rows, cols, *mine, *[swap(a) for a in mine]
    )
    to_l = pack(tuple((0, k * N, H) for k in range(4)), dl)
    to_r = pack(tuple((0, k * N + H, H) for k in range(4)), dr)
    i0, i1 = rows_from(held[:5], held[5:])
    score = lambda a: inner(i0, a[0]) + inner(i1, a[1])
    blocks = [group, dl, dr]
    parts = [score(a) for a in blocks]
    others = [swap(after(a, part)) for a, part in zip(blocks, parts)]
    gl, gr, i0, i1, *held = settle(along(to_l, SECOND[1]), along(to_r, SECOND[3]), i0, i1, *parts, *blocks)
    parts, blocks = held[:3], held[3:]
    last = pack(((0, 0, 2 * N), (1, 0, 2 * N)), gl, gr)
    blocks.append(last)

    amax = jnp.maximum(
        jnp.max(jnp.abs(queries.astype(jnp.float32))), jnp.max(jnp.abs(passages.astype(jnp.float32)))
    )

    parts.append(score(last))
    found, *held = settle(stats_of(core, amax.reshape(1), parts, rows, cols), *others, swap(last), *blocks)
    others, blocks = held[:4], held[4:]
    found = ring(found, line)
    lse_i, ends = merged(core, found, [swap(a) for a in found])
    loss = lse_i[4, :N]
    plane = ring(jnp.concatenate(ring(ends, by_first)), by_second)

    args = (core, parts, rows, cols, lse_i, plane)
    m_far, bound = weights_of(3, 1, *args)
    m_rest, _ = weights_of(0, 3, *args)
    f16, f32 = jnp.float16, jnp.float32
    here, to_down, to_up, opposite = product_of(bound, m_rest, swap(m_rest), m_far, swap(m_far), blocks, others)
    opposite, near_q, near_p = opposite.astype(f16), to_down[:N].astype(f16), to_up[N:].astype(f16)
    got_q, got_p, down_q, up_p = settle(up(opposite[:N]), down(opposite[N:]), down(near_q), up(near_p))
    up_q = up((to_up[:N] + got_q.astype(f32)).astype(f16))
    down_p = down((to_down[N:] + got_p.astype(f32)).astype(f16))
    grow = bound[0, 0]
    grad_q = here[:N] + (up_q.astype(f32) + down_q.astype(f32)) * grow
    grad_p = here[N:] + (up_p.astype(f32) + down_p.astype(f32)) * grow
    return loss, grad_q, grad_p


def solution(mesh):
    grid = Mesh(mesh.devices.reshape(4, 4, 4, 2), GRID)
    pair = ("y", "z", "x")
    placed = (P(pair, "w"), P(pair, "w"), P(pair), P(pair))
    return jax.shard_map(
        body,
        mesh=grid,
        in_specs=placed,
        out_specs=(P(pair), P(pair, "w"), P(pair, "w")),
        check_vma=False,
    )
```

```python
import functools
import math

import jax
import jax.numpy as jnp
from jax import lax
from jax.experimental import pallas as pl
from jax.experimental.pallas import tpu as pltpu
from jax.sharding import Mesh, PartitionSpec as P

D = 4096
N = 64
H = N // 2
SCALE = 3.0 / math.sqrt(D)
BIG = 1e30
GRID = ("y", "z", "x", "w")
UP = [(i, (i + 1) % 4) for i in range(4)]
DOWN = [(i, (i - 1) % 4) for i in range(4)]
FAR = [(i, (i + 2) % 4) for i in range(4)]
RING = (0, 1, 3, 2)
PARTS = (256, 256, 256, 128, 128)
J = sum(PARTS)


def steps(first, second, by):
    moves = []
    for y in range(4):
        for z in range(4):
            for x in range(4):
                for w in range(2):
                    axis = second if w else first
                    to_y, to_z = ((y + by) % 4, z) if axis == "y" else (y, (z + by) % 4)
                    flat = lambda y, z: ((y * 4 + z) * 4 + x) * 2 + w
                    moves.append((flat(y, z), flat(to_y, to_z)))
    return moves


FIRST = {by: steps("y", "z", by) for by in (1, 2, 3)}
SECOND = {by: steps("z", "y", by) for by in (1, 2, 3)}


def along(value, moves):
    return lax.ppermute(value, GRID, moves)


def swap(value):
    return lax.ppermute(value, "w", [(0, 1), (1, 0)])


def up(value):
    return lax.ppermute(value, "x", UP)


def down(value):
    return lax.ppermute(value, "x", DOWN)


def far(value):
    return lax.ppermute(value, "x", FAR)


def inner(left, right):
    return lax.dot_general(
        left, right, (((1,), (1,)), ((), ())), preferred_element_type=jnp.float32
    )


def plain(left, right):
    return jnp.dot(left, right, preferred_element_type=jnp.float32)


VMEM = pl.BlockSpec(memory_space=pltpu.VMEM)
SMEM = pl.BlockSpec(memory_space=pltpu.SMEM)


def params(mib):
    return pltpu.CompilerParams(vmem_limit_bytes=mib << 20)


def cost(flops, moved, transcendentals=0):
    return pl.CostEstimate(flops=flops, bytes_accessed=moved, transcendentals=transcendentals)


def pack_kernel(plan, *refs):
    pieces, out = refs[:-1], refs[-1]
    at = 0
    for k, start, count in plan:
        out[:, at:at + count, :] = pieces[k][:, start:start + count, :]
        at += count


def pack(plan, *pieces):
    rows, wide = sum(count for _, _, count in plan), pieces[0].shape[2]
    return pl.pallas_call(
        functools.partial(pack_kernel, plan),
        out_shape=jax.ShapeDtypeStruct((2, rows, wide), jnp.bfloat16),
        in_specs=[VMEM] * len(pieces),
        out_specs=VMEM,
        compiler_params=params(8),
        cost_estimate=cost(0, 8 * rows * wide),
    )(*pieces)


def rows_kernel(*refs):
    mine, theirs, outs = refs[:5], refs[5:10], refs[10:]
    for k, pieces in enumerate((mine, theirs)):
        at = 4 * k * N
        for piece in pieces:
            count = piece.shape[1]
            for h in (0, 1):
                outs[h][at:at + count, :] = piece[h ^ k]
            at += count


def rows_from(mine, theirs):
    wide = mine[0].shape[2]
    return pl.pallas_call(
        rows_kernel,
        out_shape=[jax.ShapeDtypeStruct((8 * N, wide), jnp.bfloat16)] * 2,
        in_specs=[VMEM] * 10,
        out_specs=[VMEM] * 2,
        compiler_params=params(12),
        cost_estimate=cost(0, 8 << 20),
    )(*mine, *theirs)


def last_kernel(i0, i1, gl, gr, out_l, out_r):
    total = None
    for h, rows in enumerate((i0, i1)):
        term = inner(rows[...], jnp.concatenate([gl[h], gr[h]]))
        total = term if total is None else total + term
    out_l[...] = total[:, :2 * N]
    out_r[...] = total[:, 2 * N:]


def last_scores(i0, i1, gl, gr):
    return pl.pallas_call(
        last_kernel,
        out_shape=[jax.ShapeDtypeStruct((8 * N, 2 * N), jnp.float32)] * 2,
        in_specs=[VMEM] * 4,
        out_specs=[VMEM] * 2,
        compiler_params=params(12),
        cost_estimate=cost(8 * 8 * N * 2 * N * i0.shape[1], 7 << 20),
    )(i0, i1, gl, gr)


def masks(rows, cols, at, count):
    same_u, cross_u, cross_e = (rows[pl.ds(at, count), k:k + 1] for k in range(3))
    same_v, cross_v, cross_p = (cols[k:k + 1, :] for k in range(3))
    hit = cross_e == cross_p
    return same_u != same_v, (cross_u != cross_v) | hit, hit


def scores_at(parts, at, count):
    return jnp.concatenate([part[pl.ds(at, count), :] for part in parts], axis=1) * SCALE


STATS = 16


def stats_kernel(core, amax, *refs):
    parts, (rows, cols, out, keep) = refs[:-4], refs[-4:]
    step = 32
    inc = core[0] == 1
    keep[...] = jnp.zeros_like(keep)

    @pl.loop(0, 4 * N // step)
    def _(k):
        at = pl.multiple_of(k * step, step)
        keep_s, keep_c, hit = masks(rows, cols, at, step)
        keep_c = keep_c & inc
        same = scores_at(parts, at, step)
        cross = scores_at(parts, pl.multiple_of(at + 4 * N, step), step)
        same = jnp.where(keep_s, same, -BIG)
        hits = jnp.sum(jnp.where(hit & inc, cross, 0.0), axis=1, keepdims=True)
        cross = jnp.where(keep_c, cross, -BIG)
        top = jnp.max(jnp.maximum(same, cross), axis=1, keepdims=True)
        total = jnp.sum(
            jnp.where(keep_s, jnp.exp(same - top), 0.0) + jnp.where(keep_c, jnp.exp(cross - top), 0.0),
            axis=1,
            keepdims=True,
        )
        group, low = k // (N // step), pl.multiple_of((k % (N // step)) * step, step)
        for n, value in enumerate((top, total, hits)):
            keep[n * 4 + group, pl.ds(low, step), :] = jnp.broadcast_to(value, (step, 128))

    for n in range(12):
        out[n:n + 1, :] = keep[n].T[0:1, :]
    out[12:16, :] = jnp.full((4, 128), amax[0], jnp.float32)


def stats_of(core, amax, parts, rows, cols):
    return pl.pallas_call(
        stats_kernel,
        out_shape=jax.ShapeDtypeStruct((STATS, 128), jnp.float32),
        in_specs=[SMEM] * 2 + [VMEM] * (len(parts) + 2),
        out_specs=VMEM,
        scratch_shapes=[pltpu.VMEM((12, 128, 128), jnp.float32)],
        compiler_params=params(8),
        cost_estimate=cost(10 << 20, 2 << 20, 1 << 19),
    )(core, amax, *parts, rows, cols)


TURNED = ((0, 1, 2, 3), (2, 0, 3, 1), (1, 3, 0, 2), (3, 2, 1, 0))


def merge_kernel(core, *refs):
    (mine, theirs), (out, ends) = (refs[:4], refs[4:8]), refs[8:]
    first = core[0] == 0
    a = [ref[...] for ref in mine]
    b = [ref[...] for ref in theirs]
    line = [jnp.where(first, u, v) for u, v in zip(a, b)] + [jnp.where(first, v, u) for u, v in zip(a, b)]
    loose = jnp.zeros((1, 128), jnp.float32)
    valid = lax.broadcasted_iota(jnp.int32, (1, 128), 1) < N
    for g in range(4):
        of = lambda k: [v[4 * k + t[g]:4 * k + t[g] + 1] for v, t in zip(line, TURNED * 2)]
        tops, sums, hits = of(0), of(1), of(2)
        top = functools.reduce(jnp.maximum, tops)
        total = sum(u * jnp.exp(t - top) for u, t in zip(sums, tops))
        lse = top + jnp.log(total)
        gap = lse - sum(hits)
        out[g:g + 1, :] = lse
        out[4 + g:5 + g, :] = gap
        loose = jnp.maximum(loose, jnp.where(valid, 1.0 - jnp.exp(-gap), 0.0))
        if g == 0:
            ends[0:1, :] = lse
    ends[1:2, :] = loose
    most = functools.reduce(jnp.maximum, [v[12:13] for v in line])
    ends[2:8, :] = jnp.broadcast_to(most, (6, 128))


def merged(core, mine, theirs):
    return pl.pallas_call(
        merge_kernel,
        out_shape=[jax.ShapeDtypeStruct((8, 128), jnp.float32)] * 2,
        in_specs=[SMEM] + [VMEM] * 8,
        out_specs=[VMEM] * 2,
        compiler_params=params(4),
        cost_estimate=cost(1 << 16, 1 << 16, 1 << 14),
    )(core, *mine, *theirs)


def lanes_of(rows):
    lane = lax.broadcasted_iota(jnp.int32, (8, 128), 1)
    wide = lambda v: jnp.broadcast_to(v, (8, 128))
    turn = lambda v, by: pltpu.roll(wide(v), by, axis=1) if by % 128 else wide(v)
    out = []
    for b in range(3):
        for a in (0, 2):
            out.append(jnp.where(lane < 64, wide(rows[4 * b + a]), turn(rows[4 * b + a + 1], 64)))
    for h in (0, 1):
        q = [turn(rows[12 + a], (32 * a - 32 * h) % 128) for a in range(4)]
        out.append(jnp.where(lane < 64, jnp.where(lane < 32, q[0], q[1]), jnp.where(lane < 96, q[2], q[3])))
    return jnp.concatenate(out, axis=1)[0:1]


def weights_kernel(first, count, core, *refs):
    parts, (rows, cols, lse_i, *plane, out, bound, col) = refs[:len(PARTS)], refs[len(PARTS):]
    step = 32
    w = core[0]
    for g in range(4):
        line = jnp.broadcast_to(lse_i[g:g + 1, :], (128, 128)).T[:N]
        col[0, g * N:(g + 1) * N, :] = line
        col[1, g * N:(g + 1) * N, :] = jnp.where(w == 1, line, 0.0)
    ends = [ref[8 * a:8 * a + 8, :] for ref in plane for a in range(4)]
    lj = lanes_of([v[0:1] for v in ends])
    cross_j = jnp.where(w == 1, 0.0, lj)
    loose = jnp.max(functools.reduce(jnp.maximum, [v[1:2] for v in ends]), axis=1, keepdims=True)
    most = jnp.max(functools.reduce(jnp.maximum, [v[2:3] for v in ends]), axis=1, keepdims=True)
    bound[...] = jnp.broadcast_to(jnp.maximum(loose, 1e-3) * jnp.maximum(most, 1e-20), (8, 128))

    @pl.loop(0, count * N // step)
    def _(k):
        at = pl.multiple_of(first * N + k * step, step)
        keep_s, keep_c, hit = masks(rows, cols, at, step)
        li = col[0, pl.ds(at, step), 0:1]
        lc = col[1, pl.ds(at, step), 0:1]
        same = scores_at(parts, at, step)
        cross = scores_at(parts, pl.multiple_of(at + 4 * N, step), step)
        m_s = jnp.where(keep_s, jnp.exp(same - li) + jnp.exp(same - lj), 0.0)
        m_c = jnp.where(keep_c, jnp.exp((cross - lc) - cross_j), 0.0) - jnp.where(hit, 1.0, 0.0)
        group = k // (N // step)
        base = group * 2 * N + (k % (N // step)) * step
        out[pl.ds(pl.multiple_of(base + w * N, step), step), :] = m_s.astype(jnp.bfloat16)
        out[pl.ds(pl.multiple_of(base + (1 - w) * N, step), step), :] = m_c.astype(jnp.bfloat16)


def weights_of(first, count, core, parts, rows, cols, lse_i, plane):
    return pl.pallas_call(
        functools.partial(weights_kernel, first, count),
        out_shape=[
            jax.ShapeDtypeStruct((count * 2 * N, J), jnp.bfloat16),
            jax.ShapeDtypeStruct((8, 128), jnp.float32),
        ],
        in_specs=[SMEM] + [VMEM] * (len(parts) + 7),
        out_specs=[VMEM] * 2,
        scratch_shapes=[pltpu.VMEM((2, 4 * N, 128), jnp.float32)],
        compiler_params=params(8),
        cost_estimate=cost(count * (3 << 20), count << 19, count * 3 * N * J),
    )(core, *parts, rows, cols, lse_i, *plane)


def product_kernel(scaled, bound, mine, theirs, *refs):
    count = mine.shape[0] // (2 * N)
    blocks, outs, (held, sems) = refs[:2 * len(PARTS)], refs[2 * len(PARTS):-2], refs[-2:]
    copies = ([], [])
    for k in (0, 1):
        at = 0
        for n, size in enumerate(PARTS):
            i = k * len(PARTS) + n
            copies[k].append(pltpu.make_async_copy(blocks[i].at[k], held.at[k, pl.ds(at, size)], sems.at[i]))
            copies[k][-1].start()
            at += size
    shrink = 1.0 / bound[0:1, 0:1]
    step = 512
    for k, weights in enumerate((mine, theirs)):
        for copy in copies[k]:
            copy.wait()

        @pl.loop(0, held.shape[2] // step)
        def _(j):
            here = pl.ds(pl.multiple_of(j * step, step), step)
            term = plain(weights[...], held[k, :, here])
            for g in range(count):
                part = term[2 * N * g:2 * N * (g + 1)]
                if k == 0:
                    outs[g][:, here] = part
                else:
                    part = outs[g][:, here] + part
                    outs[g][:, here] = part * shrink if g >= scaled else part


def product_of(scaled, bound, mine, theirs, blocks, others):
    rows, wide = mine.shape[0], blocks[0].shape[2]
    outs = rows // (2 * N)
    return pl.pallas_call(
        functools.partial(product_kernel, scaled),
        out_shape=[jax.ShapeDtypeStruct((2 * N, wide), jnp.float32)] * outs,
        in_specs=[VMEM] * 3 + [pl.BlockSpec(memory_space=pl.ANY)] * (2 * len(PARTS)),
        out_specs=[VMEM] * outs,
        scratch_shapes=[pltpu.VMEM((2, J, wide), jnp.bfloat16), pltpu.SemaphoreType.DMA((2 * len(PARTS),))],
        compiler_params=params(20),
        cost_estimate=cost(4 * rows * J * wide, 4 * J * wide + 4 * rows * wide),
    )(bound, mine, theirs, *blocks, *others)


def after(value, *others):
    return lax.optimization_barrier((value, *others))[0]


def settle(*values):
    return lax.optimization_barrier(values)


def body(queries, passages, passage_ids, pos_index):
    y, z, x, w = (lax.axis_index(name) for name in GRID)
    first = w == 0
    core = w.astype(jnp.int32).reshape(1)
    pick = lambda a, b: jnp.where(first, a, b)
    rows_of = functools.partial(lax.slice_in_dim, axis=1)
    low = lambda a: [rows_of(a, k * N, k * N + H) for k in range(a.shape[1] // N)]
    high = lambda a: [rows_of(a, k * N + H, (k + 1) * N) for k in range(a.shape[1] // N)]
    join = lambda parts: jnp.concatenate(parts, axis=1)
    line = lambda v, k: (up, far, down)[k - 1](v)
    by_first = lambda v, k: along(v, FIRST[k])
    by_second = lambda v, k: along(v, SECOND[k])
    ring = lambda v, send: [v] + [send(v, k) for k in RING[1:]]

    got = swap(pick(passages, queries))
    own = jnp.stack([pick(queries, passages), got])
    ints = jnp.stack([passage_ids, pos_index])

    fl, fr, own, *ints = settle(along(own, FIRST[1]), along(own, FIRST[3]), own, *ring(ints, line))
    f_low, f_high, own, fl, fr, *ints = settle(
        along(low(fl)[0], FIRST[1]), along(high(fr)[0], FIRST[3]), own, fl, fr, *ring(jnp.stack(ints), by_first)
    )
    group = pack(((0, 0, N), (1, 0, N), (2, 0, N), (3, 0, H), (4, 0, H)), own, fl, fr, f_low, f_high)
    group, own, *ints = settle(group, own, *ring(jnp.stack(ints), by_second))
    ints = jnp.stack(ints)
    ids = ints[..., 0, :]
    dev, off = ints[..., 1, :] // N, ints[..., 1, :] % N
    near = lambda at, other: (lambda d: d ^ (d >> 1))((at - other) % 4)
    dy, dz, dx = near(y, dev // 16), near(z, dev // 4 % 4), near(x, dev % 4)
    pos = ((pick(dz, dy) * 4 + pick(dy, dz)) * 4 + dx) * N + off
    pair = jnp.arange(64 * N, dtype=jnp.int32).reshape(4, 4, 4, N)
    i_of = lambda t: t[0, 0].reshape(-1)
    j_of = lambda t: jnp.concatenate(
        [t[:3, :, 0].reshape(-1), t[3, :, 0].reshape(4, 2, H).transpose(1, 0, 2).reshape(-1)]
    )
    i_pair, i_id, i_pos = i_of(pair), i_of(ids), i_of(pos)
    j_pair, j_id, j_pos = j_of(pair), j_of(ids), j_of(pos)
    table, every = ids.reshape(1, -1), pair.reshape(1, -1)
    look = lambda at: jnp.sum(jnp.where(at[:, None] == every, table, 0), axis=1)
    i_tgt, j_tgt = look(i_pos), look(j_pos)
    rows = jnp.stack([pick(i_pair, i_id), pick(i_id, i_tgt), pick(i_pair, i_pos)] + [i_pair] * 5, axis=1)
    cols = jnp.stack([pick(j_pair, j_id), pick(j_tgt, j_id), pick(j_pos, j_pair)] + [j_pair] * 5)
    amax = jnp.maximum(
        jnp.max(jnp.abs(queries.astype(jnp.float32))), jnp.max(jnp.abs(passages.astype(jnp.float32)))
    )
    xl, xr = up(own), down(own)
    mine = [own, xl, xr, up(low(xl)[0]), down(high(xr)[0])]
    dl, dr, group, rows, cols, amax, *held = settle(
        along(group, SECOND[1]), along(group, SECOND[3]), group, rows, cols, amax, *mine, *[swap(a) for a in mine]
    )
    to_l = pack(tuple((0, k * N, H) for k in range(4)), dl)
    to_r = pack(tuple((0, k * N + H, H) for k in range(4)), dr)
    i0, i1 = rows_from(held[:5], held[5:])
    score = lambda a: inner(i0, a[0]) + inner(i1, a[1])
    blocks = [group, dl, dr]
    parts = [score(a) for a in blocks]
    others = [swap(after(a, part)) for a, part in zip(blocks, parts)]
    gl, gr, i0, i1, *held = settle(along(to_l, SECOND[1]), along(to_r, SECOND[3]), i0, i1, *parts, *blocks)
    parts, blocks = held[:3], held[3:]
    blocks += [gl, gr]

    parts += last_scores(i0, i1, gl, gr)
    found, *held = settle(stats_of(core, amax.reshape(1), parts, rows, cols), *others, swap(gl), swap(gr), *blocks)
    others, blocks = held[:5], held[5:]
    found = ring(found, line)
    lse_i, ends = merged(core, found, [swap(a) for a in found])
    loss = lse_i[4, :N]
    plane = ring(jnp.concatenate(ring(ends, by_first)), by_second)

    f16, f32 = jnp.float16, jnp.float32
    args = (parts, rows, cols, lse_i, plane)
    m_far, bound = weights_of(3, 1, core, *args)
    m_far_o = swap(m_far)
    m_rest, _ = weights_of(0, 3, after(core, m_far), *args)
    (opposite,) = product_of(0, bound, m_far, m_far_o, blocks, others)
    opposite = opposite.astype(f16)
    got_q, got_p, here, to_down, to_up = settle(
        up(opposite[:N]), down(opposite[N:]), *product_of(1, bound, m_rest, swap(m_rest), blocks, others)
    )
    below = up(jnp.concatenate([to_up[:N] + got_q.astype(f32), to_up[N:]]).astype(f16))
    above = down(jnp.concatenate([to_down[:N], to_down[N:] + got_p.astype(f32)]).astype(f16))
    grad = here + (below.astype(f32) + above.astype(f32)) * bound[0, 0]
    grad_q, grad_p = grad[:N], grad[N:]
    return loss, grad_q, grad_p


def solution(mesh):
    grid = Mesh(mesh.devices.reshape(4, 4, 4, 2), GRID)
    pair = ("y", "z", "x")
    placed = (P(pair, "w"), P(pair, "w"), P(pair), P(pair))
    return jax.shard_map(
        body,
        mesh=grid,
        in_specs=placed,
        out_specs=(P(pair), P(pair, "w"), P(pair, "w")),
        check_vma=False,
    )
```

```python
import functools
import math

import jax
import jax.numpy as jnp
from jax import lax
from jax.experimental import pallas as pl
from jax.experimental.pallas import tpu as pltpu
from jax.sharding import Mesh, PartitionSpec as P

D = 4096
N = 64
H = N // 2
SCALE = 3.0 / math.sqrt(D)
BIG = 1e30
GRID = ("y", "z", "x", "w")
UP = [(i, (i + 1) % 4) for i in range(4)]
DOWN = [(i, (i - 1) % 4) for i in range(4)]
FAR = [(i, (i + 2) % 4) for i in range(4)]
RING = (0, 1, 3, 2)
PARTS = (256, 256, 256, 128, 128)
J = sum(PARTS)


def steps(first, second, by):
    moves = []
    for y in range(4):
        for z in range(4):
            for x in range(4):
                for w in range(2):
                    axis = second if w else first
                    to_y, to_z = ((y + by) % 4, z) if axis == "y" else (y, (z + by) % 4)
                    flat = lambda y, z: ((y * 4 + z) * 4 + x) * 2 + w
                    moves.append((flat(y, z), flat(to_y, to_z)))
    return moves


FIRST = {by: steps("y", "z", by) for by in (1, 2, 3)}
SECOND = {by: steps("z", "y", by) for by in (1, 2, 3)}


def along(value, moves):
    return lax.ppermute(value, GRID, moves)


def swap(value):
    return lax.ppermute(value, "w", [(0, 1), (1, 0)])


def up(value):
    return lax.ppermute(value, "x", UP)


def down(value):
    return lax.ppermute(value, "x", DOWN)


def far(value):
    return lax.ppermute(value, "x", FAR)


def inner(left, right):
    return lax.dot_general(
        left, right, (((1,), (1,)), ((), ())), preferred_element_type=jnp.float32
    )


def plain(left, right):
    return jnp.dot(left, right, preferred_element_type=jnp.float32)


VMEM = pl.BlockSpec(memory_space=pltpu.VMEM)
SMEM = pl.BlockSpec(memory_space=pltpu.SMEM)
HBM = pl.BlockSpec(memory_space=pltpu.HBM)
GRANT = 52


def params(mib):
    return pltpu.CompilerParams(vmem_limit_bytes=mib << 20)


FREE = pl.CostEstimate(flops=0, bytes_accessed=0, transcendentals=0)


def pack_kernel(plan, *refs):
    pieces, out, sems = refs[:-2], refs[-2], refs[-1]
    copies, at = [], 0
    for n, (k, start, count) in enumerate(plan):
        copies.append(
            pltpu.make_async_copy(
                pieces[k].at[:, pl.ds(start, count)], out.at[:, pl.ds(at, count)], sems.at[n]
            )
        )
        copies[n].start()
        at += count
    for copy in copies:
        copy.wait()


def pack(plan, *pieces):
    rows, wide = sum(count for _, _, count in plan), pieces[0].shape[2]
    return pl.pallas_call(
        functools.partial(pack_kernel, plan),
        out_shape=jax.ShapeDtypeStruct((2, rows, wide), jnp.bfloat16),
        in_specs=[pl.BlockSpec(memory_space=pl.ANY)] * len(pieces),
        out_specs=VMEM,
        scratch_shapes=[pltpu.SemaphoreType.DMA((len(plan),))],
        compiler_params=params(8),
        cost_estimate=FREE,
    )(*pieces)


def rows_kernel(*refs):
    pieces, out = refs[:10], refs[10]
    at = 0
    for k, piece in enumerate(pieces):
        count = piece.shape[1]
        for h in (0, 1):
            out[h ^ (k // 5), at:at + count, :] = piece[h]
        at += count


def rows_from(pieces):
    wide = pieces[0].shape[2]
    return pl.pallas_call(
        rows_kernel,
        out_shape=jax.ShapeDtypeStruct((2, 8 * N, wide), jnp.bfloat16),
        in_specs=[VMEM] * 10,
        out_specs=VMEM,
        compiler_params=params(12),
        cost_estimate=FREE,
    )(*pieces)


def scores_kernel(plan, *refs):
    blocks = sum(len(group) for group in plan)
    rows, parts, outs = refs[0], refs[1:1 + blocks], refs[1 + blocks:1 + 2 * blocks]
    left, held, made, row_sems, sems, out_sems = refs[1 + 2 * blocks:]
    row_copies = [pltpu.make_async_copy(rows.at[h], left.at[h], row_sems.at[h]) for h in (0, 1)]
    copies = []
    for n, group in enumerate(plan):
        at = 0
        copies.append([])
        for k in group:
            count = parts[k].shape[1]
            copies[n].append(pltpu.make_async_copy(parts[k], held.at[n, :, pl.ds(at, count)], sems.at[k]))
            at += count
    order = [row_copies[0]] + copies[0] + [row_copies[1]] + [copy for group in copies[1:] for copy in group]
    for copy in order:
        copy.start()
    results = []
    for n, group in enumerate(plan):
        for copy in copies[n]:
            copy.wait()
        if n == 0:
            row_copies[0].wait()
        total = inner(left[0], held[n, 0])
        if n == 0:
            row_copies[1].wait()
        made[n] = total + inner(left[1], held[n, 1])
        at = 0
        for k in group:
            count = parts[k].shape[1]
            results.append(pltpu.make_async_copy(made.at[n, :, pl.ds(at, count)], outs[k], out_sems.at[k]))
            results[-1].start()
            at += count
    for copy in results:
        copy.wait()


def scores_of(grant, rows, plan, *blocks):
    wide = rows.shape[2]
    return pl.pallas_call(
        functools.partial(scores_kernel, plan),
        out_shape=[jax.ShapeDtypeStruct((8 * N, a.shape[1]), jnp.float32) for a in blocks],
        in_specs=[pl.BlockSpec(memory_space=pl.ANY)] * (1 + len(blocks)),
        out_specs=[HBM] * len(blocks),
        scratch_shapes=[
            pltpu.VMEM((2, 8 * N, wide), jnp.bfloat16),
            pltpu.VMEM((len(plan), 2, 4 * N, wide), jnp.bfloat16),
            pltpu.VMEM((len(plan), 8 * N, 4 * N), jnp.float32),
            pltpu.SemaphoreType.DMA((2,)),
            pltpu.SemaphoreType.DMA((len(blocks),)),
            pltpu.SemaphoreType.DMA((len(blocks),)),
        ],
        compiler_params=params(grant),
        cost_estimate=FREE,
    )(rows, *blocks)


def masks(rows, cols, at, count):
    same_u, cross_u, cross_e = (rows[pl.ds(at, count), k:k + 1] for k in range(3))
    same_v, cross_v, cross_p = (cols[k:k + 1, :] for k in range(3))
    hit = cross_e == cross_p
    return same_u != same_v, (cross_u != cross_v) | hit, hit


def gather_parts(parts, held, sems):
    copies, at = [], 0
    for n, (part, size) in enumerate(zip(parts, PARTS)):
        copies.append(pltpu.make_async_copy(part, held.at[:, pl.ds(at, size)], sems.at[n]))
        copies[n].start()
        at += size
    return copies


HELD = [pltpu.VMEM((8 * N, J), jnp.float32), pltpu.SemaphoreType.DMA((len(PARTS),))]


STATS = 16


def stats_kernel(core, amax, *refs):
    parts, (rows, cols, out, keep, held, sems) = refs[:-6], refs[-6:]
    copies = gather_parts(parts, held, sems)
    step = 32
    inc = core[0] == 1
    keep[...] = jnp.zeros_like(keep)
    for copy in copies:
        copy.wait()

    @pl.loop(0, 4 * N // step)
    def _(k):
        at = pl.multiple_of(k * step, step)
        keep_s, keep_c, hit = masks(rows, cols, at, step)
        keep_c = keep_c & inc
        same = held[pl.ds(at, step), :] * SCALE
        cross = held[pl.ds(pl.multiple_of(at + 4 * N, step), step), :] * SCALE
        same = jnp.where(keep_s, same, -BIG)
        hits = jnp.sum(jnp.where(hit & inc, cross, 0.0), axis=1, keepdims=True)
        cross = jnp.where(keep_c, cross, -BIG)
        top = jnp.max(jnp.maximum(same, cross), axis=1, keepdims=True)
        total = jnp.sum(
            jnp.where(keep_s, jnp.exp(same - top), 0.0) + jnp.where(keep_c, jnp.exp(cross - top), 0.0),
            axis=1,
            keepdims=True,
        )
        group, low = k // (N // step), pl.multiple_of((k % (N // step)) * step, step)
        for n, value in enumerate((top, total, hits)):
            keep[n * 4 + group, pl.ds(low, step), :] = jnp.broadcast_to(value, (step, 128))

    for n in range(12):
        out[n:n + 1, :] = keep[n].T[0:1, :]
    out[12:16, :] = jnp.full((4, 128), amax[0], jnp.float32)


def stats_of(core, amax, parts, rows, cols):
    return pl.pallas_call(
        stats_kernel,
        out_shape=jax.ShapeDtypeStruct((STATS, 128), jnp.float32),
        in_specs=[SMEM] * 2 + [HBM] * len(parts) + [VMEM] * 2,
        out_specs=VMEM,
        scratch_shapes=[pltpu.VMEM((12, 128, 128), jnp.float32)] + HELD,
        compiler_params=params(GRANT),
        cost_estimate=FREE,
    )(core, amax, *parts, rows, cols)


TURNED = ((0, 1, 2, 3), (2, 0, 3, 1), (1, 3, 0, 2), (3, 2, 1, 0))


def merge_kernel(core, *refs):
    (mine, theirs), (out, ends) = (refs[:4], refs[4:8]), refs[8:]
    first = core[0] == 0
    a = [ref[...] for ref in mine]
    b = [ref[...] for ref in theirs]
    line = [jnp.where(first, u, v) for u, v in zip(a, b)] + [jnp.where(first, v, u) for u, v in zip(a, b)]
    loose = jnp.zeros((1, 128), jnp.float32)
    valid = lax.broadcasted_iota(jnp.int32, (1, 128), 1) < N
    for g in range(4):
        of = lambda k: [v[4 * k + t[g]:4 * k + t[g] + 1] for v, t in zip(line, TURNED * 2)]
        tops, sums, hits = of(0), of(1), of(2)
        top = functools.reduce(jnp.maximum, tops)
        total = sum(u * jnp.exp(t - top) for u, t in zip(sums, tops))
        lse = top + jnp.log(total)
        gap = lse - sum(hits)
        out[g:g + 1, :] = lse
        out[4 + g:5 + g, :] = gap
        loose = jnp.maximum(loose, jnp.where(valid, 1.0 - jnp.exp(-gap), 0.0))
        if g == 0:
            ends[0:1, :] = lse
    ends[1:2, :] = loose
    most = functools.reduce(jnp.maximum, [v[12:13] for v in line])
    ends[2:8, :] = jnp.broadcast_to(most, (6, 128))


def merged(core, mine, theirs):
    return pl.pallas_call(
        merge_kernel,
        out_shape=[jax.ShapeDtypeStruct((8, 128), jnp.float32)] * 2,
        in_specs=[SMEM] + [VMEM] * 8,
        out_specs=[VMEM] * 2,
        compiler_params=params(4),
        cost_estimate=FREE,
    )(core, *mine, *theirs)


def lanes_of(rows):
    lane = lax.broadcasted_iota(jnp.int32, (8, 128), 1)
    wide = lambda v: jnp.broadcast_to(v, (8, 128))
    turn = lambda v, by: pltpu.roll(wide(v), by, axis=1) if by % 128 else wide(v)
    out = []
    for b in range(3):
        for a in (0, 2):
            out.append(jnp.where(lane < 64, wide(rows[4 * b + a]), turn(rows[4 * b + a + 1], 64)))
    for h in (0, 1):
        q = [turn(rows[12 + a], (32 * a - 32 * h) % 128) for a in range(4)]
        out.append(jnp.where(lane < 64, jnp.where(lane < 32, q[0], q[1]), jnp.where(lane < 96, q[2], q[3])))
    return jnp.concatenate(out, axis=1)[0:1]


def weights_kernel(first, count, core, *refs):
    parts, (rows, cols, lse_i, *plane, out, bound, col, held, sems) = refs[:len(PARTS)], refs[len(PARTS):]
    copies = gather_parts(parts, held, sems)
    step = 32
    w = core[0]
    for g in range(4):
        line = jnp.broadcast_to(lse_i[g:g + 1, :], (128, 128)).T[:N]
        col[0, g * N:(g + 1) * N, :] = line
        col[1, g * N:(g + 1) * N, :] = jnp.where(w == 1, line, 0.0)
    ends = [ref[8 * a:8 * a + 8, :] for ref in plane for a in range(4)]
    lj = lanes_of([v[0:1] for v in ends])
    cross_j = jnp.where(w == 1, 0.0, lj)
    loose = jnp.max(functools.reduce(jnp.maximum, [v[1:2] for v in ends]), axis=1, keepdims=True)
    most = jnp.max(functools.reduce(jnp.maximum, [v[2:3] for v in ends]), axis=1, keepdims=True)
    bound[...] = jnp.broadcast_to(jnp.maximum(loose, 1e-3) * jnp.maximum(most, 1e-20), (8, 128))
    for copy in copies:
        copy.wait()

    @pl.loop(0, count * N // step)
    def _(k):
        at = pl.multiple_of(first * N + k * step, step)
        keep_s, keep_c, hit = masks(rows, cols, at, step)
        li = col[0, pl.ds(at, step), 0:1]
        lc = col[1, pl.ds(at, step), 0:1]
        same = held[pl.ds(at, step), :] * SCALE
        cross = held[pl.ds(pl.multiple_of(at + 4 * N, step), step), :] * SCALE
        m_s = jnp.where(keep_s, jnp.exp(same - li) + jnp.exp(same - lj), 0.0)
        m_c = jnp.where(keep_c, jnp.exp((cross - lc) - cross_j), 0.0) - jnp.where(hit, 1.0, 0.0)
        group = k // (N // step)
        base = group * 2 * N + (k % (N // step)) * step
        out[pl.ds(pl.multiple_of(base + w * N, step), step), :] = m_s.astype(jnp.bfloat16)
        out[pl.ds(pl.multiple_of(base + (1 - w) * N, step), step), :] = m_c.astype(jnp.bfloat16)


def weights_of(first, count, core, parts, rows, cols, lse_i, plane):
    return pl.pallas_call(
        functools.partial(weights_kernel, first, count),
        out_shape=[
            jax.ShapeDtypeStruct((count * 2 * N, J), jnp.bfloat16),
            jax.ShapeDtypeStruct((8, 128), jnp.float32),
        ],
        in_specs=[SMEM] + [HBM] * len(parts) + [VMEM] * 7,
        out_specs=[VMEM] * 2,
        scratch_shapes=[pltpu.VMEM((2, 4 * N, 128), jnp.float32)] + HELD,
        compiler_params=params(GRANT),
        cost_estimate=FREE,
    )(core, *parts, rows, cols, lse_i, *plane)


def product_kernel(scaled, bound, mine, theirs, *refs):
    count = mine.shape[0] // (2 * N)
    blocks, outs, (held, sems) = refs[:2 * len(PARTS)], refs[2 * len(PARTS):-2], refs[-2:]
    copies = ([], [])
    for k in (0, 1):
        at = 0
        for n, size in enumerate(PARTS):
            i = k * len(PARTS) + n
            copies[k].append(pltpu.make_async_copy(blocks[i].at[k], held.at[k, pl.ds(at, size)], sems.at[i]))
            copies[k][-1].start()
            at += size
    shrink = 1.0 / bound[0:1, 0:1]
    step = 512
    for k, weights in enumerate((mine, theirs)):
        for copy in copies[k]:
            copy.wait()

        @pl.loop(0, held.shape[2] // step)
        def _(j):
            here = pl.ds(pl.multiple_of(j * step, step), step)
            term = plain(weights[...], held[k, :, here])
            for g in range(count):
                part = term[2 * N * g:2 * N * (g + 1)]
                if k == 0:
                    outs[g][:, here] = part
                else:
                    part = outs[g][:, here] + part
                    outs[g][:, here] = part * shrink if g >= scaled else part


def product_of(scaled, bound, mine, theirs, blocks, others):
    rows, wide = mine.shape[0], blocks[0].shape[2]
    outs = rows // (2 * N)
    return pl.pallas_call(
        functools.partial(product_kernel, scaled),
        out_shape=[jax.ShapeDtypeStruct((2 * N, wide), jnp.float32)] * outs,
        in_specs=[VMEM] * 3 + [HBM] * (2 * len(PARTS)),
        out_specs=[VMEM] * outs,
        scratch_shapes=[pltpu.VMEM((2, J, wide), jnp.bfloat16), pltpu.SemaphoreType.DMA((2 * len(PARTS),))],
        compiler_params=params(GRANT),
        cost_estimate=FREE,
    )(bound, mine, theirs, *blocks, *others)


def after(value, *others):
    return lax.optimization_barrier((value, *others))[0]


def settle(*values):
    return lax.optimization_barrier(values)


def body(queries, passages, passage_ids, pos_index):
    y, z, x, w = (lax.axis_index(name) for name in GRID)
    first = w == 0
    core = w.astype(jnp.int32).reshape(1)
    pick = lambda a, b: jnp.where(first, a, b)
    rows_of = functools.partial(lax.slice_in_dim, axis=1)
    low = lambda a: [rows_of(a, k * N, k * N + H) for k in range(a.shape[1] // N)]
    high = lambda a: [rows_of(a, k * N + H, (k + 1) * N) for k in range(a.shape[1] // N)]
    join = lambda parts: jnp.concatenate(parts, axis=1)
    line = lambda v, k: (up, far, down)[k - 1](v)
    by_first = lambda v, k: along(v, FIRST[k])
    by_second = lambda v, k: along(v, SECOND[k])
    ring = lambda v, send: [v] + [send(v, k) for k in RING[1:]]

    got = swap(pick(passages, queries))
    own = jnp.stack([pick(queries, passages), got])
    ints = jnp.stack([passage_ids, pos_index])

    fl, fr, own, *ints = settle(along(own, FIRST[1]), along(own, FIRST[3]), own, *ring(ints, line))
    f_low, f_high, own, fl, fr, *ints = settle(
        along(low(fl)[0], FIRST[1]), along(high(fr)[0], FIRST[3]), own, fl, fr, *ring(jnp.stack(ints), by_first)
    )
    group = pack(((0, 0, N), (1, 0, N), (2, 0, N), (3, 0, H), (4, 0, H)), own, fl, fr, f_low, f_high)
    group, own, *ints = settle(group, own, *ring(jnp.stack(ints), by_second))
    ints = jnp.stack(ints)
    ids = ints[..., 0, :]
    dev, off = ints[..., 1, :] // N, ints[..., 1, :] % N
    near = lambda at, other: (lambda d: d ^ (d >> 1))((at - other) % 4)
    dy, dz, dx = near(y, dev // 16), near(z, dev // 4 % 4), near(x, dev % 4)
    pos = ((pick(dz, dy) * 4 + pick(dy, dz)) * 4 + dx) * N + off
    pair = jnp.arange(64 * N, dtype=jnp.int32).reshape(4, 4, 4, N)
    i_of = lambda t: t[0, 0].reshape(-1)
    j_of = lambda t: jnp.concatenate(
        [t[:3, :, 0].reshape(-1), t[3, :, 0].reshape(4, 2, H).transpose(1, 0, 2).reshape(-1)]
    )
    i_pair, i_id, i_pos = i_of(pair), i_of(ids), i_of(pos)
    j_pair, j_id, j_pos = j_of(pair), j_of(ids), j_of(pos)
    table, every = ids.reshape(1, -1), pair.reshape(1, -1)
    look = lambda at: jnp.sum(jnp.where(at[:, None] == every, table, 0), axis=1)
    i_tgt, j_tgt = look(i_pos), look(j_pos)
    rows = jnp.stack([pick(i_pair, i_id), pick(i_id, i_tgt), pick(i_pair, i_pos)] + [i_pair] * 5, axis=1)
    cols = jnp.stack([pick(j_pair, j_id), pick(j_tgt, j_id), pick(j_pos, j_pair)] + [j_pair] * 5)
    amax = jnp.maximum(
        jnp.max(jnp.abs(queries.astype(jnp.float32))), jnp.max(jnp.abs(passages.astype(jnp.float32)))
    )
    xl, xr = up(own), down(own)
    mine = [own, xl, xr, up(low(xl)[0]), down(high(xr)[0])]
    dl, dr, group, rows, cols, amax, *held = settle(
        along(group, SECOND[1]), along(group, SECOND[3]), group, rows, cols, amax, *mine, *[swap(a) for a in mine]
    )
    to_l = pack(tuple((0, k * N, H) for k in range(4)), dl)
    to_r = pack(tuple((0, k * N + H, H) for k in range(4)), dr)
    rows_i = rows_from([after(held[0], to_l, to_r)] + held[1:])
    blocks = [group, dl, dr]
    parts = scores_of(24, rows_i, ((0,), (1,), (2,)), *blocks)
    others = [swap(after(a, rows_i)) for a in blocks]
    gl, gr, *held = settle(along(to_l, SECOND[1]), along(to_r, SECOND[3]), *parts, *blocks)
    parts, blocks = held[:3], held[3:]
    blocks += [gl, gr]

    parts += scores_of(56, rows_i, ((0, 1),), gl, gr)
    found, *held = settle(stats_of(core, amax.reshape(1), parts, rows, cols), *others, swap(gl), swap(gr), *blocks)
    others, blocks = held[:5], held[5:]
    found = ring(found, line)
    lse_i, ends = merged(core, found, [swap(a) for a in found])
    loss = lse_i[4, :N]
    plane = ring(jnp.concatenate(ring(ends, by_first)), by_second)

    f16, f32 = jnp.float16, jnp.float32
    args = (parts, rows, cols, lse_i, plane)
    m_far, bound = weights_of(3, 1, core, *args)
    m_far_o = swap(m_far)
    m_rest, _ = weights_of(0, 3, after(core, m_far), *args)
    (opposite,) = product_of(0, bound, m_far, m_far_o, blocks, others)
    opposite = opposite.astype(f16)
    got_q, got_p, here, to_down, to_up = settle(
        up(opposite[:N]), down(opposite[N:]), *product_of(1, bound, m_rest, swap(m_rest), blocks, others)
    )
    below = up(jnp.concatenate([to_up[:N] + got_q.astype(f32), to_up[N:]]).astype(f16))
    above = down(jnp.concatenate([to_down[:N], to_down[N:] + got_p.astype(f32)]).astype(f16))
    grad = here + (below.astype(f32) + above.astype(f32)) * bound[0, 0]
    grad_q, grad_p = grad[:N], grad[N:]
    return loss, grad_q, grad_p


def solution(mesh):
    grid = Mesh(mesh.devices.reshape(4, 4, 4, 2), GRID)
    pair = ("y", "z", "x")
    placed = (P(pair, "w"), P(pair, "w"), P(pair), P(pair))
    return jax.shard_map(
        body,
        mesh=grid,
        in_specs=placed,
        out_specs=(P(pair), P(pair, "w"), P(pair, "w")),
        check_vma=False,
    )
```

```python
import functools
import math

import jax
import jax.numpy as jnp
from jax import lax
from jax.experimental import pallas as pl
from jax.experimental.pallas import tpu as pltpu
from jax.sharding import Mesh, PartitionSpec as P

D = 4096
N = 64
H = N // 2
SCALE = 3.0 / math.sqrt(D)
BIG = 1e30
GRID = ("y", "z", "x", "w")
UP = [(i, (i + 1) % 4) for i in range(4)]
DOWN = [(i, (i - 1) % 4) for i in range(4)]
FAR = [(i, (i + 2) % 4) for i in range(4)]
RING = (0, 1, 3, 2)
PARTS = (256, 256, 256, 128, 128)
J = sum(PARTS)


def steps(first, second, by):
    moves = []
    for y in range(4):
        for z in range(4):
            for x in range(4):
                for w in range(2):
                    axis = second if w else first
                    to_y, to_z = ((y + by) % 4, z) if axis == "y" else (y, (z + by) % 4)
                    flat = lambda y, z: ((y * 4 + z) * 4 + x) * 2 + w
                    moves.append((flat(y, z), flat(to_y, to_z)))
    return moves


FIRST = {by: steps("y", "z", by) for by in (1, 2, 3)}
SECOND = {by: steps("z", "y", by) for by in (1, 2, 3)}


def along(value, moves):
    return lax.ppermute(value, GRID, moves)


def swap(value):
    return lax.ppermute(value, "w", [(0, 1), (1, 0)])


def up(value):
    return lax.ppermute(value, "x", UP)


def down(value):
    return lax.ppermute(value, "x", DOWN)


def far(value):
    return lax.ppermute(value, "x", FAR)


def inner(left, right):
    return lax.dot_general(
        left, right, (((1,), (1,)), ((), ())), preferred_element_type=jnp.float32
    )


def plain(left, right):
    return jnp.dot(left, right, preferred_element_type=jnp.float32)


VMEM = pl.BlockSpec(memory_space=pltpu.VMEM)
SMEM = pl.BlockSpec(memory_space=pltpu.SMEM)
HBM = pl.BlockSpec(memory_space=pltpu.HBM)
def params(mib):
    return pltpu.CompilerParams(vmem_limit_bytes=mib << 20)


FREE = pl.CostEstimate(flops=0, bytes_accessed=0, transcendentals=0)


def pack_kernel(plan, *refs):
    pieces, out, sems = refs[:-2], refs[-2], refs[-1]
    copies, at = [], 0
    for n, (k, start, count) in enumerate(plan):
        copies.append(
            pltpu.make_async_copy(
                pieces[k].at[:, pl.ds(start, count)], out.at[:, pl.ds(at, count)], sems.at[n]
            )
        )
        copies[n].start()
        at += count
    for copy in copies:
        copy.wait()


def pack(plan, *pieces):
    rows, wide = sum(count for _, _, count in plan), pieces[0].shape[2]
    return pl.pallas_call(
        functools.partial(pack_kernel, plan),
        out_shape=jax.ShapeDtypeStruct((2, rows, wide), jnp.bfloat16),
        in_specs=[pl.BlockSpec(memory_space=pl.ANY)] * len(pieces),
        out_specs=VMEM,
        scratch_shapes=[pltpu.SemaphoreType.DMA((len(plan),))],
        compiler_params=params(8),
        cost_estimate=FREE,
    )(*pieces)


def rows_kernel(*refs):
    pieces, out = refs[:10], refs[10]
    at = 0
    for k, piece in enumerate(pieces):
        count = piece.shape[1]
        for h in (0, 1):
            out[h ^ (k // 5), at:at + count, :] = piece[h]
        at += count


def rows_from(pieces):
    wide = pieces[0].shape[2]
    return pl.pallas_call(
        rows_kernel,
        out_shape=jax.ShapeDtypeStruct((2, 8 * N, wide), jnp.bfloat16),
        in_specs=[VMEM] * 10,
        out_specs=VMEM,
        compiler_params=params(12),
        cost_estimate=FREE,
    )(*pieces)


def scores_kernel(plan, *refs):
    blocks = sum(len(group) for group in plan)
    rows, parts, outs = refs[0], refs[1:1 + blocks], refs[1 + blocks:1 + 2 * blocks]
    left, held, made, row_sems, sems, out_sems = refs[1 + 2 * blocks:]
    row_copies = [pltpu.make_async_copy(rows.at[h], left.at[h], row_sems.at[h]) for h in (0, 1)]
    copies = []
    for n, group in enumerate(plan):
        at = 0
        copies.append([])
        for k in group:
            count = parts[k].shape[1]
            copies[n].append(pltpu.make_async_copy(parts[k], held.at[n, :, pl.ds(at, count)], sems.at[k]))
            at += count
    order = [row_copies[0]] + copies[0] + [row_copies[1]] + [copy for group in copies[1:] for copy in group]
    for copy in order:
        copy.start()
    results = []
    for n, group in enumerate(plan):
        for copy in copies[n]:
            copy.wait()
        if n == 0:
            row_copies[0].wait()
        total = inner(left[0], held[n, 0])
        if n == 0:
            row_copies[1].wait()
        made[n] = total + inner(left[1], held[n, 1])
        at = 0
        for k in group:
            count = parts[k].shape[1]
            results.append(pltpu.make_async_copy(made.at[n, :, pl.ds(at, count)], outs[k], out_sems.at[k]))
            results[-1].start()
            at += count
    for copy in results:
        copy.wait()


def scores_of(grant, rows, plan, *blocks):
    wide = rows.shape[2]
    return pl.pallas_call(
        functools.partial(scores_kernel, plan),
        out_shape=[jax.ShapeDtypeStruct((8 * N, a.shape[1]), jnp.float32) for a in blocks],
        in_specs=[pl.BlockSpec(memory_space=pl.ANY)] * (1 + len(blocks)),
        out_specs=[pl.BlockSpec(memory_space=pl.ANY)] * len(blocks),
        scratch_shapes=[
            pltpu.VMEM((2, 8 * N, wide), jnp.bfloat16),
            pltpu.VMEM((len(plan), 2, 4 * N, wide), jnp.bfloat16),
            pltpu.VMEM((len(plan), 8 * N, 4 * N), jnp.float32),
            pltpu.SemaphoreType.DMA((2,)),
            pltpu.SemaphoreType.DMA((len(blocks),)),
            pltpu.SemaphoreType.DMA((len(blocks),)),
        ],
        compiler_params=params(grant),
        cost_estimate=FREE,
    )(rows, *blocks)


def masks(rows, cols, at, count):
    same_u, cross_u, cross_e = (rows[pl.ds(at, count), k:k + 1] for k in range(3))
    same_v, cross_v, cross_p = (cols[k:k + 1, :] for k in range(3))
    hit = cross_e == cross_p
    return same_u != same_v, (cross_u != cross_v) | hit, hit


def scores_at(parts, at, count):
    return jnp.concatenate([part[pl.ds(at, count), :] for part in parts], axis=1) * SCALE


STATS = 16


def stats_kernel(core, amax, *refs):
    parts, (rows, cols, out, keep) = refs[:-4], refs[-4:]
    step = 32
    inc = core[0] == 1
    keep[...] = jnp.zeros_like(keep)

    @pl.loop(0, 4 * N // step)
    def _(k):
        at = pl.multiple_of(k * step, step)
        keep_s, keep_c, hit = masks(rows, cols, at, step)
        keep_c = keep_c & inc
        same = scores_at(parts, at, step)
        cross = scores_at(parts, pl.multiple_of(at + 4 * N, step), step)
        same = jnp.where(keep_s, same, -BIG)
        hits = jnp.sum(jnp.where(hit & inc, cross, 0.0), axis=1, keepdims=True)
        cross = jnp.where(keep_c, cross, -BIG)
        top = jnp.max(jnp.maximum(same, cross), axis=1, keepdims=True)
        total = jnp.sum(
            jnp.where(keep_s, jnp.exp(same - top), 0.0) + jnp.where(keep_c, jnp.exp(cross - top), 0.0),
            axis=1,
            keepdims=True,
        )
        group, low = k // (N // step), pl.multiple_of((k % (N // step)) * step, step)
        for n, value in enumerate((top, total, hits)):
            keep[n * 4 + group, pl.ds(low, step), :] = jnp.broadcast_to(value, (step, 128))

    for n in range(12):
        out[n:n + 1, :] = keep[n].T[0:1, :]
    out[12:16, :] = jnp.full((4, 128), amax[0], jnp.float32)


def stats_of(core, amax, parts, rows, cols):
    return pl.pallas_call(
        stats_kernel,
        out_shape=jax.ShapeDtypeStruct((STATS, 128), jnp.float32),
        in_specs=[SMEM] * 2 + [VMEM] * (len(parts) + 2),
        out_specs=VMEM,
        scratch_shapes=[pltpu.VMEM((12, 128, 128), jnp.float32)],
        compiler_params=params(8),
        cost_estimate=FREE,
    )(core, amax, *parts, rows, cols)


TURNED = ((0, 1, 2, 3), (2, 0, 3, 1), (1, 3, 0, 2), (3, 2, 1, 0))


def merge_kernel(core, *refs):
    (mine, theirs), (out, ends) = (refs[:4], refs[4:8]), refs[8:]
    first = core[0] == 0
    a = [ref[...] for ref in mine]
    b = [ref[...] for ref in theirs]
    line = [jnp.where(first, u, v) for u, v in zip(a, b)] + [jnp.where(first, v, u) for u, v in zip(a, b)]
    loose = jnp.zeros((1, 128), jnp.float32)
    valid = lax.broadcasted_iota(jnp.int32, (1, 128), 1) < N
    for g in range(4):
        of = lambda k: [v[4 * k + t[g]:4 * k + t[g] + 1] for v, t in zip(line, TURNED * 2)]
        tops, sums, hits = of(0), of(1), of(2)
        top = functools.reduce(jnp.maximum, tops)
        total = sum(u * jnp.exp(t - top) for u, t in zip(sums, tops))
        lse = top + jnp.log(total)
        gap = lse - sum(hits)
        out[g:g + 1, :] = lse
        out[4 + g:5 + g, :] = gap
        loose = jnp.maximum(loose, jnp.where(valid, 1.0 - jnp.exp(-gap), 0.0))
        if g == 0:
            ends[0:1, :] = lse
    ends[1:2, :] = loose
    most = functools.reduce(jnp.maximum, [v[12:13] for v in line])
    ends[2:8, :] = jnp.broadcast_to(most, (6, 128))


def merged(core, mine, theirs):
    return pl.pallas_call(
        merge_kernel,
        out_shape=[jax.ShapeDtypeStruct((8, 128), jnp.float32)] * 2,
        in_specs=[SMEM] + [VMEM] * 8,
        out_specs=[VMEM] * 2,
        compiler_params=params(4),
        cost_estimate=FREE,
    )(core, *mine, *theirs)


def lanes_of(rows):
    lane = lax.broadcasted_iota(jnp.int32, (8, 128), 1)
    wide = lambda v: jnp.broadcast_to(v, (8, 128))
    turn = lambda v, by: pltpu.roll(wide(v), by, axis=1) if by % 128 else wide(v)
    out = []
    for b in range(3):
        for a in (0, 2):
            out.append(jnp.where(lane < 64, wide(rows[4 * b + a]), turn(rows[4 * b + a + 1], 64)))
    for h in (0, 1):
        q = [turn(rows[12 + a], (32 * a - 32 * h) % 128) for a in range(4)]
        out.append(jnp.where(lane < 64, jnp.where(lane < 32, q[0], q[1]), jnp.where(lane < 96, q[2], q[3])))
    return jnp.concatenate(out, axis=1)[0:1]


def weights_kernel(first, count, core, *refs):
    parts, (rows, cols, lse_i, *plane, out, bound, col) = refs[:len(PARTS)], refs[len(PARTS):]
    step = 32
    w = core[0]
    for g in range(4):
        line = jnp.broadcast_to(lse_i[g:g + 1, :], (128, 128)).T[:N]
        col[0, g * N:(g + 1) * N, :] = line
        col[1, g * N:(g + 1) * N, :] = jnp.where(w == 1, line, 0.0)
    ends = [ref[8 * a:8 * a + 8, :] for ref in plane for a in range(4)]
    lj = lanes_of([v[0:1] for v in ends])
    cross_j = jnp.where(w == 1, 0.0, lj)
    loose = jnp.max(functools.reduce(jnp.maximum, [v[1:2] for v in ends]), axis=1, keepdims=True)
    most = jnp.max(functools.reduce(jnp.maximum, [v[2:3] for v in ends]), axis=1, keepdims=True)
    bound[...] = jnp.broadcast_to(jnp.maximum(loose, 1e-3) * jnp.maximum(most, 1e-20), (8, 128))

    @pl.loop(0, count * N // step)
    def _(k):
        at = pl.multiple_of(first * N + k * step, step)
        keep_s, keep_c, hit = masks(rows, cols, at, step)
        li = col[0, pl.ds(at, step), 0:1]
        lc = col[1, pl.ds(at, step), 0:1]
        same = scores_at(parts, at, step)
        cross = scores_at(parts, pl.multiple_of(at + 4 * N, step), step)
        m_s = jnp.where(keep_s, jnp.exp(same - li) + jnp.exp(same - lj), 0.0)
        m_c = jnp.where(keep_c, jnp.exp((cross - lc) - cross_j), 0.0) - jnp.where(hit, 1.0, 0.0)
        group = k // (N // step)
        base = group * 2 * N + (k % (N // step)) * step
        out[pl.ds(pl.multiple_of(base + w * N, step), step), :] = m_s.astype(jnp.bfloat16)
        out[pl.ds(pl.multiple_of(base + (1 - w) * N, step), step), :] = m_c.astype(jnp.bfloat16)


def weights_of(first, count, core, parts, rows, cols, lse_i, plane):
    return pl.pallas_call(
        functools.partial(weights_kernel, first, count),
        out_shape=[
            jax.ShapeDtypeStruct((count * 2 * N, J), jnp.bfloat16),
            jax.ShapeDtypeStruct((8, 128), jnp.float32),
        ],
        in_specs=[SMEM] + [VMEM] * (len(parts) + 7),
        out_specs=[VMEM] * 2,
        scratch_shapes=[pltpu.VMEM((2, 4 * N, 128), jnp.float32)],
        compiler_params=params(8),
        cost_estimate=FREE,
    )(core, *parts, rows, cols, lse_i, *plane)


def product_kernel(scaled, bound, mine, theirs, *refs):
    count = mine.shape[0] // (2 * N)
    blocks, outs, (held, sems) = refs[:2 * len(PARTS)], refs[2 * len(PARTS):-2], refs[-2:]
    copies = ([], [])
    for k in (0, 1):
        at = 0
        for n, size in enumerate(PARTS):
            i = k * len(PARTS) + n
            copies[k].append(pltpu.make_async_copy(blocks[i].at[k], held.at[k, pl.ds(at, size)], sems.at[i]))
            copies[k][-1].start()
            at += size
    shrink = 1.0 / bound[0:1, 0:1]
    step = 512
    for k, weights in enumerate((mine, theirs)):
        for copy in copies[k]:
            copy.wait()

        @pl.loop(0, held.shape[2] // step)
        def _(j):
            here = pl.ds(pl.multiple_of(j * step, step), step)
            term = plain(weights[...], held[k, :, here])
            for g in range(count):
                part = term[2 * N * g:2 * N * (g + 1)]
                if k == 0:
                    outs[g][:, here] = part
                else:
                    part = outs[g][:, here] + part
                    outs[g][:, here] = part * shrink if g >= scaled else part


def product_of(scaled, bound, mine, theirs, blocks, others):
    rows, wide = mine.shape[0], blocks[0].shape[2]
    outs = rows // (2 * N)
    return pl.pallas_call(
        functools.partial(product_kernel, scaled),
        out_shape=[jax.ShapeDtypeStruct((2 * N, wide), jnp.float32)] * outs,
        in_specs=[VMEM] * 3 + [pl.BlockSpec(memory_space=pl.ANY)] * (2 * len(PARTS)),
        out_specs=[VMEM] * outs,
        scratch_shapes=[pltpu.VMEM((2, J, wide), jnp.bfloat16), pltpu.SemaphoreType.DMA((2 * len(PARTS),))],
        compiler_params=params(20),
        cost_estimate=FREE,
    )(bound, mine, theirs, *blocks, *others)


def after(value, *others):
    return lax.optimization_barrier((value, *others))[0]


def settle(*values):
    return lax.optimization_barrier(values)


def body(queries, passages, passage_ids, pos_index):
    y, z, x, w = (lax.axis_index(name) for name in GRID)
    first = w == 0
    core = w.astype(jnp.int32).reshape(1)
    pick = lambda a, b: jnp.where(first, a, b)
    rows_of = functools.partial(lax.slice_in_dim, axis=1)
    low = lambda a: [rows_of(a, k * N, k * N + H) for k in range(a.shape[1] // N)]
    high = lambda a: [rows_of(a, k * N + H, (k + 1) * N) for k in range(a.shape[1] // N)]
    join = lambda parts: jnp.concatenate(parts, axis=1)
    line = lambda v, k: (up, far, down)[k - 1](v)
    by_first = lambda v, k: along(v, FIRST[k])
    by_second = lambda v, k: along(v, SECOND[k])
    ring = lambda v, send: [v] + [send(v, k) for k in RING[1:]]

    got = swap(pick(passages, queries))
    own = jnp.stack([pick(queries, passages), got])
    ints = jnp.stack([passage_ids, pos_index])

    fl, fr, own, *ints = settle(along(own, FIRST[1]), along(own, FIRST[3]), own, *ring(ints, line))
    f_low, f_high, own, fl, fr, *ints = settle(
        along(low(fl)[0], FIRST[1]), along(high(fr)[0], FIRST[3]), own, fl, fr, *ring(jnp.stack(ints), by_first)
    )
    group = pack(((0, 0, N), (1, 0, N), (2, 0, N), (3, 0, H), (4, 0, H)), own, fl, fr, f_low, f_high)
    group, own, *ints = settle(group, own, *ring(jnp.stack(ints), by_second))
    ints = jnp.stack(ints)
    ids = ints[..., 0, :]
    dev, off = ints[..., 1, :] // N, ints[..., 1, :] % N
    near = lambda at, other: (lambda d: d ^ (d >> 1))((at - other) % 4)
    dy, dz, dx = near(y, dev // 16), near(z, dev // 4 % 4), near(x, dev % 4)
    pos = ((pick(dz, dy) * 4 + pick(dy, dz)) * 4 + dx) * N + off
    pair = jnp.arange(64 * N, dtype=jnp.int32).reshape(4, 4, 4, N)
    i_of = lambda t: t[0, 0].reshape(-1)
    j_of = lambda t: jnp.concatenate(
        [t[:3, :, 0].reshape(-1), t[3, :, 0].reshape(4, 2, H).transpose(1, 0, 2).reshape(-1)]
    )
    i_pair, i_id, i_pos = i_of(pair), i_of(ids), i_of(pos)
    j_pair, j_id, j_pos = j_of(pair), j_of(ids), j_of(pos)
    table, every = ids.reshape(1, -1), pair.reshape(1, -1)
    look = lambda at: jnp.sum(jnp.where(at[:, None] == every, table, 0), axis=1)
    i_tgt, j_tgt = look(i_pos), look(j_pos)
    rows = jnp.stack([pick(i_pair, i_id), pick(i_id, i_tgt), pick(i_pair, i_pos)] + [i_pair] * 5, axis=1)
    cols = jnp.stack([pick(j_pair, j_id), pick(j_tgt, j_id), pick(j_pos, j_pair)] + [j_pair] * 5)
    amax = jnp.maximum(
        jnp.max(jnp.abs(queries.astype(jnp.float32))), jnp.max(jnp.abs(passages.astype(jnp.float32)))
    )
    xl, xr = up(own), down(own)
    mine = [own, xl, xr, up(low(xl)[0]), down(high(xr)[0])]
    dl, dr, group, rows, cols, amax, *held = settle(
        along(group, SECOND[1]), along(group, SECOND[3]), group, rows, cols, amax, *mine, *[swap(a) for a in mine]
    )
    to_l = pack(tuple((0, k * N, H) for k in range(4)), dl)
    to_r = pack(tuple((0, k * N + H, H) for k in range(4)), dr)
    rows_i = rows_from([after(held[0], to_l, to_r)] + held[1:])
    blocks = [group, dl, dr]
    parts = scores_of(24, rows_i, ((0,), (1,), (2,)), *blocks)
    others = [swap(after(a, rows_i)) for a in blocks]
    gl, gr, *held = settle(along(to_l, SECOND[1]), along(to_r, SECOND[3]), *parts, *blocks)
    parts, blocks = held[:3], held[3:]
    blocks += [gl, gr]

    parts += scores_of(24, rows_i, ((0, 1),), gl, gr)
    found, *held = settle(stats_of(core, amax.reshape(1), parts, rows, cols), *others, swap(gl), swap(gr), *blocks)
    others, blocks = held[:5], held[5:]
    found = ring(found, line)
    lse_i, ends = merged(core, found, [swap(a) for a in found])
    loss = lse_i[4, :N]
    plane = ring(jnp.concatenate(ring(ends, by_first)), by_second)

    f16, f32 = jnp.float16, jnp.float32
    args = (parts, rows, cols, lse_i, plane)
    m_far, bound = weights_of(3, 1, core, *args)
    m_far_o = swap(m_far)
    m_rest, _ = weights_of(0, 3, after(core, m_far), *args)
    (opposite,) = product_of(0, bound, m_far, m_far_o, blocks, others)
    opposite = opposite.astype(f16)
    got_q, got_p, here, to_down, to_up = settle(
        up(opposite[:N]), down(opposite[N:]), *product_of(1, bound, m_rest, swap(m_rest), blocks, others)
    )
    below = up(jnp.concatenate([to_up[:N] + got_q.astype(f32), to_up[N:]]).astype(f16))
    above = down(jnp.concatenate([to_down[:N], to_down[N:] + got_p.astype(f32)]).astype(f16))
    grad = here + (below.astype(f32) + above.astype(f32)) * bound[0, 0]
    grad_q, grad_p = grad[:N], grad[N:]
    return loss, grad_q, grad_p


def solution(mesh):
    grid = Mesh(mesh.devices.reshape(4, 4, 4, 2), GRID)
    pair = ("y", "z", "x")
    placed = (P(pair, "w"), P(pair, "w"), P(pair), P(pair))
    return jax.shard_map(
        body,
        mesh=grid,
        in_specs=placed,
        out_specs=(P(pair), P(pair, "w"), P(pair, "w")),
        check_vma=False,
    )
```

```python
import functools
import math

import jax
import jax.numpy as jnp
from jax import lax
from jax.experimental import pallas as pl
from jax.experimental.pallas import tpu as pltpu
from jax.sharding import Mesh, PartitionSpec as P

D = 4096
N = 64
H = N // 2
SCALE = 3.0 / math.sqrt(D)
BIG = 1e30
GRID = ("y", "z", "x", "w")
UP = [(i, (i + 1) % 4) for i in range(4)]
DOWN = [(i, (i - 1) % 4) for i in range(4)]
FAR = [(i, (i + 2) % 4) for i in range(4)]
RING = (0, 1, 3, 2)
PARTS = (256, 256, 256, 128, 128)
J = sum(PARTS)


def steps(first, second, by):
    moves = []
    for y in range(4):
        for z in range(4):
            for x in range(4):
                for w in range(2):
                    axis = second if w else first
                    to_y, to_z = ((y + by) % 4, z) if axis == "y" else (y, (z + by) % 4)
                    flat = lambda y, z: ((y * 4 + z) * 4 + x) * 2 + w
                    moves.append((flat(y, z), flat(to_y, to_z)))
    return moves


FIRST = {by: steps("y", "z", by) for by in (1, 2, 3)}
SECOND = {by: steps("z", "y", by) for by in (1, 2, 3)}


def along(value, moves):
    return lax.ppermute(value, GRID, moves)


def swap(value):
    return lax.ppermute(value, "w", [(0, 1), (1, 0)])


def up(value):
    return lax.ppermute(value, "x", UP)


def down(value):
    return lax.ppermute(value, "x", DOWN)


def far(value):
    return lax.ppermute(value, "x", FAR)


def inner(left, right):
    return lax.dot_general(
        left, right, (((1,), (1,)), ((), ())), preferred_element_type=jnp.float32
    )


def plain(left, right):
    return jnp.dot(left, right, preferred_element_type=jnp.float32)


VMEM = pl.BlockSpec(memory_space=pltpu.VMEM)
SMEM = pl.BlockSpec(memory_space=pltpu.SMEM)
def params(mib):
    return pltpu.CompilerParams(vmem_limit_bytes=mib << 20)


FREE = pl.CostEstimate(flops=0, bytes_accessed=0, transcendentals=0)


def pack_kernel(plan, *refs):
    pieces, out, sems = refs[:-2], refs[-2], refs[-1]
    copies, at = [], 0
    for n, (k, start, count) in enumerate(plan):
        copies.append(
            pltpu.make_async_copy(
                pieces[k].at[:, pl.ds(start, count)], out.at[:, pl.ds(at, count)], sems.at[n]
            )
        )
        copies[n].start()
        at += count
    for copy in copies:
        copy.wait()


def pack(plan, *pieces):
    rows, wide = sum(count for _, _, count in plan), pieces[0].shape[2]
    return pl.pallas_call(
        functools.partial(pack_kernel, plan),
        out_shape=jax.ShapeDtypeStruct((2, rows, wide), jnp.bfloat16),
        in_specs=[pl.BlockSpec(memory_space=pl.ANY)] * len(pieces),
        out_specs=VMEM,
        scratch_shapes=[pltpu.SemaphoreType.DMA((len(plan),))],
        compiler_params=params(8),
        cost_estimate=FREE,
    )(*pieces)


def rows_kernel(*refs):
    pieces, out = refs[:10], refs[10]
    at = 0
    for k, piece in enumerate(pieces):
        count = piece.shape[1]
        for h in (0, 1):
            out[h ^ (k // 5), at:at + count, :] = piece[h]
        at += count


def rows_from(pieces):
    wide = pieces[0].shape[2]
    return pl.pallas_call(
        rows_kernel,
        out_shape=jax.ShapeDtypeStruct((2, 8 * N, wide), jnp.bfloat16),
        in_specs=[VMEM] * 10,
        out_specs=VMEM,
        compiler_params=params(12),
        cost_estimate=FREE,
    )(*pieces)


def scores_kernel(plan, *refs):
    blocks = sum(len(group) for group in plan)
    rows, parts, outs = refs[0], refs[1:1 + blocks], refs[1 + blocks:1 + 2 * blocks]
    held, made, sems, out_sems = refs[1 + 2 * blocks:]
    copies = []
    for n, group in enumerate(plan):
        at = 0
        copies.append([])
        for k in group:
            count = parts[k].shape[1]
            copies[n].append(pltpu.make_async_copy(parts[k], held.at[n, :, pl.ds(at, count)], sems.at[k]))
            at += count
    for copy in [copy for group in copies for copy in group]:
        copy.start()
    results = []
    for n, group in enumerate(plan):
        for copy in copies[n]:
            copy.wait()
        made[n] = inner(rows[0], held[n, 0]) + inner(rows[1], held[n, 1])
        at = 0
        for k in group:
            count = parts[k].shape[1]
            results.append(pltpu.make_async_copy(made.at[n, :, pl.ds(at, count)], outs[k], out_sems.at[k]))
            results[-1].start()
            at += count
    for copy in results:
        copy.wait()


def scores_of(grant, rows, plan, *blocks):
    wide = rows.shape[2]
    return pl.pallas_call(
        functools.partial(scores_kernel, plan),
        out_shape=[jax.ShapeDtypeStruct((8 * N, a.shape[1]), jnp.float32) for a in blocks],
        in_specs=[VMEM] + [pl.BlockSpec(memory_space=pl.ANY)] * len(blocks),
        out_specs=[pl.BlockSpec(memory_space=pl.ANY)] * len(blocks),
        scratch_shapes=[
            pltpu.VMEM((len(plan), 2, 4 * N, wide), jnp.bfloat16),
            pltpu.VMEM((len(plan), 8 * N, 4 * N), jnp.float32),
            pltpu.SemaphoreType.DMA((len(blocks),)),
            pltpu.SemaphoreType.DMA((len(blocks),)),
        ],
        compiler_params=params(grant),
        cost_estimate=FREE,
    )(rows, *blocks)


def masks(rows, cols, at, count):
    same_u, cross_u, cross_e = (rows[pl.ds(at, count), k:k + 1] for k in range(3))
    same_v, cross_v, cross_p = (cols[k:k + 1, :] for k in range(3))
    hit = cross_e == cross_p
    return same_u != same_v, (cross_u != cross_v) | hit, hit


def scores_at(parts, at, count):
    return jnp.concatenate([part[pl.ds(at, count), :] for part in parts], axis=1) * SCALE


STATS = 16


def stats_kernel(core, amax, *refs):
    parts, (rows, cols, out, keep) = refs[:-4], refs[-4:]
    step = 32
    inc = core[0] == 1
    keep[...] = jnp.zeros_like(keep)

    @pl.loop(0, 4 * N // step)
    def _(k):
        at = pl.multiple_of(k * step, step)
        keep_s, keep_c, hit = masks(rows, cols, at, step)
        keep_c = keep_c & inc
        same = scores_at(parts, at, step)
        cross = scores_at(parts, pl.multiple_of(at + 4 * N, step), step)
        same = jnp.where(keep_s, same, -BIG)
        hits = jnp.sum(jnp.where(hit & inc, cross, 0.0), axis=1, keepdims=True)
        cross = jnp.where(keep_c, cross, -BIG)
        top = jnp.max(jnp.maximum(same, cross), axis=1, keepdims=True)
        total = jnp.sum(
            jnp.where(keep_s, jnp.exp(same - top), 0.0) + jnp.where(keep_c, jnp.exp(cross - top), 0.0),
            axis=1,
            keepdims=True,
        )
        group, low = k // (N // step), pl.multiple_of((k % (N // step)) * step, step)
        for n, value in enumerate((top, total, hits)):
            keep[n * 4 + group, pl.ds(low, step), :] = jnp.broadcast_to(value, (step, 128))

    for n in range(12):
        out[n:n + 1, :] = keep[n].T[0:1, :]
    out[12:16, :] = jnp.full((4, 128), amax[0], jnp.float32)


def stats_of(core, amax, parts, rows, cols):
    return pl.pallas_call(
        stats_kernel,
        out_shape=jax.ShapeDtypeStruct((STATS, 128), jnp.float32),
        in_specs=[SMEM] * 2 + [VMEM] * (len(parts) + 2),
        out_specs=VMEM,
        scratch_shapes=[pltpu.VMEM((12, 128, 128), jnp.float32)],
        compiler_params=params(8),
        cost_estimate=FREE,
    )(core, amax, *parts, rows, cols)


TURNED = ((0, 1, 2, 3), (2, 0, 3, 1), (1, 3, 0, 2), (3, 2, 1, 0))


def merge_kernel(core, *refs):
    (mine, theirs), (out, ends) = (refs[:4], refs[4:8]), refs[8:]
    first = core[0] == 0
    a = [ref[...] for ref in mine]
    b = [ref[...] for ref in theirs]
    line = [jnp.where(first, u, v) for u, v in zip(a, b)] + [jnp.where(first, v, u) for u, v in zip(a, b)]
    loose = jnp.zeros((1, 128), jnp.float32)
    valid = lax.broadcasted_iota(jnp.int32, (1, 128), 1) < N
    for g in range(4):
        of = lambda k: [v[4 * k + t[g]:4 * k + t[g] + 1] for v, t in zip(line, TURNED * 2)]
        tops, sums, hits = of(0), of(1), of(2)
        top = functools.reduce(jnp.maximum, tops)
        total = sum(u * jnp.exp(t - top) for u, t in zip(sums, tops))
        lse = top + jnp.log(total)
        gap = lse - sum(hits)
        out[g:g + 1, :] = lse
        out[4 + g:5 + g, :] = gap
        loose = jnp.maximum(loose, jnp.where(valid, 1.0 - jnp.exp(-gap), 0.0))
        if g == 0:
            ends[0:1, :] = lse
    ends[1:2, :] = loose
    most = functools.reduce(jnp.maximum, [v[12:13] for v in line])
    ends[2:8, :] = jnp.broadcast_to(most, (6, 128))


def merged(core, mine, theirs):
    return pl.pallas_call(
        merge_kernel,
        out_shape=[jax.ShapeDtypeStruct((8, 128), jnp.float32)] * 2,
        in_specs=[SMEM] + [VMEM] * 8,
        out_specs=[VMEM] * 2,
        compiler_params=params(4),
        cost_estimate=FREE,
    )(core, *mine, *theirs)


def lanes_of(rows):
    lane = lax.broadcasted_iota(jnp.int32, (8, 128), 1)
    wide = lambda v: jnp.broadcast_to(v, (8, 128))
    turn = lambda v, by: pltpu.roll(wide(v), by, axis=1) if by % 128 else wide(v)
    out = []
    for b in range(3):
        for a in (0, 2):
            out.append(jnp.where(lane < 64, wide(rows[4 * b + a]), turn(rows[4 * b + a + 1], 64)))
    for h in (0, 1):
        q = [turn(rows[12 + a], (32 * a - 32 * h) % 128) for a in range(4)]
        out.append(jnp.where(lane < 64, jnp.where(lane < 32, q[0], q[1]), jnp.where(lane < 96, q[2], q[3])))
    return jnp.concatenate(out, axis=1)[0:1]


def weights_kernel(first, count, core, *refs):
    parts, (rows, cols, lse_i, *plane, out, bound, col) = refs[:len(PARTS)], refs[len(PARTS):]
    step = 32
    w = core[0]
    for g in range(4):
        line = jnp.broadcast_to(lse_i[g:g + 1, :], (128, 128)).T[:N]
        col[0, g * N:(g + 1) * N, :] = line
        col[1, g * N:(g + 1) * N, :] = jnp.where(w == 1, line, 0.0)
    ends = [ref[8 * a:8 * a + 8, :] for ref in plane for a in range(4)]
    lj = lanes_of([v[0:1] for v in ends])
    cross_j = jnp.where(w == 1, 0.0, lj)
    loose = jnp.max(functools.reduce(jnp.maximum, [v[1:2] for v in ends]), axis=1, keepdims=True)
    most = jnp.max(functools.reduce(jnp.maximum, [v[2:3] for v in ends]), axis=1, keepdims=True)
    bound[...] = jnp.broadcast_to(jnp.maximum(loose, 1e-3) * jnp.maximum(most, 1e-20), (8, 128))

    @pl.loop(0, count * N // step)
    def _(k):
        at = pl.multiple_of(first * N + k * step, step)
        keep_s, keep_c, hit = masks(rows, cols, at, step)
        li = col[0, pl.ds(at, step), 0:1]
        lc = col[1, pl.ds(at, step), 0:1]
        same = scores_at(parts, at, step)
        cross = scores_at(parts, pl.multiple_of(at + 4 * N, step), step)
        m_s = jnp.where(keep_s, jnp.exp(same - li) + jnp.exp(same - lj), 0.0)
        m_c = jnp.where(keep_c, jnp.exp((cross - lc) - cross_j), 0.0) - jnp.where(hit, 1.0, 0.0)
        group = k // (N // step)
        base = group * 2 * N + (k % (N // step)) * step
        out[pl.ds(pl.multiple_of(base + w * N, step), step), :] = m_s.astype(jnp.bfloat16)
        out[pl.ds(pl.multiple_of(base + (1 - w) * N, step), step), :] = m_c.astype(jnp.bfloat16)


def weights_of(first, count, core, parts, rows, cols, lse_i, plane):
    return pl.pallas_call(
        functools.partial(weights_kernel, first, count),
        out_shape=[
            jax.ShapeDtypeStruct((count * 2 * N, J), jnp.bfloat16),
            jax.ShapeDtypeStruct((8, 128), jnp.float32),
        ],
        in_specs=[SMEM] + [VMEM] * (len(parts) + 7),
        out_specs=[VMEM] * 2,
        scratch_shapes=[pltpu.VMEM((2, 4 * N, 128), jnp.float32)],
        compiler_params=params(8),
        cost_estimate=FREE,
    )(core, *parts, rows, cols, lse_i, *plane)


def product_kernel(scaled, bound, mine, theirs, *refs):
    count = mine.shape[0] // (2 * N)
    blocks, outs, (held, sems) = refs[:2 * len(PARTS)], refs[2 * len(PARTS):-2], refs[-2:]
    copies = ([], [])
    for k in (0, 1):
        at = 0
        for n, size in enumerate(PARTS):
            i = k * len(PARTS) + n
            copies[k].append(pltpu.make_async_copy(blocks[i].at[k], held.at[k, pl.ds(at, size)], sems.at[i]))
            copies[k][-1].start()
            at += size
    shrink = 1.0 / bound[0:1, 0:1]
    step = 512
    for k, weights in enumerate((mine, theirs)):
        for copy in copies[k]:
            copy.wait()

        @pl.loop(0, held.shape[2] // step)
        def _(j):
            here = pl.ds(pl.multiple_of(j * step, step), step)
            term = plain(weights[...], held[k, :, here])
            for g in range(count):
                part = term[2 * N * g:2 * N * (g + 1)]
                if k == 0:
                    outs[g][:, here] = part
                else:
                    part = outs[g][:, here] + part
                    outs[g][:, here] = part * shrink if g >= scaled else part


def product_of(scaled, bound, mine, theirs, blocks, others):
    rows, wide = mine.shape[0], blocks[0].shape[2]
    outs = rows // (2 * N)
    return pl.pallas_call(
        functools.partial(product_kernel, scaled),
        out_shape=[jax.ShapeDtypeStruct((2 * N, wide), jnp.float32)] * outs,
        in_specs=[VMEM] * 3 + [pl.BlockSpec(memory_space=pl.ANY)] * (2 * len(PARTS)),
        out_specs=[VMEM] * outs,
        scratch_shapes=[pltpu.VMEM((2, J, wide), jnp.bfloat16), pltpu.SemaphoreType.DMA((2 * len(PARTS),))],
        compiler_params=params(20),
        cost_estimate=FREE,
    )(bound, mine, theirs, *blocks, *others)


def after(value, *others):
    return lax.optimization_barrier((value, *others))[0]


def settle(*values):
    return lax.optimization_barrier(values)


def body(queries, passages, passage_ids, pos_index):
    y, z, x, w = (lax.axis_index(name) for name in GRID)
    first = w == 0
    core = w.astype(jnp.int32).reshape(1)
    pick = lambda a, b: jnp.where(first, a, b)
    rows_of = functools.partial(lax.slice_in_dim, axis=1)
    low = lambda a: [rows_of(a, k * N, k * N + H) for k in range(a.shape[1] // N)]
    high = lambda a: [rows_of(a, k * N + H, (k + 1) * N) for k in range(a.shape[1] // N)]
    join = lambda parts: jnp.concatenate(parts, axis=1)
    line = lambda v, k: (up, far, down)[k - 1](v)
    by_first = lambda v, k: along(v, FIRST[k])
    by_second = lambda v, k: along(v, SECOND[k])
    ring = lambda v, send: [v] + [send(v, k) for k in RING[1:]]

    got = swap(pick(passages, queries))
    own = jnp.stack([pick(queries, passages), got])
    ints = jnp.stack([passage_ids, pos_index])

    fl, fr, own, *ints = settle(along(own, FIRST[1]), along(own, FIRST[3]), own, *ring(ints, line))
    f_low, f_high, own, fl, fr, *ints = settle(
        along(low(fl)[0], FIRST[1]), along(high(fr)[0], FIRST[3]), own, fl, fr, *ring(jnp.stack(ints), by_first)
    )
    group = pack(((0, 0, N), (1, 0, N), (2, 0, N), (3, 0, H), (4, 0, H)), own, fl, fr, f_low, f_high)
    group, own, *ints = settle(group, own, *ring(jnp.stack(ints), by_second))
    ints = jnp.stack(ints)
    ids = ints[..., 0, :]
    dev, off = ints[..., 1, :] // N, ints[..., 1, :] % N
    near = lambda at, other: (lambda d: d ^ (d >> 1))((at - other) % 4)
    dy, dz, dx = near(y, dev // 16), near(z, dev // 4 % 4), near(x, dev % 4)
    pos = ((pick(dz, dy) * 4 + pick(dy, dz)) * 4 + dx) * N + off
    pair = jnp.arange(64 * N, dtype=jnp.int32).reshape(4, 4, 4, N)
    i_of = lambda t: t[0, 0].reshape(-1)
    j_of = lambda t: jnp.concatenate(
        [t[:3, :, 0].reshape(-1), t[3, :, 0].reshape(4, 2, H).transpose(1, 0, 2).reshape(-1)]
    )
    i_pair, i_id, i_pos = i_of(pair), i_of(ids), i_of(pos)
    j_pair, j_id, j_pos = j_of(pair), j_of(ids), j_of(pos)
    table, every = ids.reshape(1, -1), pair.reshape(1, -1)
    look = lambda at: jnp.sum(jnp.where(at[:, None] == every, table, 0), axis=1)
    i_tgt, j_tgt = look(i_pos), look(j_pos)
    rows = jnp.stack([pick(i_pair, i_id), pick(i_id, i_tgt), pick(i_pair, i_pos)] + [i_pair] * 5, axis=1)
    cols = jnp.stack([pick(j_pair, j_id), pick(j_tgt, j_id), pick(j_pos, j_pair)] + [j_pair] * 5)
    amax = jnp.maximum(
        jnp.max(jnp.abs(queries.astype(jnp.float32))), jnp.max(jnp.abs(passages.astype(jnp.float32)))
    )
    xl, xr = up(own), down(own)
    mine = [own, xl, xr, up(low(xl)[0]), down(high(xr)[0])]
    dl, dr, group, rows, cols, amax, *held = settle(
        along(group, SECOND[1]), along(group, SECOND[3]), group, rows, cols, amax, *mine, *[swap(a) for a in mine]
    )
    to_l = pack(tuple((0, k * N, H) for k in range(4)), dl)
    to_r = pack(tuple((0, k * N + H, H) for k in range(4)), dr)
    rows_i = rows_from([after(held[0], to_l, to_r)] + held[1:])
    blocks = [group, dl, dr]
    parts = scores_of(14, rows_i, ((0,), (1,), (2,)), *blocks)
    others = [swap(after(a, rows_i)) for a in blocks]
    gl, gr, *held = settle(along(to_l, SECOND[1]), along(to_r, SECOND[3]), *parts, *blocks)
    parts, blocks = held[:3], held[3:]
    blocks += [gl, gr]

    parts += scores_of(9, rows_i, ((0, 1),), gl, gr)
    found, *held = settle(stats_of(core, amax.reshape(1), parts, rows, cols), *others, swap(gl), swap(gr), *blocks)
    others, blocks = held[:5], held[5:]
    found = ring(found, line)
    lse_i, ends = merged(core, found, [swap(a) for a in found])
    loss = lse_i[4, :N]
    plane = ring(jnp.concatenate(ring(ends, by_first)), by_second)

    f16, f32 = jnp.float16, jnp.float32
    args = (parts, rows, cols, lse_i, plane)
    m_far, bound = weights_of(3, 1, core, *args)
    m_far_o = swap(m_far)
    m_rest, _ = weights_of(0, 3, after(core, m_far), *args)
    (opposite,) = product_of(0, bound, m_far, m_far_o, blocks, others)
    opposite = opposite.astype(f16)
    got_q, got_p, here, to_down, to_up = settle(
        up(opposite[:N]), down(opposite[N:]), *product_of(1, bound, m_rest, swap(m_rest), blocks, others)
    )
    below = up(jnp.concatenate([to_up[:N] + got_q.astype(f32), to_up[N:]]).astype(f16))
    above = down(jnp.concatenate([to_down[:N], to_down[N:] + got_p.astype(f32)]).astype(f16))
    grad = here + (below.astype(f32) + above.astype(f32)) * bound[0, 0]
    grad_q, grad_p = grad[:N], grad[N:]
    return loss, grad_q, grad_p


def solution(mesh):
    grid = Mesh(mesh.devices.reshape(4, 4, 4, 2), GRID)
    pair = ("y", "z", "x")
    placed = (P(pair, "w"), P(pair, "w"), P(pair), P(pair))
    return jax.shard_map(
        body,
        mesh=grid,
        in_specs=placed,
        out_specs=(P(pair), P(pair, "w"), P(pair, "w")),
        check_vma=False,
    )
```

```python
import functools
import math

import jax
import jax.numpy as jnp
from jax import lax
from jax.experimental import pallas as pl
from jax.experimental.pallas import tpu as pltpu
from jax.sharding import Mesh, PartitionSpec as P

D = 4096
N = 64
H = N // 2
SCALE = 3.0 / math.sqrt(D)
BIG = 1e30
GRID = ("y", "z", "x", "w")
UP = [(i, (i + 1) % 4) for i in range(4)]
DOWN = [(i, (i - 1) % 4) for i in range(4)]
FAR = [(i, (i + 2) % 4) for i in range(4)]
RING = (0, 1, 3, 2)
PARTS = (256, 256, 256, 128, 128)
J = sum(PARTS)


def steps(first, second, by):
    moves = []
    for y in range(4):
        for z in range(4):
            for x in range(4):
                for w in range(2):
                    axis = second if w else first
                    to_y, to_z = ((y + by) % 4, z) if axis == "y" else (y, (z + by) % 4)
                    flat = lambda y, z: ((y * 4 + z) * 4 + x) * 2 + w
                    moves.append((flat(y, z), flat(to_y, to_z)))
    return moves


FIRST = {by: steps("y", "z", by) for by in (1, 2, 3)}
SECOND = {by: steps("z", "y", by) for by in (1, 2, 3)}


def along(value, moves):
    return lax.ppermute(value, GRID, moves)


def swap(value):
    return lax.ppermute(value, "w", [(0, 1), (1, 0)])


def up(value):
    return lax.ppermute(value, "x", UP)


def down(value):
    return lax.ppermute(value, "x", DOWN)


def far(value):
    return lax.ppermute(value, "x", FAR)


def inner(left, right):
    return lax.dot_general(
        left, right, (((1,), (1,)), ((), ())), preferred_element_type=jnp.float32
    )


def plain(left, right):
    return jnp.dot(left, right, preferred_element_type=jnp.float32)


VMEM = pl.BlockSpec(memory_space=pltpu.VMEM)
SMEM = pl.BlockSpec(memory_space=pltpu.SMEM)
def params(mib):
    return pltpu.CompilerParams(vmem_limit_bytes=mib << 20)


FREE = pl.CostEstimate(flops=0, bytes_accessed=0, transcendentals=0)


def pack_kernel(plan, *refs):
    pieces, out, sems = refs[:-2], refs[-2], refs[-1]
    copies, at = [], 0
    for n, (k, start, count) in enumerate(plan):
        copies.append(
            pltpu.make_async_copy(
                pieces[k].at[:, pl.ds(start, count)], out.at[:, pl.ds(at, count)], sems.at[n]
            )
        )
        copies[n].start()
        at += count
    for copy in copies:
        copy.wait()


def pack(plan, *pieces):
    rows, wide = sum(count for _, _, count in plan), pieces[0].shape[2]
    return pl.pallas_call(
        functools.partial(pack_kernel, plan),
        out_shape=jax.ShapeDtypeStruct((2, rows, wide), jnp.bfloat16),
        in_specs=[pl.BlockSpec(memory_space=pl.ANY)] * len(pieces),
        out_specs=VMEM,
        scratch_shapes=[pltpu.SemaphoreType.DMA((len(plan),))],
        compiler_params=params(8),
        cost_estimate=FREE,
    )(*pieces)


def place_kernel(plan, *refs):
    pieces, out = refs[:-1], refs[-1]
    at = 0
    for k, start, count in plan:
        out[:, at:at + count, :] = pieces[k][:, start:start + count, :]
        at += count


def place(plan, *pieces):
    rows, wide = sum(count for _, _, count in plan), pieces[0].shape[2]
    return pl.pallas_call(
        functools.partial(place_kernel, plan),
        out_shape=jax.ShapeDtypeStruct((2, rows, wide), jnp.bfloat16),
        in_specs=[VMEM] * len(pieces),
        out_specs=VMEM,
        compiler_params=params(8),
        cost_estimate=FREE,
    )(*pieces)


def rows_kernel(*refs):
    pieces, out = refs[:10], refs[10]
    at = 0
    for k, piece in enumerate(pieces):
        count = piece.shape[1]
        for h in (0, 1):
            out[h ^ (k // 5), at:at + count, :] = piece[h]
        at += count


def rows_from(pieces):
    wide = pieces[0].shape[2]
    return pl.pallas_call(
        rows_kernel,
        out_shape=jax.ShapeDtypeStruct((2, 8 * N, wide), jnp.bfloat16),
        in_specs=[VMEM] * 10,
        out_specs=VMEM,
        compiler_params=params(12),
        cost_estimate=FREE,
    )(*pieces)


def scores_kernel(plan, *refs):
    blocks = sum(len(group) for group in plan)
    rows, parts, outs = refs[0], refs[1:1 + blocks], refs[1 + blocks:1 + 2 * blocks]
    held, made, sems, out_sems = refs[1 + 2 * blocks:]
    copies = []
    for n, group in enumerate(plan):
        at = 0
        copies.append([])
        for k in group:
            count = parts[k].shape[1]
            copies[n].append(pltpu.make_async_copy(parts[k], held.at[n, :, pl.ds(at, count)], sems.at[k]))
            at += count
    for copy in [copy for group in copies for copy in group]:
        copy.start()
    results = []
    for n, group in enumerate(plan):
        for copy in copies[n]:
            copy.wait()
        made[n] = inner(rows[0], held[n, 0]) + inner(rows[1], held[n, 1])
        at = 0
        for k in group:
            count = parts[k].shape[1]
            results.append(pltpu.make_async_copy(made.at[n, :, pl.ds(at, count)], outs[k], out_sems.at[k]))
            results[-1].start()
            at += count
    for copy in results:
        copy.wait()


def scores_of(grant, rows, plan, *blocks):
    wide = rows.shape[2]
    return pl.pallas_call(
        functools.partial(scores_kernel, plan),
        out_shape=[jax.ShapeDtypeStruct((8 * N, a.shape[1]), jnp.float32) for a in blocks],
        in_specs=[VMEM] + [pl.BlockSpec(memory_space=pl.ANY)] * len(blocks),
        out_specs=[pl.BlockSpec(memory_space=pl.ANY)] * len(blocks),
        scratch_shapes=[
            pltpu.VMEM((len(plan), 2, 4 * N, wide), jnp.bfloat16),
            pltpu.VMEM((len(plan), 8 * N, 4 * N), jnp.float32),
            pltpu.SemaphoreType.DMA((len(blocks),)),
            pltpu.SemaphoreType.DMA((len(blocks),)),
        ],
        compiler_params=params(grant),
        cost_estimate=FREE,
    )(rows, *blocks)


def masks(rows, cols, at, count):
    same_u, cross_u, cross_e = (rows[pl.ds(at, count), k:k + 1] for k in range(3))
    same_v, cross_v, cross_p = (cols[k:k + 1, :] for k in range(3))
    hit = cross_e == cross_p
    return same_u != same_v, (cross_u != cross_v) | hit, hit


def scores_at(parts, at, count):
    return jnp.concatenate([part[pl.ds(at, count), :] for part in parts], axis=1) * SCALE


STATS = 16


def stats_kernel(core, amax, *refs):
    parts, (rows, cols, out, keep) = refs[:-4], refs[-4:]
    step = 32
    inc = core[0] == 1
    keep[...] = jnp.zeros_like(keep)

    @pl.loop(0, 4 * N // step)
    def _(k):
        at = pl.multiple_of(k * step, step)
        keep_s, keep_c, hit = masks(rows, cols, at, step)
        keep_c = keep_c & inc
        same = scores_at(parts, at, step)
        cross = scores_at(parts, pl.multiple_of(at + 4 * N, step), step)
        same = jnp.where(keep_s, same, -BIG)
        hits = jnp.sum(jnp.where(hit & inc, cross, 0.0), axis=1, keepdims=True)
        cross = jnp.where(keep_c, cross, -BIG)
        top = jnp.max(jnp.maximum(same, cross), axis=1, keepdims=True)
        total = jnp.sum(
            jnp.where(keep_s, jnp.exp(same - top), 0.0) + jnp.where(keep_c, jnp.exp(cross - top), 0.0),
            axis=1,
            keepdims=True,
        )
        group, low = k // (N // step), pl.multiple_of((k % (N // step)) * step, step)
        for n, value in enumerate((top, total, hits)):
            keep[n * 4 + group, pl.ds(low, step), :] = jnp.broadcast_to(value, (step, 128))

    for n in range(12):
        out[n:n + 1, :] = keep[n].T[0:1, :]
    out[12:16, :] = jnp.full((4, 128), amax[0], jnp.float32)


def stats_of(core, amax, parts, rows, cols):
    return pl.pallas_call(
        stats_kernel,
        out_shape=jax.ShapeDtypeStruct((STATS, 128), jnp.float32),
        in_specs=[SMEM] * 2 + [VMEM] * (len(parts) + 2),
        out_specs=VMEM,
        scratch_shapes=[pltpu.VMEM((12, 128, 128), jnp.float32)],
        compiler_params=params(8),
        cost_estimate=FREE,
    )(core, amax, *parts, rows, cols)


TURNED = ((0, 1, 2, 3), (2, 0, 3, 1), (1, 3, 0, 2), (3, 2, 1, 0))


def merge_kernel(core, *refs):
    (mine, theirs), (out, ends) = (refs[:4], refs[4:8]), refs[8:]
    first = core[0] == 0
    a = [ref[...] for ref in mine]
    b = [ref[...] for ref in theirs]
    line = [jnp.where(first, u, v) for u, v in zip(a, b)] + [jnp.where(first, v, u) for u, v in zip(a, b)]
    loose = jnp.zeros((1, 128), jnp.float32)
    valid = lax.broadcasted_iota(jnp.int32, (1, 128), 1) < N
    for g in range(4):
        of = lambda k: [v[4 * k + t[g]:4 * k + t[g] + 1] for v, t in zip(line, TURNED * 2)]
        tops, sums, hits = of(0), of(1), of(2)
        top = functools.reduce(jnp.maximum, tops)
        total = sum(u * jnp.exp(t - top) for u, t in zip(sums, tops))
        lse = top + jnp.log(total)
        gap = lse - sum(hits)
        out[g:g + 1, :] = lse
        out[4 + g:5 + g, :] = gap
        loose = jnp.maximum(loose, jnp.where(valid, 1.0 - jnp.exp(-gap), 0.0))
        if g == 0:
            ends[0:1, :] = lse
    ends[1:2, :] = loose
    most = functools.reduce(jnp.maximum, [v[12:13] for v in line])
    ends[2:8, :] = jnp.broadcast_to(most, (6, 128))


def merged(core, mine, theirs):
    return pl.pallas_call(
        merge_kernel,
        out_shape=[jax.ShapeDtypeStruct((8, 128), jnp.float32)] * 2,
        in_specs=[SMEM] + [VMEM] * 8,
        out_specs=[VMEM] * 2,
        compiler_params=params(4),
        cost_estimate=FREE,
    )(core, *mine, *theirs)


def lanes_of(rows):
    lane = lax.broadcasted_iota(jnp.int32, (8, 128), 1)
    wide = lambda v: jnp.broadcast_to(v, (8, 128))
    turn = lambda v, by: pltpu.roll(wide(v), by, axis=1) if by % 128 else wide(v)
    out = []
    for b in range(3):
        for a in (0, 2):
            out.append(jnp.where(lane < 64, wide(rows[4 * b + a]), turn(rows[4 * b + a + 1], 64)))
    for h in (0, 1):
        q = [turn(rows[12 + a], (32 * a - 32 * h) % 128) for a in range(4)]
        out.append(jnp.where(lane < 64, jnp.where(lane < 32, q[0], q[1]), jnp.where(lane < 96, q[2], q[3])))
    return jnp.concatenate(out, axis=1)[0:1]


def weights_kernel(first, count, core, *refs):
    parts, (rows, cols, lse_i, *plane, out, bound, col) = refs[:len(PARTS)], refs[len(PARTS):]
    step = 32
    w = core[0]
    for g in range(4):
        line = jnp.broadcast_to(lse_i[g:g + 1, :], (128, 128)).T[:N]
        col[0, g * N:(g + 1) * N, :] = line
        col[1, g * N:(g + 1) * N, :] = jnp.where(w == 1, line, 0.0)
    ends = [ref[8 * a:8 * a + 8, :] for ref in plane for a in range(4)]
    lj = lanes_of([v[0:1] for v in ends])
    cross_j = jnp.where(w == 1, 0.0, lj)
    loose = jnp.max(functools.reduce(jnp.maximum, [v[1:2] for v in ends]), axis=1, keepdims=True)
    most = jnp.max(functools.reduce(jnp.maximum, [v[2:3] for v in ends]), axis=1, keepdims=True)
    bound[...] = jnp.broadcast_to(jnp.maximum(loose, 1e-3) * jnp.maximum(most, 1e-20), (8, 128))

    @pl.loop(0, count * N // step)
    def _(k):
        at = pl.multiple_of(first * N + k * step, step)
        keep_s, keep_c, hit = masks(rows, cols, at, step)
        li = col[0, pl.ds(at, step), 0:1]
        lc = col[1, pl.ds(at, step), 0:1]
        same = scores_at(parts, at, step)
        cross = scores_at(parts, pl.multiple_of(at + 4 * N, step), step)
        m_s = jnp.where(keep_s, jnp.exp(same - li) + jnp.exp(same - lj), 0.0)
        m_c = jnp.where(keep_c, jnp.exp((cross - lc) - cross_j), 0.0) - jnp.where(hit, 1.0, 0.0)
        group = k // (N // step)
        base = group * 2 * N + (k % (N // step)) * step
        out[pl.ds(pl.multiple_of(base + w * N, step), step), :] = m_s.astype(jnp.bfloat16)
        out[pl.ds(pl.multiple_of(base + (1 - w) * N, step), step), :] = m_c.astype(jnp.bfloat16)


def weights_of(first, count, core, parts, rows, cols, lse_i, plane):
    return pl.pallas_call(
        functools.partial(weights_kernel, first, count),
        out_shape=[
            jax.ShapeDtypeStruct((count * 2 * N, J), jnp.bfloat16),
            jax.ShapeDtypeStruct((8, 128), jnp.float32),
        ],
        in_specs=[SMEM] + [VMEM] * (len(parts) + 7),
        out_specs=[VMEM] * 2,
        scratch_shapes=[pltpu.VMEM((2, 4 * N, 128), jnp.float32)],
        compiler_params=params(8),
        cost_estimate=FREE,
    )(core, *parts, rows, cols, lse_i, *plane)


def product_kernel(scaled, bound, mine, theirs, *refs):
    count = mine.shape[0] // (2 * N)
    blocks, outs, (held, sems) = refs[:2 * len(PARTS)], refs[2 * len(PARTS):-2], refs[-2:]
    copies = ([], [])
    for k in (0, 1):
        at = 0
        for n, size in enumerate(PARTS):
            i = k * len(PARTS) + n
            copies[k].append(pltpu.make_async_copy(blocks[i].at[k], held.at[k, pl.ds(at, size)], sems.at[i]))
            copies[k][-1].start()
            at += size
    shrink = 1.0 / bound[0:1, 0:1]
    step = 512
    for k, weights in enumerate((mine, theirs)):
        for copy in copies[k]:
            copy.wait()

        @pl.loop(0, held.shape[2] // step)
        def _(j):
            here = pl.ds(pl.multiple_of(j * step, step), step)
            term = plain(weights[...], held[k, :, here])
            for g in range(count):
                part = term[2 * N * g:2 * N * (g + 1)]
                if k == 0:
                    outs[g][:, here] = part
                else:
                    part = outs[g][:, here] + part
                    outs[g][:, here] = part * shrink if g >= scaled else part


def product_of(scaled, bound, mine, theirs, blocks, others):
    rows, wide = mine.shape[0], blocks[0].shape[2]
    outs = rows // (2 * N)
    return pl.pallas_call(
        functools.partial(product_kernel, scaled),
        out_shape=[jax.ShapeDtypeStruct((2 * N, wide), jnp.float32)] * outs,
        in_specs=[VMEM] * 3 + [pl.BlockSpec(memory_space=pl.ANY)] * (2 * len(PARTS)),
        out_specs=[VMEM] * outs,
        scratch_shapes=[pltpu.VMEM((2, J, wide), jnp.bfloat16), pltpu.SemaphoreType.DMA((2 * len(PARTS),))],
        compiler_params=params(20),
        cost_estimate=FREE,
    )(bound, mine, theirs, *blocks, *others)


def after(value, *others):
    return lax.optimization_barrier((value, *others))[0]


def settle(*values):
    return lax.optimization_barrier(values)


def body(queries, passages, passage_ids, pos_index):
    y, z, x, w = (lax.axis_index(name) for name in GRID)
    first = w == 0
    core = w.astype(jnp.int32).reshape(1)
    pick = lambda a, b: jnp.where(first, a, b)
    rows_of = functools.partial(lax.slice_in_dim, axis=1)
    low = lambda a: [rows_of(a, k * N, k * N + H) for k in range(a.shape[1] // N)]
    high = lambda a: [rows_of(a, k * N + H, (k + 1) * N) for k in range(a.shape[1] // N)]
    join = lambda parts: jnp.concatenate(parts, axis=1)
    line = lambda v, k: (up, far, down)[k - 1](v)
    by_first = lambda v, k: along(v, FIRST[k])
    by_second = lambda v, k: along(v, SECOND[k])
    ring = lambda v, send: [v] + [send(v, k) for k in RING[1:]]

    got = swap(pick(passages, queries))
    own = jnp.stack([pick(queries, passages), got])
    ints = jnp.stack([passage_ids, pos_index])

    fl, fr, own, *ints = settle(along(own, FIRST[1]), along(own, FIRST[3]), own, *ring(ints, line))
    f_low, f_high, own, fl, fr, *ints = settle(
        along(low(fl)[0], FIRST[1]), along(high(fr)[0], FIRST[3]), own, fl, fr, *ring(jnp.stack(ints), by_first)
    )
    group = place(((0, 0, N), (1, 0, N), (2, 0, N), (3, 0, H), (4, 0, H)), own, fl, fr, f_low, f_high)
    group, own, *ints = settle(group, own, *ring(jnp.stack(ints), by_second))
    ints = jnp.stack(ints)
    ids = ints[..., 0, :]
    dev, off = ints[..., 1, :] // N, ints[..., 1, :] % N
    near = lambda at, other: (lambda d: d ^ (d >> 1))((at - other) % 4)
    dy, dz, dx = near(y, dev // 16), near(z, dev // 4 % 4), near(x, dev % 4)
    pos = ((pick(dz, dy) * 4 + pick(dy, dz)) * 4 + dx) * N + off
    pair = jnp.arange(64 * N, dtype=jnp.int32).reshape(4, 4, 4, N)
    i_of = lambda t: t[0, 0].reshape(-1)
    j_of = lambda t: jnp.concatenate(
        [t[:3, :, 0].reshape(-1), t[3, :, 0].reshape(4, 2, H).transpose(1, 0, 2).reshape(-1)]
    )
    i_pair, i_id, i_pos = i_of(pair), i_of(ids), i_of(pos)
    j_pair, j_id, j_pos = j_of(pair), j_of(ids), j_of(pos)
    table, every = ids.reshape(1, -1), pair.reshape(1, -1)
    look = lambda at: jnp.sum(jnp.where(at[:, None] == every, table, 0), axis=1)
    i_tgt, j_tgt = look(i_pos), look(j_pos)
    rows = jnp.stack([pick(i_pair, i_id), pick(i_id, i_tgt), pick(i_pair, i_pos)] + [i_pair] * 5, axis=1)
    cols = jnp.stack([pick(j_pair, j_id), pick(j_tgt, j_id), pick(j_pos, j_pair)] + [j_pair] * 5)
    amax = jnp.maximum(
        jnp.max(jnp.abs(queries.astype(jnp.float32))), jnp.max(jnp.abs(passages.astype(jnp.float32)))
    )
    xl, xr = up(own), down(own)
    mine = [own, xl, xr, up(low(xl)[0]), down(high(xr)[0])]
    dl, dr, group, rows, cols, amax, *held = settle(
        along(group, SECOND[1]), along(group, SECOND[3]), group, rows, cols, amax, *mine, *[swap(a) for a in mine]
    )
    to_l = pack(tuple((0, k * N, H) for k in range(4)), dl)
    to_r = pack(tuple((0, k * N + H, H) for k in range(4)), dr)
    rows_i = rows_from([after(held[0], to_l, to_r)] + held[1:])
    blocks = [group, dl, dr]
    parts = scores_of(14, rows_i, ((0,), (1,), (2,)), *blocks)
    others = [swap(after(a, rows_i)) for a in blocks]
    gl, gr, *held = settle(along(to_l, SECOND[1]), along(to_r, SECOND[3]), *parts, *blocks)
    parts, blocks = held[:3], held[3:]
    blocks += [gl, gr]

    parts += scores_of(9, rows_i, ((0, 1),), gl, gr)
    found, *held = settle(stats_of(core, amax.reshape(1), parts, rows, cols), *others, swap(gl), swap(gr), *blocks)
    others, blocks = held[:5], held[5:]
    found = ring(found, line)
    lse_i, ends = merged(core, found, [swap(a) for a in found])
    loss = lse_i[4, :N]
    plane = ring(jnp.concatenate(ring(ends, by_first)), by_second)

    f16, f32 = jnp.float16, jnp.float32
    args = (parts, rows, cols, lse_i, plane)
    m_far, bound = weights_of(3, 1, core, *args)
    m_far_o = swap(m_far)
    m_rest, _ = weights_of(0, 3, after(core, m_far), *args)
    (opposite,) = product_of(0, bound, m_far, m_far_o, blocks, others)
    opposite = opposite.astype(f16)
    got_q, got_p, here, to_down, to_up = settle(
        up(opposite[:N]), down(opposite[N:]), *product_of(1, bound, m_rest, swap(m_rest), blocks, others)
    )
    below = up(jnp.concatenate([to_up[:N] + got_q.astype(f32), to_up[N:]]).astype(f16))
    above = down(jnp.concatenate([to_down[:N], to_down[N:] + got_p.astype(f32)]).astype(f16))
    grad = here + (below.astype(f32) + above.astype(f32)) * bound[0, 0]
    grad_q, grad_p = grad[:N], grad[N:]
    return loss, grad_q, grad_p


def solution(mesh):
    grid = Mesh(mesh.devices.reshape(4, 4, 4, 2), GRID)
    pair = ("y", "z", "x")
    placed = (P(pair, "w"), P(pair, "w"), P(pair), P(pair))
    return jax.shard_map(
        body,
        mesh=grid,
        in_specs=placed,
        out_specs=(P(pair), P(pair, "w"), P(pair, "w")),
        check_vma=False,
    )
```

```python
import functools
import math

import jax
import jax.numpy as jnp
from jax import lax
from jax.experimental import pallas as pl
from jax.experimental.pallas import tpu as pltpu
from jax.sharding import Mesh, PartitionSpec as P

D = 4096
N = 64
H = N // 2
SCALE = 3.0 / math.sqrt(D)
BIG = 1e30
GRID = ("y", "z", "x", "w")
UP = [(i, (i + 1) % 4) for i in range(4)]
DOWN = [(i, (i - 1) % 4) for i in range(4)]
FAR = [(i, (i + 2) % 4) for i in range(4)]
RING = (0, 1, 3, 2)
PARTS = (256, 256, 256, 128, 128)
J = sum(PARTS)


def steps(first, second, by):
    moves = []
    for y in range(4):
        for z in range(4):
            for x in range(4):
                for w in range(2):
                    axis = second if w else first
                    to_y, to_z = ((y + by) % 4, z) if axis == "y" else (y, (z + by) % 4)
                    flat = lambda y, z: ((y * 4 + z) * 4 + x) * 2 + w
                    moves.append((flat(y, z), flat(to_y, to_z)))
    return moves


FIRST = {by: steps("y", "z", by) for by in (1, 2, 3)}
SECOND = {by: steps("z", "y", by) for by in (1, 2, 3)}


def along(value, moves):
    return lax.ppermute(value, GRID, moves)


def swap(value):
    return lax.ppermute(value, "w", [(0, 1), (1, 0)])


def up(value):
    return lax.ppermute(value, "x", UP)


def down(value):
    return lax.ppermute(value, "x", DOWN)


def far(value):
    return lax.ppermute(value, "x", FAR)


def inner(left, right):
    return lax.dot_general(
        left, right, (((1,), (1,)), ((), ())), preferred_element_type=jnp.float32
    )


def plain(left, right):
    return jnp.dot(left, right, preferred_element_type=jnp.float32)


VMEM = pl.BlockSpec(memory_space=pltpu.VMEM)
SMEM = pl.BlockSpec(memory_space=pltpu.SMEM)
def params(mib):
    return pltpu.CompilerParams(vmem_limit_bytes=mib << 20)


FREE = pl.CostEstimate(flops=0, bytes_accessed=0, transcendentals=0)


def pack_kernel(plan, *refs):
    pieces, out, sems = refs[:-2], refs[-2], refs[-1]
    copies, at = [], 0
    for n, (k, start, count) in enumerate(plan):
        copies.append(
            pltpu.make_async_copy(
                pieces[k].at[:, pl.ds(start, count)], out.at[:, pl.ds(at, count)], sems.at[n]
            )
        )
        copies[n].start()
        at += count
    for copy in copies:
        copy.wait()


def pack(plan, *pieces):
    rows, wide = sum(count for _, _, count in plan), pieces[0].shape[2]
    return pl.pallas_call(
        functools.partial(pack_kernel, plan),
        out_shape=jax.ShapeDtypeStruct((2, rows, wide), jnp.bfloat16),
        in_specs=[pl.BlockSpec(memory_space=pl.ANY)] * len(pieces),
        out_specs=VMEM,
        scratch_shapes=[pltpu.SemaphoreType.DMA((len(plan),))],
        compiler_params=params(8),
        cost_estimate=FREE,
    )(*pieces)


def place_kernel(plan, *refs):
    pieces, out = refs[:-1], refs[-1]
    at = 0
    for k, start, count in plan:
        out[:, at:at + count, :] = pieces[k][:, start:start + count, :]
        at += count


def place(plan, *pieces):
    rows, wide = sum(count for _, _, count in plan), pieces[0].shape[2]
    return pl.pallas_call(
        functools.partial(place_kernel, plan),
        out_shape=jax.ShapeDtypeStruct((2, rows, wide), jnp.bfloat16),
        in_specs=[VMEM] * len(pieces),
        out_specs=VMEM,
        compiler_params=params(8),
        cost_estimate=FREE,
    )(*pieces)


def rows_kernel(*refs):
    pieces, out = refs[:10], refs[10]
    at = 0
    for k, piece in enumerate(pieces):
        count = piece.shape[1]
        for h in (0, 1):
            out[h ^ (k // 5), at:at + count, :] = piece[h]
        at += count


def rows_from(pieces):
    wide = pieces[0].shape[2]
    return pl.pallas_call(
        rows_kernel,
        out_shape=jax.ShapeDtypeStruct((2, 8 * N, wide), jnp.bfloat16),
        in_specs=[VMEM] * 10,
        out_specs=VMEM,
        compiler_params=params(12),
        cost_estimate=FREE,
    )(*pieces)


def scores_kernel(plan, *refs):
    blocks = sum(len(group) for group in plan)
    rows, parts, outs = refs[0], refs[1:1 + blocks], refs[1 + blocks:1 + 2 * blocks]
    held, made, sems, out_sems = refs[1 + 2 * blocks:]
    copies = []
    for n, group in enumerate(plan):
        at = 0
        copies.append([])
        for k in group:
            count = parts[k].shape[1]
            copies[n].append(pltpu.make_async_copy(parts[k], held.at[n, :, pl.ds(at, count)], sems.at[k]))
            at += count
    for copy in [copy for group in copies for copy in group]:
        copy.start()
    results = []
    for n, group in enumerate(plan):
        for copy in copies[n]:
            copy.wait()
        made[n] = inner(rows[0], held[n, 0]) + inner(rows[1], held[n, 1])
        at = 0
        for k in group:
            count = parts[k].shape[1]
            results.append(pltpu.make_async_copy(made.at[n, :, pl.ds(at, count)], outs[k], out_sems.at[k]))
            results[-1].start()
            at += count
    for copy in results:
        copy.wait()


def scores_of(grant, rows, plan, *blocks):
    wide = rows.shape[2]
    return pl.pallas_call(
        functools.partial(scores_kernel, plan),
        out_shape=[jax.ShapeDtypeStruct((8 * N, a.shape[1]), jnp.float32) for a in blocks],
        in_specs=[VMEM] + [pl.BlockSpec(memory_space=pl.ANY)] * len(blocks),
        out_specs=[pl.BlockSpec(memory_space=pl.ANY)] * len(blocks),
        scratch_shapes=[
            pltpu.VMEM((len(plan), 2, 4 * N, wide), jnp.bfloat16),
            pltpu.VMEM((len(plan), 8 * N, 4 * N), jnp.float32),
            pltpu.SemaphoreType.DMA((len(blocks),)),
            pltpu.SemaphoreType.DMA((len(blocks),)),
        ],
        compiler_params=params(grant),
        cost_estimate=FREE,
    )(rows, *blocks)


def masks(rows, cols, at, count):
    same_u, cross_u, cross_e = (rows[pl.ds(at, count), k:k + 1] for k in range(3))
    same_v, cross_v, cross_p = (cols[k:k + 1, :] for k in range(3))
    hit = cross_e == cross_p
    return same_u != same_v, (cross_u != cross_v) | hit, hit


def scores_at(parts, at, count):
    return jnp.concatenate([part[pl.ds(at, count), :] for part in parts], axis=1) * SCALE


STATS = 16


def stats_kernel(core, amax, *refs):
    parts, (rows, cols, out, keep) = refs[:-4], refs[-4:]
    step = 32
    inc = core[0] == 1
    keep[...] = jnp.zeros_like(keep)

    @pl.loop(0, 4 * N // step)
    def _(k):
        at = pl.multiple_of(k * step, step)
        keep_s, keep_c, hit = masks(rows, cols, at, step)
        keep_c = keep_c & inc
        same = scores_at(parts, at, step)
        cross = scores_at(parts, pl.multiple_of(at + 4 * N, step), step)
        same = jnp.where(keep_s, same, -BIG)
        hits = jnp.sum(jnp.where(hit & inc, cross, 0.0), axis=1, keepdims=True)
        cross = jnp.where(keep_c, cross, -BIG)
        top = jnp.max(jnp.maximum(same, cross), axis=1, keepdims=True)
        total = jnp.sum(
            jnp.where(keep_s, jnp.exp(same - top), 0.0) + jnp.where(keep_c, jnp.exp(cross - top), 0.0),
            axis=1,
            keepdims=True,
        )
        group, low = k // (N // step), pl.multiple_of((k % (N // step)) * step, step)
        for n, value in enumerate((top, total, hits)):
            keep[n * 4 + group, pl.ds(low, step), :] = jnp.broadcast_to(value, (step, 128))

    for n in range(12):
        out[n:n + 1, :] = keep[n].T[0:1, :]
    out[12:16, :] = jnp.full((4, 128), amax[0], jnp.float32)


def stats_of(core, amax, parts, rows, cols):
    return pl.pallas_call(
        stats_kernel,
        out_shape=jax.ShapeDtypeStruct((STATS, 128), jnp.float32),
        in_specs=[SMEM] * 2 + [VMEM] * (len(parts) + 2),
        out_specs=VMEM,
        scratch_shapes=[pltpu.VMEM((12, 128, 128), jnp.float32)],
        compiler_params=params(8),
        cost_estimate=FREE,
    )(core, amax, *parts, rows, cols)


TURNED = ((0, 1, 2, 3), (2, 0, 3, 1), (1, 3, 0, 2), (3, 2, 1, 0))


def merge_kernel(core, *refs):
    (mine, theirs), (out, ends) = (refs[:4], refs[4:8]), refs[8:]
    first = core[0] == 0
    a = [ref[...] for ref in mine]
    b = [ref[...] for ref in theirs]
    line = [jnp.where(first, u, v) for u, v in zip(a, b)] + [jnp.where(first, v, u) for u, v in zip(a, b)]
    loose = jnp.zeros((1, 128), jnp.float32)
    valid = lax.broadcasted_iota(jnp.int32, (1, 128), 1) < N
    for g in range(4):
        of = lambda k: [v[4 * k + t[g]:4 * k + t[g] + 1] for v, t in zip(line, TURNED * 2)]
        tops, sums, hits = of(0), of(1), of(2)
        top = functools.reduce(jnp.maximum, tops)
        total = sum(u * jnp.exp(t - top) for u, t in zip(sums, tops))
        lse = top + jnp.log(total)
        gap = lse - sum(hits)
        out[g:g + 1, :] = lse
        out[4 + g:5 + g, :] = gap
        loose = jnp.maximum(loose, jnp.where(valid, 1.0 - jnp.exp(-gap), 0.0))
        if g == 0:
            ends[0:1, :] = lse
    ends[1:2, :] = loose
    most = functools.reduce(jnp.maximum, [v[12:13] for v in line])
    ends[2:8, :] = jnp.broadcast_to(most, (6, 128))


def merged(core, mine, theirs):
    return pl.pallas_call(
        merge_kernel,
        out_shape=[jax.ShapeDtypeStruct((8, 128), jnp.float32)] * 2,
        in_specs=[SMEM] + [VMEM] * 8,
        out_specs=[VMEM] * 2,
        compiler_params=params(4),
        cost_estimate=FREE,
    )(core, *mine, *theirs)


def lanes_of(rows):
    lane = lax.broadcasted_iota(jnp.int32, (8, 128), 1)
    wide = lambda v: jnp.broadcast_to(v, (8, 128))
    turn = lambda v, by: pltpu.roll(wide(v), by, axis=1) if by % 128 else wide(v)
    out = []
    for b in range(3):
        for a in (0, 2):
            out.append(jnp.where(lane < 64, wide(rows[4 * b + a]), turn(rows[4 * b + a + 1], 64)))
    for h in (0, 1):
        q = [turn(rows[12 + a], (32 * a - 32 * h) % 128) for a in range(4)]
        out.append(jnp.where(lane < 64, jnp.where(lane < 32, q[0], q[1]), jnp.where(lane < 96, q[2], q[3])))
    return jnp.concatenate(out, axis=1)[0:1]


def weights_kernel(first, count, core, *refs):
    parts, (rows, cols, lse_i, *plane, out, bound, col) = refs[:len(PARTS)], refs[len(PARTS):]
    step = 32
    w = core[0]
    for g in range(4):
        line = jnp.broadcast_to(lse_i[g:g + 1, :], (128, 128)).T[:N]
        col[0, g * N:(g + 1) * N, :] = line
        col[1, g * N:(g + 1) * N, :] = jnp.where(w == 1, line, 0.0)
    ends = [ref[8 * a:8 * a + 8, :] for ref in plane for a in range(4)]
    lj = lanes_of([v[0:1] for v in ends])
    cross_j = jnp.where(w == 1, 0.0, lj)
    loose = jnp.max(functools.reduce(jnp.maximum, [v[1:2] for v in ends]), axis=1, keepdims=True)
    most = jnp.max(functools.reduce(jnp.maximum, [v[2:3] for v in ends]), axis=1, keepdims=True)
    bound[...] = jnp.broadcast_to(jnp.maximum(loose, 1e-3) * jnp.maximum(most, 1e-20), (8, 128))

    @pl.loop(0, count * N // step)
    def _(k):
        at = pl.multiple_of(first * N + k * step, step)
        keep_s, keep_c, hit = masks(rows, cols, at, step)
        li = col[0, pl.ds(at, step), 0:1]
        lc = col[1, pl.ds(at, step), 0:1]
        same = scores_at(parts, at, step)
        cross = scores_at(parts, pl.multiple_of(at + 4 * N, step), step)
        m_s = jnp.where(keep_s, jnp.exp(same - li) + jnp.exp(same - lj), 0.0)
        m_c = jnp.where(keep_c, jnp.exp((cross - lc) - cross_j), 0.0) - jnp.where(hit, 1.0, 0.0)
        group = k // (N // step)
        base = group * 2 * N + (k % (N // step)) * step
        out[pl.ds(pl.multiple_of(base + w * N, step), step), :] = m_s.astype(jnp.bfloat16)
        out[pl.ds(pl.multiple_of(base + (1 - w) * N, step), step), :] = m_c.astype(jnp.bfloat16)


def weights_of(first, count, core, parts, rows, cols, lse_i, plane):
    return pl.pallas_call(
        functools.partial(weights_kernel, first, count),
        out_shape=[
            jax.ShapeDtypeStruct((count * 2 * N, J), jnp.bfloat16),
            jax.ShapeDtypeStruct((8, 128), jnp.float32),
        ],
        in_specs=[SMEM] + [VMEM] * (len(parts) + 7),
        out_specs=[VMEM] * 2,
        scratch_shapes=[pltpu.VMEM((2, 4 * N, 128), jnp.float32)],
        compiler_params=params(8),
        cost_estimate=FREE,
    )(core, *parts, rows, cols, lse_i, *plane)


def product_kernel(scaled, bound, mine, theirs, *refs):
    count = mine.shape[0] // (2 * N)
    blocks, outs, (held, sems) = refs[:2 * len(PARTS)], refs[2 * len(PARTS):-2], refs[-2:]
    copies = ([], [])
    for k in (0, 1):
        at = 0
        for n, size in enumerate(PARTS):
            i = k * len(PARTS) + n
            copies[k].append(pltpu.make_async_copy(blocks[i].at[k], held.at[k, pl.ds(at, size)], sems.at[i]))
            copies[k][-1].start()
            at += size
    shrink = 1.0 / bound[0:1, 0:1]
    step = 512
    for k, weights in enumerate((mine, theirs)):
        for copy in copies[k]:
            copy.wait()

        @pl.loop(0, held.shape[2] // step)
        def _(j):
            here = pl.ds(pl.multiple_of(j * step, step), step)
            term = plain(weights[...], held[k, :, here])
            for g in range(count):
                part = term[2 * N * g:2 * N * (g + 1)]
                if k == 0:
                    outs[g][:, here] = part
                else:
                    part = outs[g][:, here] + part
                    outs[g][:, here] = part * shrink if g >= scaled else part


def product_of(scaled, bound, mine, theirs, blocks, others):
    rows, wide = mine.shape[0], blocks[0].shape[2]
    outs = rows // (2 * N)
    return pl.pallas_call(
        functools.partial(product_kernel, scaled),
        out_shape=[jax.ShapeDtypeStruct((2 * N, wide), jnp.float32)] * outs,
        in_specs=[VMEM] * 3 + [pl.BlockSpec(memory_space=pl.ANY)] * (2 * len(PARTS)),
        out_specs=[VMEM] * outs,
        scratch_shapes=[pltpu.VMEM((2, J, wide), jnp.bfloat16), pltpu.SemaphoreType.DMA((2 * len(PARTS),))],
        compiler_params=params(20),
        cost_estimate=FREE,
    )(bound, mine, theirs, *blocks, *others)


def after(value, *others):
    return lax.optimization_barrier((value, *others))[0]


def settle(*values):
    return lax.optimization_barrier(values)


def body(queries, passages, passage_ids, pos_index):
    y, z, x, w = (lax.axis_index(name) for name in GRID)
    first = w == 0
    core = w.astype(jnp.int32).reshape(1)
    pick = lambda a, b: jnp.where(first, a, b)
    rows_of = functools.partial(lax.slice_in_dim, axis=1)
    low = lambda a: [rows_of(a, k * N, k * N + H) for k in range(a.shape[1] // N)]
    high = lambda a: [rows_of(a, k * N + H, (k + 1) * N) for k in range(a.shape[1] // N)]
    join = lambda parts: jnp.concatenate(parts, axis=1)
    line = lambda v, k: (up, far, down)[k - 1](v)
    by_first = lambda v, k: along(v, FIRST[k])
    by_second = lambda v, k: along(v, SECOND[k])
    ring = lambda v, send: [v] + [send(v, k) for k in RING[1:]]

    got = swap(pick(passages, queries))
    own = jnp.stack([pick(queries, passages), got])
    ints = jnp.stack([passage_ids, pos_index])

    fl, fr, own, *ints = settle(along(own, FIRST[1]), along(own, FIRST[3]), own, *ring(ints, line))
    f_low, f_high, own, fl, fr, *ints = settle(
        along(low(fl)[0], FIRST[1]), along(high(fr)[0], FIRST[3]), own, fl, fr, *ring(jnp.stack(ints), by_first)
    )
    group = place(((0, 0, N), (1, 0, N), (2, 0, N), (3, 0, H), (4, 0, H)), own, fl, fr, f_low, f_high)
    group, own, *ints = settle(group, own, *ring(jnp.stack(ints), by_second))
    ints = jnp.stack(ints)
    ids = ints[..., 0, :]
    dev, off = ints[..., 1, :] // N, ints[..., 1, :] % N
    near = lambda at, other: (lambda d: d ^ (d >> 1))((at - other) % 4)
    dy, dz, dx = near(y, dev // 16), near(z, dev // 4 % 4), near(x, dev % 4)
    pos = ((pick(dz, dy) * 4 + pick(dy, dz)) * 4 + dx) * N + off
    pair = jnp.arange(64 * N, dtype=jnp.int32).reshape(4, 4, 4, N)
    i_of = lambda t: t[0, 0].reshape(-1)
    j_of = lambda t: jnp.concatenate(
        [t[:3, :, 0].reshape(-1), t[3, :, 0].reshape(4, 2, H).transpose(1, 0, 2).reshape(-1)]
    )
    i_pair, i_id, i_pos = i_of(pair), i_of(ids), i_of(pos)
    j_pair, j_id, j_pos = j_of(pair), j_of(ids), j_of(pos)
    table, every = ids.reshape(1, -1), pair.reshape(1, -1)
    look = lambda at: jnp.sum(jnp.where(at[:, None] == every, table, 0), axis=1)
    i_tgt, j_tgt = look(i_pos), look(j_pos)
    rows = jnp.stack([pick(i_pair, i_id), pick(i_id, i_tgt), pick(i_pair, i_pos)] + [i_pair] * 5, axis=1)
    cols = jnp.stack([pick(j_pair, j_id), pick(j_tgt, j_id), pick(j_pos, j_pair)] + [j_pair] * 5)
    xl, xr = up(own), down(own)
    mine = [own, xl, xr, up(low(xl)[0]), down(high(xr)[0])]
    amax = jnp.maximum(
        *[jnp.max(jnp.abs(after(a, group, ids).astype(jnp.float32))) for a in (queries, passages)]
    )
    dl, dr, group, rows, cols, amax, *held = settle(
        along(group, SECOND[1]), along(group, SECOND[3]), group, rows, cols, amax, *mine, *[swap(a) for a in mine]
    )
    to_l = pack(tuple((0, k * N, H) for k in range(4)), dl)
    to_r = pack(tuple((0, k * N + H, H) for k in range(4)), dr)
    rows_i = rows_from([after(held[0], to_l, to_r)] + held[1:])
    blocks = [group, dl, dr]
    parts = scores_of(14, rows_i, ((0,), (1,), (2,)), *blocks)
    others = [swap(after(a, rows_i)) for a in blocks]
    gl, gr, *held = settle(along(to_l, SECOND[1]), along(to_r, SECOND[3]), *parts, *blocks)
    parts, blocks = held[:3], held[3:]
    blocks += [gl, gr]

    parts += scores_of(9, rows_i, ((0, 1),), gl, gr)
    found, *held = settle(stats_of(core, amax.reshape(1), parts, rows, cols), *others, swap(gl), swap(gr), *blocks)
    others, blocks = held[:5], held[5:]
    found = ring(found, line)
    lse_i, ends = merged(core, found, [swap(a) for a in found])
    loss = lse_i[4, :N]
    plane = ring(jnp.concatenate(ring(ends, by_first)), by_second)

    f16, f32 = jnp.float16, jnp.float32
    args = (parts, rows, cols, lse_i, plane)
    m_far, bound = weights_of(3, 1, core, *args)
    m_far_o = swap(m_far)
    m_rest, _ = weights_of(0, 3, after(core, m_far), *args)
    (opposite,) = product_of(0, bound, m_far, m_far_o, blocks, others)
    opposite = opposite.astype(f16)
    got_q, got_p, here, to_down, to_up = settle(
        up(opposite[:N]), down(opposite[N:]), *product_of(1, bound, m_rest, swap(m_rest), blocks, others)
    )
    below = up(jnp.concatenate([to_up[:N] + got_q.astype(f32), to_up[N:]]).astype(f16))
    above = down(jnp.concatenate([to_down[:N], to_down[N:] + got_p.astype(f32)]).astype(f16))
    grad = here + (below.astype(f32) + above.astype(f32)) * bound[0, 0]
    grad_q, grad_p = grad[:N], grad[N:]
    return loss, grad_q, grad_p


def solution(mesh):
    grid = Mesh(mesh.devices.reshape(4, 4, 4, 2), GRID)
    pair = ("y", "z", "x")
    placed = (P(pair, "w"), P(pair, "w"), P(pair), P(pair))
    return jax.shard_map(
        body,
        mesh=grid,
        in_specs=placed,
        out_specs=(P(pair), P(pair, "w"), P(pair, "w")),
        check_vma=False,
    )
```

```python
import functools
import math

import jax
import jax.numpy as jnp
from jax import lax
from jax.experimental import pallas as pl
from jax.experimental.pallas import tpu as pltpu
from jax.sharding import Mesh, PartitionSpec as P

D = 4096
N = 64
H = N // 2
SCALE = 3.0 / math.sqrt(D)
BIG = 1e30
GRID = ("y", "z", "x", "w")
UP = [(i, (i + 1) % 4) for i in range(4)]
DOWN = [(i, (i - 1) % 4) for i in range(4)]
FAR = [(i, (i + 2) % 4) for i in range(4)]
RING = (0, 1, 3, 2)
PARTS = (256, 256, 256, 128, 128)
J = sum(PARTS)


def steps(first, second, by):
    moves = []
    for y in range(4):
        for z in range(4):
            for x in range(4):
                for w in range(2):
                    axis = second if w else first
                    to_y, to_z = ((y + by) % 4, z) if axis == "y" else (y, (z + by) % 4)
                    flat = lambda y, z: ((y * 4 + z) * 4 + x) * 2 + w
                    moves.append((flat(y, z), flat(to_y, to_z)))
    return moves


FIRST = {by: steps("y", "z", by) for by in (1, 2, 3)}
SECOND = {by: steps("z", "y", by) for by in (1, 2, 3)}


def along(value, moves):
    return lax.ppermute(value, GRID, moves)


def swap(value):
    return lax.ppermute(value, "w", [(0, 1), (1, 0)])


def up(value):
    return lax.ppermute(value, "x", UP)


def down(value):
    return lax.ppermute(value, "x", DOWN)


def far(value):
    return lax.ppermute(value, "x", FAR)


def inner(left, right):
    return lax.dot_general(
        left, right, (((1,), (1,)), ((), ())), preferred_element_type=jnp.float32
    )


def plain(left, right):
    return jnp.dot(left, right, preferred_element_type=jnp.float32)


VMEM = pl.BlockSpec(memory_space=pltpu.VMEM)
SMEM = pl.BlockSpec(memory_space=pltpu.SMEM)
def params(mib):
    return pltpu.CompilerParams(vmem_limit_bytes=mib << 20)


FREE = pl.CostEstimate(flops=0, bytes_accessed=0, transcendentals=0)


def pack_kernel(plan, *refs):
    pieces, out, sems = refs[:-2], refs[-2], refs[-1]
    copies, at = [], 0
    for n, (k, start, count) in enumerate(plan):
        copies.append(
            pltpu.make_async_copy(
                pieces[k].at[:, pl.ds(start, count)], out.at[:, pl.ds(at, count)], sems.at[n]
            )
        )
        copies[n].start()
        at += count
    for copy in copies:
        copy.wait()


def pack(plan, *pieces):
    rows, wide = sum(count for _, _, count in plan), pieces[0].shape[2]
    return pl.pallas_call(
        functools.partial(pack_kernel, plan),
        out_shape=jax.ShapeDtypeStruct((2, rows, wide), jnp.bfloat16),
        in_specs=[pl.BlockSpec(memory_space=pl.ANY)] * len(pieces),
        out_specs=VMEM,
        scratch_shapes=[pltpu.SemaphoreType.DMA((len(plan),))],
        compiler_params=params(8),
        cost_estimate=FREE,
    )(*pieces)


def place_kernel(plan, *refs):
    pieces, out = refs[:-1], refs[-1]
    at = 0
    for k, start, count in plan:
        out[:, at:at + count, :] = pieces[k][:, start:start + count, :]
        at += count


def place(plan, *pieces):
    rows, wide = sum(count for _, _, count in plan), pieces[0].shape[2]
    return pl.pallas_call(
        functools.partial(place_kernel, plan),
        out_shape=jax.ShapeDtypeStruct((2, rows, wide), jnp.bfloat16),
        in_specs=[VMEM] * len(pieces),
        out_specs=VMEM,
        compiler_params=params(8),
        cost_estimate=FREE,
    )(*pieces)


def rows_kernel(*refs):
    pieces, out = refs[:10], refs[10]
    at = 0
    for k, piece in enumerate(pieces):
        count = piece.shape[1]
        for h in (0, 1):
            out[h ^ (k // 5), at:at + count, :] = piece[h]
        at += count


def rows_from(pieces):
    wide = pieces[0].shape[2]
    return pl.pallas_call(
        rows_kernel,
        out_shape=jax.ShapeDtypeStruct((2, 8 * N, wide), jnp.bfloat16),
        in_specs=[VMEM] * 10,
        out_specs=VMEM,
        compiler_params=params(12),
        cost_estimate=FREE,
    )(*pieces)


def scores_kernel(plan, *refs):
    blocks = sum(len(group) for group in plan)
    rows, parts, outs = refs[0], refs[1:1 + blocks], refs[1 + blocks:1 + 2 * blocks]
    held, made, sems, out_sems = refs[1 + 2 * blocks:]
    copies = []
    for n, group in enumerate(plan):
        at = 0
        copies.append([])
        for k in group:
            count = parts[k].shape[1]
            copies[n].append(pltpu.make_async_copy(parts[k], held.at[n, :, pl.ds(at, count)], sems.at[k]))
            at += count
    for copy in [copy for group in copies for copy in group]:
        copy.start()
    results = []
    for n, group in enumerate(plan):
        for copy in copies[n]:
            copy.wait()
        made[n] = inner(rows[0], held[n, 0]) + inner(rows[1], held[n, 1])
        at = 0
        for k in group:
            count = parts[k].shape[1]
            results.append(pltpu.make_async_copy(made.at[n, :, pl.ds(at, count)], outs[k], out_sems.at[k]))
            results[-1].start()
            at += count
    for copy in results:
        copy.wait()


def scores_of(grant, rows, plan, *blocks):
    wide = rows.shape[2]
    return pl.pallas_call(
        functools.partial(scores_kernel, plan),
        out_shape=[jax.ShapeDtypeStruct((8 * N, a.shape[1]), jnp.float32) for a in blocks],
        in_specs=[VMEM] + [pl.BlockSpec(memory_space=pl.ANY)] * len(blocks),
        out_specs=[pl.BlockSpec(memory_space=pl.ANY)] * len(blocks),
        scratch_shapes=[
            pltpu.VMEM((len(plan), 2, 4 * N, wide), jnp.bfloat16),
            pltpu.VMEM((len(plan), 8 * N, 4 * N), jnp.float32),
            pltpu.SemaphoreType.DMA((len(blocks),)),
            pltpu.SemaphoreType.DMA((len(blocks),)),
        ],
        compiler_params=params(grant),
        cost_estimate=FREE,
    )(rows, *blocks)


def masks(rows, cols, at, count):
    same_u, cross_u, cross_e = (rows[pl.ds(at, count), k:k + 1] for k in range(3))
    same_v, cross_v, cross_p = (cols[k:k + 1, :] for k in range(3))
    hit = cross_e == cross_p
    return same_u != same_v, (cross_u != cross_v) | hit, hit


def scores_at(parts, at, count):
    return jnp.concatenate([part[pl.ds(at, count), :] for part in parts], axis=1) * SCALE


STATS = 16


def stats_kernel(core, amax, *refs):
    parts, (rows, cols, out, keep) = refs[:-4], refs[-4:]
    step = 32
    inc = core[0] == 1
    keep[...] = jnp.zeros_like(keep)

    @pl.loop(0, 4 * N // step)
    def _(k):
        at = pl.multiple_of(k * step, step)
        keep_s, keep_c, hit = masks(rows, cols, at, step)
        keep_c = keep_c & inc
        same = scores_at(parts, at, step)
        cross = scores_at(parts, pl.multiple_of(at + 4 * N, step), step)
        same = jnp.where(keep_s, same, -BIG)
        hits = jnp.sum(jnp.where(hit & inc, cross, 0.0), axis=1, keepdims=True)
        cross = jnp.where(keep_c, cross, -BIG)
        top = jnp.max(jnp.maximum(same, cross), axis=1, keepdims=True)
        total = jnp.sum(
            jnp.where(keep_s, jnp.exp(same - top), 0.0) + jnp.where(keep_c, jnp.exp(cross - top), 0.0),
            axis=1,
            keepdims=True,
        )
        group, low = k // (N // step), pl.multiple_of((k % (N // step)) * step, step)
        for n, value in enumerate((top, total, hits)):
            keep[n * 4 + group, pl.ds(low, step), :] = jnp.broadcast_to(value, (step, 128))

    for n in range(12):
        out[n:n + 1, :] = keep[n].T[0:1, :]
    out[12:16, :] = jnp.full((4, 128), amax[0], jnp.float32)


def stats_of(core, amax, parts, rows, cols):
    return pl.pallas_call(
        stats_kernel,
        out_shape=jax.ShapeDtypeStruct((STATS, 128), jnp.float32),
        in_specs=[SMEM] * 2 + [VMEM] * (len(parts) + 2),
        out_specs=VMEM,
        scratch_shapes=[pltpu.VMEM((12, 128, 128), jnp.float32)],
        compiler_params=params(8),
        cost_estimate=FREE,
    )(core, amax, *parts, rows, cols)


TURNED = ((0, 1, 2, 3), (2, 0, 3, 1), (1, 3, 0, 2), (3, 2, 1, 0))


def merge_kernel(core, *refs):
    (mine, theirs), (out, ends) = (refs[:4], refs[4:8]), refs[8:]
    first = core[0] == 0
    a = [ref[...] for ref in mine]
    b = [ref[...] for ref in theirs]
    line = [jnp.where(first, u, v) for u, v in zip(a, b)] + [jnp.where(first, v, u) for u, v in zip(a, b)]
    loose = jnp.zeros((1, 128), jnp.float32)
    valid = lax.broadcasted_iota(jnp.int32, (1, 128), 1) < N
    for g in range(4):
        of = lambda k: [v[4 * k + t[g]:4 * k + t[g] + 1] for v, t in zip(line, TURNED * 2)]
        tops, sums, hits = of(0), of(1), of(2)
        top = functools.reduce(jnp.maximum, tops)
        total = sum(u * jnp.exp(t - top) for u, t in zip(sums, tops))
        lse = top + jnp.log(total)
        gap = lse - sum(hits)
        out[g:g + 1, :] = lse
        out[4 + g:5 + g, :] = gap
        loose = jnp.maximum(loose, jnp.where(valid, 1.0 - jnp.exp(-gap), 0.0))
        if g == 0:
            ends[0:1, :] = lse
    ends[1:2, :] = loose
    most = functools.reduce(jnp.maximum, [v[12:13] for v in line])
    ends[2:8, :] = jnp.broadcast_to(most, (6, 128))


def merged(core, mine, theirs):
    return pl.pallas_call(
        merge_kernel,
        out_shape=[jax.ShapeDtypeStruct((8, 128), jnp.float32)] * 2,
        in_specs=[SMEM] + [VMEM] * 8,
        out_specs=[VMEM] * 2,
        compiler_params=params(4),
        cost_estimate=FREE,
    )(core, *mine, *theirs)


def lanes_of(rows):
    lane = lax.broadcasted_iota(jnp.int32, (8, 128), 1)
    wide = lambda v: jnp.broadcast_to(v, (8, 128))
    turn = lambda v, by: pltpu.roll(wide(v), by, axis=1) if by % 128 else wide(v)
    out = []
    for b in range(3):
        for a in (0, 2):
            out.append(jnp.where(lane < 64, wide(rows[4 * b + a]), turn(rows[4 * b + a + 1], 64)))
    for h in (0, 1):
        q = [turn(rows[12 + a], (32 * a - 32 * h) % 128) for a in range(4)]
        out.append(jnp.where(lane < 64, jnp.where(lane < 32, q[0], q[1]), jnp.where(lane < 96, q[2], q[3])))
    return jnp.concatenate(out, axis=1)[0:1]


def weights_kernel(first, count, core, *refs):
    parts, (rows, cols, lse_i, *plane, out, bound, col) = refs[:len(PARTS)], refs[len(PARTS):]
    step = 32
    w = core[0]
    for g in range(4):
        line = jnp.broadcast_to(lse_i[g:g + 1, :], (128, 128)).T[:N]
        col[0, g * N:(g + 1) * N, :] = line
        col[1, g * N:(g + 1) * N, :] = jnp.where(w == 1, line, 0.0)
    ends = [ref[8 * a:8 * a + 8, :] for ref in plane for a in range(4)]
    lj = lanes_of([v[0:1] for v in ends])
    cross_j = jnp.where(w == 1, 0.0, lj)
    loose = jnp.max(functools.reduce(jnp.maximum, [v[1:2] for v in ends]), axis=1, keepdims=True)
    most = jnp.max(functools.reduce(jnp.maximum, [v[2:3] for v in ends]), axis=1, keepdims=True)
    bound[...] = jnp.broadcast_to(jnp.maximum(loose, 1e-3) * jnp.maximum(most, 1e-20), (8, 128))

    @pl.loop(0, count * N // step)
    def _(k):
        at = pl.multiple_of(first * N + k * step, step)
        keep_s, keep_c, hit = masks(rows, cols, at, step)
        li = col[0, pl.ds(at, step), 0:1]
        lc = col[1, pl.ds(at, step), 0:1]
        same = scores_at(parts, at, step)
        cross = scores_at(parts, pl.multiple_of(at + 4 * N, step), step)
        m_s = jnp.where(keep_s, jnp.exp(same - li) + jnp.exp(same - lj), 0.0)
        m_c = jnp.where(keep_c, jnp.exp((cross - lc) - cross_j), 0.0) - jnp.where(hit, 1.0, 0.0)
        group = k // (N // step)
        base = group * 2 * N + (k % (N // step)) * step
        out[pl.ds(pl.multiple_of(base + w * N, step), step), :] = m_s.astype(jnp.bfloat16)
        out[pl.ds(pl.multiple_of(base + (1 - w) * N, step), step), :] = m_c.astype(jnp.bfloat16)


def weights_of(first, count, core, parts, rows, cols, lse_i, plane):
    return pl.pallas_call(
        functools.partial(weights_kernel, first, count),
        out_shape=[
            jax.ShapeDtypeStruct((count * 2 * N, J), jnp.bfloat16),
            jax.ShapeDtypeStruct((8, 128), jnp.float32),
        ],
        in_specs=[SMEM] + [VMEM] * (len(parts) + 7),
        out_specs=[VMEM] * 2,
        scratch_shapes=[pltpu.VMEM((2, 4 * N, 128), jnp.float32)],
        compiler_params=params(8),
        cost_estimate=FREE,
    )(core, *parts, rows, cols, lse_i, *plane)


def product_kernel(scaled, bound, mine, theirs, *refs):
    count = mine.shape[0] // (2 * N)
    blocks, outs, (held, sems) = refs[:2 * len(PARTS)], refs[2 * len(PARTS):-2], refs[-2:]
    copies = ([], [])
    for k in (0, 1):
        at = 0
        for n, size in enumerate(PARTS):
            i = k * len(PARTS) + n
            copies[k].append(pltpu.make_async_copy(blocks[i].at[k], held.at[k, pl.ds(at, size)], sems.at[i]))
            copies[k][-1].start()
            at += size
    shrink = 1.0 / bound[0:1, 0:1]
    step = 512
    for k, weights in enumerate((mine, theirs)):
        for copy in copies[k]:
            copy.wait()

        @pl.loop(0, held.shape[2] // step)
        def _(j):
            here = pl.ds(pl.multiple_of(j * step, step), step)
            term = plain(weights[...], held[k, :, here])
            for g in range(count):
                part = term[2 * N * g:2 * N * (g + 1)]
                if k == 0:
                    outs[g][:, here] = part
                else:
                    part = outs[g][:, here] + part
                    outs[g][:, here] = part * shrink if g >= scaled else part


def product_of(scaled, bound, mine, theirs, blocks, others):
    rows, wide = mine.shape[0], blocks[0].shape[2]
    outs = rows // (2 * N)
    return pl.pallas_call(
        functools.partial(product_kernel, scaled),
        out_shape=[jax.ShapeDtypeStruct((2 * N, wide), jnp.float32)] * outs,
        in_specs=[VMEM] * 3 + [pl.BlockSpec(memory_space=pl.ANY)] * (2 * len(PARTS)),
        out_specs=[VMEM] * outs,
        scratch_shapes=[pltpu.VMEM((2, J, wide), jnp.bfloat16), pltpu.SemaphoreType.DMA((2 * len(PARTS),))],
        compiler_params=params(20),
        cost_estimate=FREE,
    )(bound, mine, theirs, *blocks, *others)


def after(value, *others):
    return lax.optimization_barrier((value, *others))[0]


def settle(*values):
    return lax.optimization_barrier(values)


def body(queries, passages, passage_ids, pos_index):
    y, z, x, w = (lax.axis_index(name) for name in GRID)
    first = w == 0
    core = w.astype(jnp.int32).reshape(1)
    pick = lambda a, b: jnp.where(first, a, b)
    rows_of = functools.partial(lax.slice_in_dim, axis=1)
    low = lambda a: [rows_of(a, k * N, k * N + H) for k in range(a.shape[1] // N)]
    high = lambda a: [rows_of(a, k * N + H, (k + 1) * N) for k in range(a.shape[1] // N)]
    join = lambda parts: jnp.concatenate(parts, axis=1)
    line = lambda v, k: (up, far, down)[k - 1](v)
    by_first = lambda v, k: along(v, FIRST[k])
    by_second = lambda v, k: along(v, SECOND[k])
    ring = lambda v, send: [v] + [send(v, k) for k in RING[1:]]

    got = swap(pick(passages, queries))
    own = jnp.stack([pick(queries, passages), got])
    ints = jnp.stack([passage_ids, pos_index])

    fl, fr, own, *ints = settle(along(own, FIRST[1]), along(own, FIRST[3]), own, *ring(ints, line))
    f_low, f_high, own, fl, fr, *ints = settle(
        along(low(fl)[0], FIRST[1]), along(high(fr)[0], FIRST[3]), own, fl, fr, *ring(jnp.stack(ints), by_first)
    )
    group = place(((0, 0, N), (1, 0, N), (2, 0, N), (3, 0, H), (4, 0, H)), own, fl, fr, f_low, f_high)
    group, own, *ints = settle(group, own, *ring(jnp.stack(ints), by_second))
    ints = jnp.stack(ints)
    ids = ints[..., 0, :]
    dev, off = ints[..., 1, :] // N, ints[..., 1, :] % N
    near = lambda at, other: (lambda d: d ^ (d >> 1))((at - other) % 4)
    dy, dz, dx = near(y, dev // 16), near(z, dev // 4 % 4), near(x, dev % 4)
    pos = ((pick(dz, dy) * 4 + pick(dy, dz)) * 4 + dx) * N + off
    pair = jnp.arange(64 * N, dtype=jnp.int32).reshape(4, 4, 4, N)
    i_of = lambda t: t[0, 0].reshape(-1)
    j_of = lambda t: jnp.concatenate(
        [t[:3, :, 0].reshape(-1), t[3, :, 0].reshape(4, 2, H).transpose(1, 0, 2).reshape(-1)]
    )
    i_pair, i_id, i_pos = i_of(pair), i_of(ids), i_of(pos)
    j_pair, j_id, j_pos = j_of(pair), j_of(ids), j_of(pos)
    table, every = ids.reshape(1, -1), pair.reshape(1, -1)
    look = lambda at: jnp.sum(jnp.where(at[:, None] == every, table, 0), axis=1)
    i_tgt, j_tgt = look(i_pos), look(j_pos)
    rows = jnp.stack([pick(i_pair, i_id), pick(i_id, i_tgt), pick(i_pair, i_pos)] + [i_pair] * 5, axis=1)
    cols = jnp.stack([pick(j_pair, j_id), pick(j_tgt, j_id), pick(j_pos, j_pair)] + [j_pair] * 5)
    xl, xr = up(own), down(own)
    mine = [own, xl, xr, up(low(xl)[0]), down(high(xr)[0])]
    amax = jnp.maximum(
        *[jnp.max(jnp.abs(after(a, group, ids).astype(jnp.float32))) for a in (queries, passages)]
    )
    dl, dr, group, rows, cols, amax, *held = settle(
        along(group, SECOND[1]), along(group, SECOND[3]), group, rows, cols, amax, *mine, *[swap(a) for a in mine]
    )
    to_l = pack(tuple((0, k * N, H) for k in range(4)), dl)
    to_r = pack(tuple((0, k * N + H, H) for k in range(4)), dr)
    rows_i = rows_from([after(held[0], to_l, to_r)] + held[1:])
    blocks = [group, dl, dr]
    parts = scores_of(14, rows_i, ((0,), (1,), (2,)), *blocks)
    others = [swap(after(a, rows_i)) for a in blocks]
    gl, gr, *held = settle(along(to_l, SECOND[1]), along(to_r, SECOND[3]), *parts, *blocks)
    parts, blocks = held[:3], held[3:]
    blocks += [gl, gr]

    parts += scores_of(9, rows_i, ((0, 1),), gl, gr)
    found, *held = settle(stats_of(core, amax.reshape(1), parts, rows, cols), *others, swap(gl), swap(gr), *blocks)
    others, blocks = held[:5], held[5:]
    found = ring(found, line)
    lse_i, ends = merged(core, found, [swap(a) for a in found])
    loss = lse_i[4, :N]
    plane = ring(jnp.concatenate(ring(ends, by_first)), by_second)

    f16, f32 = jnp.float16, jnp.float32
    args = (parts, rows, cols, lse_i, plane)
    m_far, bound = weights_of(3, 1, core, *args)
    m_far_o = swap(m_far)
    m_near, _ = weights_of(1, 2, after(core, m_far), *args)
    (opposite,) = product_of(0, bound, m_far, m_far_o, blocks, others)
    opposite = opposite.astype(f16)
    got_q, got_p, to_down, to_up = settle(
        up(opposite[:N]), down(opposite[N:]), *product_of(0, bound, m_near, swap(m_near), blocks, others)
    )
    below = up(jnp.concatenate([to_up[:N] + got_q.astype(f32), to_up[N:]]).astype(f16))
    above = down(jnp.concatenate([to_down[:N], to_down[N:] + got_p.astype(f32)]).astype(f16))
    m_own, _ = weights_of(0, 1, after(core, to_up), *args)
    (here,) = product_of(1, bound, m_own, swap(m_own), blocks, others)
    grad = here + (below.astype(f32) + above.astype(f32)) * bound[0, 0]
    grad_q, grad_p = grad[:N], grad[N:]
    return loss, grad_q, grad_p


def solution(mesh):
    grid = Mesh(mesh.devices.reshape(4, 4, 4, 2), GRID)
    pair = ("y", "z", "x")
    placed = (P(pair, "w"), P(pair, "w"), P(pair), P(pair))
    return jax.shard_map(
        body,
        mesh=grid,
        in_specs=placed,
        out_specs=(P(pair), P(pair, "w"), P(pair, "w")),
        check_vma=False,
    )
```

```python
import functools
import math

import jax
import jax.numpy as jnp
from jax import lax
from jax.experimental import pallas as pl
from jax.experimental.pallas import tpu as pltpu
from jax.sharding import Mesh, PartitionSpec as P

D = 4096
N = 64
H = N // 2
SCALE = 3.0 / math.sqrt(D)
BIG = 1e30
GRID = ("y", "z", "x", "w")
UP = [(i, (i + 1) % 4) for i in range(4)]
DOWN = [(i, (i - 1) % 4) for i in range(4)]
FAR = [(i, (i + 2) % 4) for i in range(4)]
RING = (0, 1, 3, 2)
PARTS = (256, 256, 256, 128, 128)
J = sum(PARTS)


def steps(first, second, by):
    moves = []
    for y in range(4):
        for z in range(4):
            for x in range(4):
                for w in range(2):
                    axis = second if w else first
                    to_y, to_z = ((y + by) % 4, z) if axis == "y" else (y, (z + by) % 4)
                    flat = lambda y, z: ((y * 4 + z) * 4 + x) * 2 + w
                    moves.append((flat(y, z), flat(to_y, to_z)))
    return moves


FIRST = {by: steps("y", "z", by) for by in (1, 2, 3)}
SECOND = {by: steps("z", "y", by) for by in (1, 2, 3)}


def along(value, moves):
    return lax.ppermute(value, GRID, moves)


def swap(value):
    return lax.ppermute(value, "w", [(0, 1), (1, 0)])


def up(value):
    return lax.ppermute(value, "x", UP)


def down(value):
    return lax.ppermute(value, "x", DOWN)


def far(value):
    return lax.ppermute(value, "x", FAR)


def inner(left, right):
    return lax.dot_general(
        left, right, (((1,), (1,)), ((), ())), preferred_element_type=jnp.float32
    )


def plain(left, right):
    return jnp.dot(left, right, preferred_element_type=jnp.float32)


VMEM = pl.BlockSpec(memory_space=pltpu.VMEM)
SMEM = pl.BlockSpec(memory_space=pltpu.SMEM)
def params(mib):
    return pltpu.CompilerParams(vmem_limit_bytes=mib << 20)


FREE = pl.CostEstimate(flops=0, bytes_accessed=0, transcendentals=0)


def pack_kernel(plan, *refs):
    pieces, out, sems = refs[:-2], refs[-2], refs[-1]
    copies, at = [], 0
    for n, (k, start, count) in enumerate(plan):
        copies.append(
            pltpu.make_async_copy(
                pieces[k].at[:, pl.ds(start, count)], out.at[:, pl.ds(at, count)], sems.at[n]
            )
        )
        copies[n].start()
        at += count
    for copy in copies:
        copy.wait()


def pack(plan, *pieces):
    rows, wide = sum(count for _, _, count in plan), pieces[0].shape[2]
    return pl.pallas_call(
        functools.partial(pack_kernel, plan),
        out_shape=jax.ShapeDtypeStruct((2, rows, wide), jnp.bfloat16),
        in_specs=[pl.BlockSpec(memory_space=pl.ANY)] * len(pieces),
        out_specs=VMEM,
        scratch_shapes=[pltpu.SemaphoreType.DMA((len(plan),))],
        compiler_params=params(8),
        cost_estimate=FREE,
    )(*pieces)


def place_kernel(plan, *refs):
    pieces, out = refs[:-1], refs[-1]
    at = 0
    for k, start, count in plan:
        out[:, at:at + count, :] = pieces[k][:, start:start + count, :]
        at += count


def place(plan, *pieces):
    rows, wide = sum(count for _, _, count in plan), pieces[0].shape[2]
    return pl.pallas_call(
        functools.partial(place_kernel, plan),
        out_shape=jax.ShapeDtypeStruct((2, rows, wide), jnp.bfloat16),
        in_specs=[VMEM] * len(pieces),
        out_specs=VMEM,
        compiler_params=params(8),
        cost_estimate=FREE,
    )(*pieces)


def rows_kernel(*refs):
    pieces, out = refs[:10], refs[10]
    at = 0
    for k, piece in enumerate(pieces):
        count = piece.shape[1]
        for h in (0, 1):
            out[h ^ (k // 5), at:at + count, :] = piece[h]
        at += count


def rows_from(pieces):
    wide = pieces[0].shape[2]
    return pl.pallas_call(
        rows_kernel,
        out_shape=jax.ShapeDtypeStruct((2, 8 * N, wide), jnp.bfloat16),
        in_specs=[VMEM] * 10,
        out_specs=VMEM,
        compiler_params=params(12),
        cost_estimate=FREE,
    )(*pieces)


def scores_kernel(plan, *refs):
    blocks = sum(len(group) for group in plan)
    rows, parts, outs = refs[0], refs[1:1 + blocks], refs[1 + blocks:1 + 2 * blocks]
    held, made, sems, out_sems = refs[1 + 2 * blocks:]
    copies = []
    for n, group in enumerate(plan):
        at = 0
        copies.append([])
        for k in group:
            count = parts[k].shape[1]
            copies[n].append(pltpu.make_async_copy(parts[k], held.at[n, :, pl.ds(at, count)], sems.at[k]))
            at += count
    for copy in [copy for group in copies for copy in group]:
        copy.start()
    results = []
    for n, group in enumerate(plan):
        for copy in copies[n]:
            copy.wait()
        made[n] = inner(rows[0], held[n, 0]) + inner(rows[1], held[n, 1])
        at = 0
        for k in group:
            count = parts[k].shape[1]
            results.append(pltpu.make_async_copy(made.at[n, :, pl.ds(at, count)], outs[k], out_sems.at[k]))
            results[-1].start()
            at += count
    for copy in results:
        copy.wait()


def scores_of(grant, rows, plan, *blocks):
    wide = rows.shape[2]
    return pl.pallas_call(
        functools.partial(scores_kernel, plan),
        out_shape=[jax.ShapeDtypeStruct((8 * N, a.shape[1]), jnp.float32) for a in blocks],
        in_specs=[VMEM] + [pl.BlockSpec(memory_space=pl.ANY)] * len(blocks),
        out_specs=[pl.BlockSpec(memory_space=pl.ANY)] * len(blocks),
        scratch_shapes=[
            pltpu.VMEM((len(plan), 2, 4 * N, wide), jnp.bfloat16),
            pltpu.VMEM((len(plan), 8 * N, 4 * N), jnp.float32),
            pltpu.SemaphoreType.DMA((len(blocks),)),
            pltpu.SemaphoreType.DMA((len(blocks),)),
        ],
        compiler_params=params(grant),
        cost_estimate=FREE,
    )(rows, *blocks)


def masks(rows, cols, at, count):
    same_u, cross_u, cross_e = (rows[pl.ds(at, count), k:k + 1] for k in range(3))
    same_v, cross_v, cross_p = (cols[k:k + 1, :] for k in range(3))
    hit = cross_e == cross_p
    return same_u != same_v, (cross_u != cross_v) | hit, hit


def scores_at(parts, at, count):
    return jnp.concatenate([part[pl.ds(at, count), :] for part in parts], axis=1) * SCALE


STATS = 16


def stats_kernel(core, amax, *refs):
    parts, (rows, cols, out, keep) = refs[:-4], refs[-4:]
    step = 32
    inc = core[0] == 1
    keep[...] = jnp.zeros_like(keep)

    @pl.loop(0, 4 * N // step)
    def _(k):
        at = pl.multiple_of(k * step, step)
        keep_s, keep_c, hit = masks(rows, cols, at, step)
        keep_c = keep_c & inc
        same = scores_at(parts, at, step)
        cross = scores_at(parts, pl.multiple_of(at + 4 * N, step), step)
        same = jnp.where(keep_s, same, -BIG)
        hits = jnp.sum(jnp.where(hit & inc, cross, 0.0), axis=1, keepdims=True)
        cross = jnp.where(keep_c, cross, -BIG)
        top = jnp.max(jnp.maximum(same, cross), axis=1, keepdims=True)
        total = jnp.sum(
            jnp.where(keep_s, jnp.exp(same - top), 0.0) + jnp.where(keep_c, jnp.exp(cross - top), 0.0),
            axis=1,
            keepdims=True,
        )
        group, low = k // (N // step), pl.multiple_of((k % (N // step)) * step, step)
        for n, value in enumerate((top, total, hits)):
            keep[n * 4 + group, pl.ds(low, step), :] = jnp.broadcast_to(value, (step, 128))

    for n in range(12):
        out[n:n + 1, :] = keep[n].T[0:1, :]
    out[12:16, :] = jnp.full((4, 128), amax[0], jnp.float32)


def stats_of(core, amax, parts, rows, cols):
    return pl.pallas_call(
        stats_kernel,
        out_shape=jax.ShapeDtypeStruct((STATS, 128), jnp.float32),
        in_specs=[SMEM] * 2 + [VMEM] * (len(parts) + 2),
        out_specs=VMEM,
        scratch_shapes=[pltpu.VMEM((12, 128, 128), jnp.float32)],
        compiler_params=params(8),
        cost_estimate=FREE,
    )(core, amax, *parts, rows, cols)


TURNED = ((0, 1, 2, 3), (2, 0, 3, 1), (1, 3, 0, 2), (3, 2, 1, 0))


def merge_kernel(core, *refs):
    (mine, theirs), (out, ends) = (refs[:4], refs[4:8]), refs[8:]
    first = core[0] == 0
    a = [ref[...] for ref in mine]
    b = [ref[...] for ref in theirs]
    line = [jnp.where(first, u, v) for u, v in zip(a, b)] + [jnp.where(first, v, u) for u, v in zip(a, b)]
    loose = jnp.zeros((1, 128), jnp.float32)
    valid = lax.broadcasted_iota(jnp.int32, (1, 128), 1) < N
    for g in range(4):
        of = lambda k: [v[4 * k + t[g]:4 * k + t[g] + 1] for v, t in zip(line, TURNED * 2)]
        tops, sums, hits = of(0), of(1), of(2)
        top = functools.reduce(jnp.maximum, tops)
        total = sum(u * jnp.exp(t - top) for u, t in zip(sums, tops))
        lse = top + jnp.log(total)
        gap = lse - sum(hits)
        out[g:g + 1, :] = lse
        out[4 + g:5 + g, :] = gap
        loose = jnp.maximum(loose, jnp.where(valid, 1.0 - jnp.exp(-gap), 0.0))
        if g == 0:
            ends[0:1, :] = lse
    ends[1:2, :] = loose
    most = functools.reduce(jnp.maximum, [v[12:13] for v in line])
    ends[2:8, :] = jnp.broadcast_to(most, (6, 128))


def merged(core, mine, theirs):
    return pl.pallas_call(
        merge_kernel,
        out_shape=[jax.ShapeDtypeStruct((8, 128), jnp.float32)] * 2,
        in_specs=[SMEM] + [VMEM] * 8,
        out_specs=[VMEM] * 2,
        compiler_params=params(4),
        cost_estimate=FREE,
    )(core, *mine, *theirs)


def lanes_of(rows):
    lane = lax.broadcasted_iota(jnp.int32, (8, 128), 1)
    wide = lambda v: jnp.broadcast_to(v, (8, 128))
    turn = lambda v, by: pltpu.roll(wide(v), by, axis=1) if by % 128 else wide(v)
    out = []
    for b in range(3):
        for a in (0, 2):
            out.append(jnp.where(lane < 64, wide(rows[4 * b + a]), turn(rows[4 * b + a + 1], 64)))
    for h in (0, 1):
        q = [turn(rows[12 + a], (32 * a - 32 * h) % 128) for a in range(4)]
        out.append(jnp.where(lane < 64, jnp.where(lane < 32, q[0], q[1]), jnp.where(lane < 96, q[2], q[3])))
    return jnp.concatenate(out, axis=1)[0:1]


def weights_kernel(first, count, core, *refs):
    parts, (rows, cols, lse_i, *plane, out, bound, col) = refs[:len(PARTS)], refs[len(PARTS):]
    step = 32
    w = core[0]
    for g in range(4):
        line = jnp.broadcast_to(lse_i[g:g + 1, :], (128, 128)).T[:N]
        col[0, g * N:(g + 1) * N, :] = line
        col[1, g * N:(g + 1) * N, :] = jnp.where(w == 1, line, 0.0)
    ends = [ref[8 * a:8 * a + 8, :] for ref in plane for a in range(4)]
    lj = lanes_of([v[0:1] for v in ends])
    cross_j = jnp.where(w == 1, 0.0, lj)
    loose = jnp.max(functools.reduce(jnp.maximum, [v[1:2] for v in ends]), axis=1, keepdims=True)
    most = jnp.max(functools.reduce(jnp.maximum, [v[2:3] for v in ends]), axis=1, keepdims=True)
    bound[...] = jnp.broadcast_to(jnp.maximum(loose, 1e-3) * jnp.maximum(most, 1e-20), (8, 128))

    @pl.loop(0, count * N // step)
    def _(k):
        at = pl.multiple_of(first * N + k * step, step)
        keep_s, keep_c, hit = masks(rows, cols, at, step)
        li = col[0, pl.ds(at, step), 0:1]
        lc = col[1, pl.ds(at, step), 0:1]
        same = scores_at(parts, at, step)
        cross = scores_at(parts, pl.multiple_of(at + 4 * N, step), step)
        m_s = jnp.where(keep_s, jnp.exp(same - li) + jnp.exp(same - lj), 0.0)
        m_c = jnp.where(keep_c, jnp.exp((cross - lc) - cross_j), 0.0) - jnp.where(hit, 1.0, 0.0)
        group = k // (N // step)
        base = group * 2 * N + (k % (N // step)) * step
        out[pl.ds(pl.multiple_of(base + w * N, step), step), :] = m_s.astype(jnp.bfloat16)
        out[pl.ds(pl.multiple_of(base + (1 - w) * N, step), step), :] = m_c.astype(jnp.bfloat16)


def weights_of(first, count, core, parts, rows, cols, lse_i, plane):
    return pl.pallas_call(
        functools.partial(weights_kernel, first, count),
        out_shape=[
            jax.ShapeDtypeStruct((count * 2 * N, J), jnp.bfloat16),
            jax.ShapeDtypeStruct((8, 128), jnp.float32),
        ],
        in_specs=[SMEM] + [VMEM] * (len(parts) + 7),
        out_specs=[VMEM] * 2,
        scratch_shapes=[pltpu.VMEM((2, 4 * N, 128), jnp.float32)],
        compiler_params=params(8),
        cost_estimate=FREE,
    )(core, *parts, rows, cols, lse_i, *plane)


def product_kernel(scaled, bound, mine, theirs, *refs):
    count = mine.shape[0] // (2 * N)
    blocks, outs, (held, sems) = refs[:2 * len(PARTS)], refs[2 * len(PARTS):-2], refs[-2:]
    copies = ([], [])
    for k in (0, 1):
        at = 0
        for n, size in enumerate(PARTS):
            i = k * len(PARTS) + n
            copies[k].append(pltpu.make_async_copy(blocks[i].at[k], held.at[k, pl.ds(at, size)], sems.at[i]))
            copies[k][-1].start()
            at += size
    shrink = 1.0 / bound[0:1, 0:1]
    step = 512
    for k, weights in enumerate((mine, theirs)):
        for copy in copies[k]:
            copy.wait()

        @pl.loop(0, held.shape[2] // step)
        def _(j):
            here = pl.ds(pl.multiple_of(j * step, step), step)
            term = plain(weights[...], held[k, :, here])
            for g in range(count):
                part = term[2 * N * g:2 * N * (g + 1)]
                if k == 0:
                    outs[g][:, here] = part
                else:
                    part = outs[g][:, here] + part
                    outs[g][:, here] = part * shrink if g >= scaled else part


def product_of(scaled, bound, mine, theirs, blocks, others):
    rows, wide = mine.shape[0], blocks[0].shape[2]
    outs = rows // (2 * N)
    return pl.pallas_call(
        functools.partial(product_kernel, scaled),
        out_shape=[jax.ShapeDtypeStruct((2 * N, wide), jnp.float32)] * outs,
        in_specs=[VMEM] * 3 + [pl.BlockSpec(memory_space=pl.ANY)] * (2 * len(PARTS)),
        out_specs=[VMEM] * outs,
        scratch_shapes=[pltpu.VMEM((2, J, wide), jnp.bfloat16), pltpu.SemaphoreType.DMA((2 * len(PARTS),))],
        compiler_params=params(20),
        cost_estimate=FREE,
    )(bound, mine, theirs, *blocks, *others)


def after(value, *others):
    return lax.optimization_barrier((value, *others))[0]


def settle(*values):
    return lax.optimization_barrier(values)


def body(queries, passages, passage_ids, pos_index):
    y, z, x, w = (lax.axis_index(name) for name in GRID)
    first = w == 0
    core = w.astype(jnp.int32).reshape(1)
    pick = lambda a, b: jnp.where(first, a, b)
    rows_of = functools.partial(lax.slice_in_dim, axis=1)
    low = lambda a: [rows_of(a, k * N, k * N + H) for k in range(a.shape[1] // N)]
    high = lambda a: [rows_of(a, k * N + H, (k + 1) * N) for k in range(a.shape[1] // N)]
    join = lambda parts: jnp.concatenate(parts, axis=1)
    line = lambda v, k: (up, far, down)[k - 1](v)
    by_first = lambda v, k: along(v, FIRST[k])
    by_second = lambda v, k: along(v, SECOND[k])
    ring = lambda v, send: [v] + [send(v, k) for k in RING[1:]]

    got = swap(pick(passages, queries))
    own = jnp.stack([pick(queries, passages), got])
    ints = jnp.stack([passage_ids, pos_index])

    fl, fr, own, *ints = settle(along(own, FIRST[1]), along(own, FIRST[3]), own, *ring(ints, line))
    f_low, f_high, own, fl, fr, *ints = settle(
        along(low(fl)[0], FIRST[1]), along(high(fr)[0], FIRST[3]), own, fl, fr, *ring(jnp.stack(ints), by_first)
    )
    group = place(((0, 0, N), (1, 0, N), (2, 0, N), (3, 0, H), (4, 0, H)), own, fl, fr, f_low, f_high)
    group, own, *ints = settle(group, own, *ring(jnp.stack(ints), by_second))
    ints = jnp.stack(ints)
    ids = ints[..., 0, :]
    dev, off = ints[..., 1, :] // N, ints[..., 1, :] % N
    near = lambda at, other: (lambda d: d ^ (d >> 1))((at - other) % 4)
    dy, dz, dx = near(y, dev // 16), near(z, dev // 4 % 4), near(x, dev % 4)
    pos = ((pick(dz, dy) * 4 + pick(dy, dz)) * 4 + dx) * N + off
    pair = jnp.arange(64 * N, dtype=jnp.int32).reshape(4, 4, 4, N)
    i_of = lambda t: t[0, 0].reshape(-1)
    j_of = lambda t: jnp.concatenate(
        [t[:3, :, 0].reshape(-1), t[3, :, 0].reshape(4, 2, H).transpose(1, 0, 2).reshape(-1)]
    )
    i_pair, i_id, i_pos = i_of(pair), i_of(ids), i_of(pos)
    j_pair, j_id, j_pos = j_of(pair), j_of(ids), j_of(pos)
    table, every = ids.reshape(1, -1), pair.reshape(1, -1)
    look = lambda at: jnp.sum(jnp.where(at[:, None] == every, table, 0), axis=1)
    i_tgt, j_tgt = look(i_pos), look(j_pos)
    rows = jnp.stack([pick(i_pair, i_id), pick(i_id, i_tgt), pick(i_pair, i_pos)] + [i_pair] * 5, axis=1)
    cols = jnp.stack([pick(j_pair, j_id), pick(j_tgt, j_id), pick(j_pos, j_pair)] + [j_pair] * 5)
    xl, xr = up(own), down(own)
    mine = [own, xl, xr, up(low(xl)[0]), down(high(xr)[0])]
    amax = jnp.maximum(
        *[jnp.max(jnp.abs(after(a, group, ids).astype(jnp.float32))) for a in (queries, passages)]
    )
    dl, dr, group, rows, cols, amax, *held = settle(
        along(group, SECOND[1]), along(group, SECOND[3]), group, rows, cols, amax, *mine, *[swap(a) for a in mine]
    )
    to_l = pack(tuple((0, k * N, H) for k in range(4)), dl)
    to_r = pack(tuple((0, k * N + H, H) for k in range(4)), dr)
    rows_i = rows_from([after(held[0], to_l, to_r)] + held[1:])
    blocks = [group, dl, dr]
    parts = scores_of(14, rows_i, ((0,), (1,), (2,)), *blocks)
    others = [swap(after(a, rows_i)) for a in blocks]
    gl, gr, *held = settle(along(to_l, SECOND[1]), along(to_r, SECOND[3]), *parts, *blocks)
    parts, blocks = held[:3], held[3:]
    blocks += [gl, gr]

    parts += scores_of(9, rows_i, ((0, 1),), gl, gr)
    found, *held = settle(stats_of(core, amax.reshape(1), parts, rows, cols), *others, swap(gl), swap(gr), *blocks)
    others, blocks = held[:5], held[5:]
    found = ring(found, line)
    lse_i, ends = merged(core, found, [swap(a) for a in found])
    loss = lse_i[4, :N]
    plane = ring(jnp.concatenate(ring(ends, by_first)), by_second)

    f16, f32 = jnp.float16, jnp.float32
    args = (parts, rows, cols, lse_i, plane)
    m_near, bound = weights_of(1, 3, core, *args)
    m_out = jnp.concatenate([m_near[4 * N:], m_near[:N], m_near[3 * N:4 * N]])
    m_mid = m_near[N:3 * N]
    opposite, free = product_of(0, bound, m_out, swap(m_out), blocks, others)
    opposite, free = opposite.astype(f16), free.astype(f16)
    got_q, got_p, above_q, below_p, mid = settle(
        up(opposite[:N]), down(opposite[N:]), down(free[:N]), up(free[N:]),
        *product_of(0, bound, m_mid, swap(m_mid), blocks, others),
    )
    above_p = down((mid[:N] + got_p.astype(f32)).astype(f16))
    below_q = up((mid[N:] + got_q.astype(f32)).astype(f16))
    m_own, _ = weights_of(0, 1, after(core, mid), *args)
    (here,) = product_of(1, bound, m_own, swap(m_own), blocks, others)
    grow = bound[0, 0]
    grad_q = here[:N] + (below_q.astype(f32) + above_q.astype(f32)) * grow
    grad_p = here[N:] + (below_p.astype(f32) + above_p.astype(f32)) * grow
    return loss, grad_q, grad_p


def solution(mesh):
    grid = Mesh(mesh.devices.reshape(4, 4, 4, 2), GRID)
    pair = ("y", "z", "x")
    placed = (P(pair, "w"), P(pair, "w"), P(pair), P(pair))
    return jax.shard_map(
        body,
        mesh=grid,
        in_specs=placed,
        out_specs=(P(pair), P(pair, "w"), P(pair, "w")),
        check_vma=False,
    )
```
